32 devices in a mesh: dp: 16 (over z, y, core), mp: 2 (over x).
Axes of the slice: x: 2, y: 2, z: 4, core: 2. Of those that a mesh axis runs over, the one named last changes fastest.
Arguments:
- inputs: bfloat16 [2, 16, 1024, 1472], P(None, 'dp', 'mp'), may hold values from -6 to 6
- cotangent: bfloat16 [2, 16, 1024, 1472], P(None, 'dp', 'mp'), may hold values from -6 to 6
- segments: int32 [2, 16, 1024], P(None, 'dp'), may hold values from 0 to 3, never falling along the last dimension, each value on 1 to 512 neighbouring positions
- rel_bucket: int32 [2047], replicated, may hold values from 0 to 31
- head_order: int32 [6], replicated, may hold values from 0 to 5, each once
- rel_table: float32 [32, 6], replicated, may hold values from -4 to 4
- norm1_gain: float32 [1472], replicated, may hold values from 0.1 to 1.9
- norm2_gain: float32 [1472], replicated, may hold values from 0.1 to 1.9
- w_query: bfloat16 [1472, 384], P('dp'), may hold values from -0.0390625 to 0.0390625
- w_key: bfloat16 [1472, 384], P('dp'), may hold values from -0.15625 to 0.15625
- w_value: bfloat16 [1472, 384], P('dp'), may hold values from -0.15625 to 0.15625
- output_weight: bfloat16 [384, 1472], P(None, 'dp'), may hold values from -1.25 to 1.25
- w_gate: bfloat16 [1472, 3584], P('dp', 'mp'), may hold values from -0.15625 to 0.15625
- w_up: bfloat16 [1472, 3584], P('dp', 'mp'), may hold values from -0.15625 to 0.15625
- w_down: bfloat16 [3584, 1472], P('mp', 'dp'), may hold values from -0.125 to 0.125
Outputs:
- outputs: bfloat16 [2, 16, 1024, 1472], P(None, 'dp', 'mp')
- grad_inputs: bfloat16 [2, 16, 1024, 1472], P(None, 'dp', 'mp')
- grad_rel: float32 [32, 6], replicated
- grad_norm1: float32 [1472], replicated
- grad_norm2: float32 [1472], replicated
- grad_query: float32 [1472, 384], P('dp')
- grad_key: float32 [1472, 384], P('dp')
- grad_value: float32 [1472, 384], P('dp')
- grad_out: float32 [384, 1472], P(None, 'dp')
- grad_gate: float32 [1472, 3584], P('dp', 'mp')
- grad_up: float32 [1472, 3584], P('dp', 'mp')
- grad_down: float32 [3584, 1472], P('mp', 'dp')
The draws below stay inside these ranges and needn't reach their ends.
Inputs may be any that keep to these rules, and one draw needn't show every extreme that they name: `segments`: ids never fall along a row; a document has 1 to 512 bytes. `head_order`: a permutation of the heads.
All inputs are finite; a program needn't handle non-finite values.
Results may differ from the reference program's by a relative error of at most 0.023.
Values may be sent and summed in bfloat16 or wider, within the bound.
No kernel may reach another device: no remote copies, remote signals or barrier semaphores. Data moves between devices by JAX's collectives and lax.ppermute only.
A program may use at most 320 MiB of HBM per device.

```python
import math
import jax
import jax.numpy as jnp
import numpy as np
from jax import lax

D = 1472
FF = 3584
HEADS = 6
HEAD = 64
NBUCKET = 32
LEN = 1024
DOCS = 4
MICRO = 2
ROWS = 16


def plant(array, key, least, largest):
    index_at = [jax.random.randint(jax.random.fold_in(key, axis), (), 0, length) for axis, length in enumerate(array.shape)]
    longest = array.shape.index(max(array.shape))
    next_to = index_at[:longest] + [(index_at[longest] + 1) % array.shape[longest]] + index_at[longest + 1:]
    return array.at[tuple(index_at)].set(least).at[tuple(next_to)].set(largest)


def with_spikes(array, rng, source, target, parts, factor):
    owner, partner = [(jnp.arange(array.shape[axis_at]) // (array.shape[axis_at] // parts)).reshape([-1 if axis == axis_at else 1 for axis in range(array.ndim)]) for axis_at in (source, target)]
    chosen = jax.random.permutation(rng, parts)[partner]
    strong = (owner == chosen) | (owner == (partner + parts // 2) % parts)
    return jnp.where(strong, factor * array, array)


def level_of(rng, shape, shards, smallest, largest):
    def one(position, parts):
        heights = jax.random.uniform(jax.random.fold_in(jax.random.fold_in(rng, 6), position), (parts,), jnp.float32, smallest / len(shards), largest / len(shards))
        return jnp.repeat(jnp.exp(heights), shape[position] // parts).reshape((-1,) + (1,) * (len(shape) - position - 1))

    factor_of = one(*shards[0])
    for cut in shards[1:]:
        factor_of = factor_of * one(*cut)
    return factor_of


def split_up(count, total, bound, slope):
    loads = [(1 << 20) // math.isqrt(standing ** slope) + 1 for standing in range(2, count + 1)]
    surplus, counts = total - bound - (count - 1), [1] * (count - 1)
    while surplus > 0:
        free = [i for i in range(count - 1) if counts[i] < bound]
        mass, remaining = sum([loads[i] for i in free]), surplus
        for i in free:
            extra = min(bound - counts[i], max(1, remaining * loads[i] // mass), surplus)
            counts[i] = counts[i] + extra
            surplus = surplus - extra
    return np.array([bound] + counts)


def ragged_sizes(stream_key, number_of, total, reach, lean):
    if number_of == 2:
        one = jax.random.randint(stream_key, (), max(1, total - reach), min(reach, total - 1) + 1)
        return jnp.stack([one, total - one])
    sizes = jnp.asarray(split_up(number_of, total, reach, lean), jnp.int32)
    pairs = (number_of - 1) // 2
    source_of, sink = sizes[1:1 + 2 * pairs:2], sizes[2:2 + 2 * pairs:2]
    room = jnp.minimum(source_of - 1, reach - sink)
    passed = jax.random.randint(jax.random.fold_in(stream_key, 1), (pairs,), 0, 1 << 20) % (room + 1)
    sizes = sizes.at[1:1 + 2 * pairs:2].set(source_of - passed).at[2:2 + 2 * pairs:2].set(sink + passed)
    return sizes[jax.random.permutation(jax.random.fold_in(stream_key, 2), number_of)]


def centred(key, shape, deviation, reach, pieces=(), kind=jnp.bfloat16):
    factor_of = level_of(key, shape, pieces, -0.22, 0.18) if pieces else 1.0
    values = jax.random.normal(key, shape, jnp.float32) * deviation * factor_of
    return jnp.minimum(jnp.maximum(values, -reach), reach).astype(kind)


def heavy_noise(stream_key, extent, spread, reach, shards, heavy, kind=jnp.bfloat16):
    entries = spread * jax.random.normal(stream_key, extent, jnp.float32)
    if shards:
        entries = entries * level_of(stream_key, extent, shards, -0.22, 0.18)
    return jnp.clip(with_spikes(entries, jax.random.fold_in(stream_key, 3), *heavy), -reach, reach).astype(kind)


def setup_inputs(seed: int = 0) -> dict:
    seeds = jax.random.split(jax.random.key(seed), 16)
    inputs = heavy_noise(seeds[0], (MICRO, ROWS, LEN, D), 1.0, 6.0, ((1, 16), (2, 2)), (1, 3, 16, 2.0))
    cotangent = heavy_noise(seeds[1], (MICRO, ROWS, LEN, D), 1.0, 6.0, ((1, 16), (2, 2)), (1, 3, 16, 2.0))
    segments = jax.vmap(lambda own: jnp.searchsorted(jnp.cumsum(ragged_sizes(own, DOCS, LEN, LEN // 2, 2)), jnp.arange(LEN), side="right"))(jax.random.split(seeds[2], MICRO * ROWS)).reshape((MICRO, ROWS, LEN)).astype(jnp.int32)
    rel_bucket = plant(jax.random.randint(seeds[3], (2 * LEN - 1,), 0, NBUCKET), jax.random.fold_in(seeds[3], 1), 0, NBUCKET - 1).astype(jnp.int32)
    head_order = jax.random.permutation(seeds[4], HEADS).astype(jnp.int32)
    rel_table = centred(seeds[5], (NBUCKET, HEADS), 1.0, 4.0, (), jnp.float32)
    norm1_gain = jnp.clip(1.0 + 0.18 * jax.random.normal(seeds[6], (D,), jnp.float32), 0.1, 1.9)
    norm2_gain = jnp.clip(1.0 + 0.18 * jax.random.normal(seeds[7], (D,), jnp.float32), 0.1, 1.9)
    w_query = centred(seeds[8], (D, HEADS * HEAD), (16 * D) ** -0.5, 0.0390625, ((0, 16),))
    w_key = centred(seeds[9], (D, HEADS * HEAD), D ** -0.5, 0.15625, ((0, 16),))
    w_value = centred(seeds[10], (D, HEADS * HEAD), D ** -0.5, 0.15625, ((0, 16),))
    output_weight = centred(seeds[11], (HEADS * HEAD, D), (HEADS * HEAD // 16) ** -0.5, 1.25, ((1, 16),))
    w_gate = centred(seeds[12], (D, FF), D ** -0.5, 0.15625, ((0, 16), (1, 2)))
    w_up = centred(seeds[13], (D, FF), D ** -0.5, 0.15625, ((0, 16), (1, 2)))
    w_down = centred(seeds[14], (FF, D), (FF // 2) ** -0.5, 0.125, ((0, 2), (1, 16)))
    return dict(inputs=inputs, cotangent=cotangent, segments=segments, rel_bucket=rel_bucket, head_order=head_order, rel_table=rel_table, norm1_gain=norm1_gain, norm2_gain=norm2_gain, w_query=w_query, w_key=w_key, w_value=w_value, output_weight=output_weight, w_gate=w_gate, w_up=w_up, w_down=w_down)


@jax.custom_vjp
def low(v):
    return lax.optimization_barrier(v.astype(jnp.bfloat16)).astype(jnp.float32)

@jax.custom_vjp
def reduced_backward(v):
    return v

def low_keep(v):
    return (low(v), None)

def low_pass(kept, grad):
    return (grad,)

def back_keep(v):
    return (v, None)

def back_low(kept, grad):
    return (low(grad),)
low.defvjp(low_keep, low_pass)
reduced_backward.defvjp(back_keep, back_low)
EPSILON = 1e-06
TOP_PRECISION = lax.Precision.HIGHEST
GELU_SCALE = 0.7978845608028654

def gelu_tanh(values):
    return 0.5 * values * (1.0 + jnp.tanh(GELU_SCALE * (values + 0.044715 * values * values * values)))

def rms_scale(values, gain):
    return values * lax.rsqrt(lax.optimization_barrier(jnp.mean(values * values, axis=-1, keepdims=True)) + EPSILON) * gain

def attend(queries, keys, values, seg_ids, offsets_bias):
    groups, length, head_count, head_size = queries.shape
    block_rows = min(512, length)
    starts = (jnp.arange(length // block_rows) * block_rows).astype(jnp.int32)

    def one_block(start):
        query_block = lax.dynamic_slice_in_dim(queries, start, block_rows, 1)
        seg_block = lax.dynamic_slice_in_dim(seg_ids, start, block_rows, 1)
        positions = start + jnp.arange(block_rows).astype(jnp.int32)
        offsets = jnp.arange(length).astype(jnp.int32)[None, :] - positions[:, None] + (length - 1)
        bias_block = jnp.transpose(jnp.take(offsets_bias, offsets, axis=0), (2, 0, 1))
        scores = jnp.einsum('gihe,gthe->ghit', query_block, keys, precision=TOP_PRECISION) + bias_block[None]
        scores = reduced_backward(scores)
        same_doc = seg_block[:, None, :, None] == seg_ids[:, None, None, :]
        scores = jnp.where(same_doc, scores, -1e+30)
        attn_probs = jax.nn.softmax(scores, axis=-1)
        return jnp.einsum('ghit,gthe->gihe', low(attn_probs), values, precision=TOP_PRECISION)
    blocks = lax.map(jax.checkpoint(one_block), starts)
    return jnp.moveaxis(blocks, 0, 1).reshape(groups, length, head_count, head_size)

def forward(inputs, seg_ids, rel_bucket, head_order, rel_table, norm1_gain, norm2_gain, w_query, w_key, w_value, output_weight, w_gate, w_up, w_down):
    groups, length, model_width = inputs.shape
    head_count = rel_table.shape[1]
    head_size = w_query.shape[1] // head_count
    offsets_bias = rel_table[rel_bucket][:, head_order]
    normalized_rows = low(rms_scale(inputs, norm1_gain))

    def project(weight_matrix):
        mixed_heads = jnp.einsum('okj,jq->okq', normalized_rows, weight_matrix, precision=TOP_PRECISION)
        return low(reduced_backward(mixed_heads)).reshape(groups, length, head_count, head_size)
    context_rows = attend(project(w_query), project(w_key), project(w_value), seg_ids, offsets_bias)
    context_rows = low(reduced_backward(context_rows)).reshape(groups, length, head_count * head_size)
    attention_output = reduced_backward(jnp.einsum('qez,zm->qem', context_rows, output_weight, precision=TOP_PRECISION))
    middle = inputs + attention_output
    normed_two = low(rms_scale(middle, norm2_gain))
    gate = reduced_backward(jnp.einsum('gld,df->glf', normed_two, w_gate, precision=TOP_PRECISION))
    upward = reduced_backward(jnp.einsum('gld,df->glf', normed_two, w_up, precision=TOP_PRECISION))
    hidden = low(gelu_tanh(gate) * upward)
    ffn_out = reduced_backward(jnp.einsum('glf,fd->gld', hidden, w_down, precision=TOP_PRECISION))
    return middle + ffn_out

def reference(inputs, cotangent, segments, rel_bucket, head_order, rel_table, norm1_gain, norm2_gain, w_query, w_key, w_value, output_weight, w_gate, w_up, w_down):
    micro_count, row_count, length, model_width = inputs.shape
    seq_total = micro_count * row_count
    group_size = math.gcd(seq_total, max(1, 4096 // length))
    group_count = seq_total // group_size
    params = tuple((param.astype(jnp.float32) for param in (rel_table, norm1_gain, norm2_gain, w_query, w_key, w_value, output_weight, w_gate, w_up, w_down)))
    flat_in = inputs.reshape(group_count, group_size, length, model_width).astype(jnp.float32)
    flat_cot = cotangent.reshape(group_count, group_size, length, model_width).astype(jnp.float32)
    flat_seg = segments.reshape(group_count, group_size, length)

    def one_group(running, item):
        group_in, group_cot, group_seg = item

        def run_layer(layer_in, *weights):
            return forward(layer_in, group_seg, rel_bucket, head_order, *weights)
        result, pullback = jax.vjp(run_layer, group_in, *params)
        gradients = pullback(group_cot)
        running = tuple((total + gradient for total, gradient in zip(running, gradients[1:])))
        return (running, (result.astype(jnp.bfloat16), gradients[0].astype(jnp.bfloat16)))
    initial = tuple((jnp.zeros(param.shape, jnp.float32) for param in params))
    totals, (outputs, grad_inputs) = lax.scan(one_group, initial, (flat_in, flat_cot, flat_seg))
    out_shape = inputs.shape
    return (outputs.reshape(out_shape), grad_inputs.reshape(out_shape), totals[0], totals[1], totals[2], totals[3], totals[4], totals[5], totals[6], totals[7], totals[8], totals[9])
```

```python
import functools

import jax
import jax.numpy as jnp
from jax import lax
from jax.experimental import pallas as pl
from jax.experimental.pallas import tpu as pltpu
from jax.sharding import PartitionSpec as P

EPSILON = 1e-06
TOP_PRECISION = lax.Precision.HIGHEST
GELU_SCALE = 0.7978845608028654
BF16 = jnp.bfloat16
F32 = jnp.float32
NEGATIVE = -1e30
VMEM_BYTES = 56 * 1024 * 1024


def swap_dp(array, mask):
    count = lax.axis_size("dp")
    return lax.ppermute(array, "dp", [(i, i ^ mask) for i in range(count)])


def swap_mp(array, mask):
    count = lax.axis_size("mp")
    return lax.ppermute(array, "mp", [(i, i ^ mask) for i in range(count)])


def place(pieces, index, axis):
    first = pieces[0]
    shape = first.shape[:axis] + (len(pieces),) + first.shape[axis:]
    whole = jnp.zeros(shape, first.dtype)
    for k, piece in enumerate(pieces):
        whole = lax.dynamic_update_index_in_dim(
            whole, jnp.expand_dims(piece, axis), index ^ k, axis
        )
    return whole


def pick(array, index, axis):
    return lax.dynamic_index_in_dim(array, index, axis, keepdims=False)


def add_low(*terms):
    total = terms[0].astype(F32)
    for term in terms[1:]:
        total = total + term.astype(F32)
    return total.astype(BF16)


def bias_kernel(window_ref, table_ref):
    block = table_ref.shape[-1]
    wide = jnp.broadcast_to(window_ref[0, 0], (block, 2 * block))
    rolled = pltpu.roll(wide, block + 1, 1, stride=1, stride_axis=0)
    table_ref[0, 0] = rolled[:, :block]


def bias_table(windows, block):
    heads, count = windows.shape[:2]
    return pl.pallas_call(
        bias_kernel,
        grid=(heads, count),
        in_specs=[pl.BlockSpec((1, 1, 1, 2 * block), lambda j, e: (j, e, 0, 0))],
        out_specs=pl.BlockSpec((1, 1, block, block), lambda j, e: (j, e, 0, 0)),
        out_shape=jax.ShapeDtypeStruct((heads, count, block, block), F32),
        name="bias_table",
    )(windows)


def transposed(value):
    return jnp.transpose(value.astype(F32), (1, 0)).astype(BF16)


def halves(value_t, half):
    zero = jnp.zeros((half, value_t.shape[1]), value_t.dtype)
    return (
        jnp.concatenate([value_t[:half], zero], axis=0),
        jnp.concatenate([zero, value_t[half:]], axis=0),
    )


def dot_nn(left, right):
    return lax.dot_general(left, right, (((1,), (0,)), ((), ())), preferred_element_type=F32)


def attend_kernel(sources, block, half, info_ref, q_ref, *refs):
    kv_refs = refs[: 2 * sources]
    segq_ref, segk_ref, table_ref, ctx_ref, lse_ref = refs[2 * sources : 2 * sources + 5]
    s_scr, m_scr, l_scr, acc_scr, vt_scr = refs[2 * sources + 5 :]
    length = q_ref.shape[1]
    q_blocks = length // block
    k_blocks = q_blocks * sources
    place_x = info_ref[0]
    step = pl.program_id(1)
    for s in range(sources):
        vt_scr[:, s * length : (s + 1) * length] = transposed(kv_refs[2 * s + 1][0])
    for qb in range(q_blocks):
        rows = pl.ds(qb * block, block)
        q_heads = halves(transposed(q_ref[0, rows, :]), half)
        seg_q = segq_ref[0, :, rows]
        m_scr[...] = jnp.full(m_scr.shape, NEGATIVE, F32)
        l_scr[...] = jnp.zeros(l_scr.shape, F32)
        acc_scr[...] = jnp.zeros(acc_scr.shape, F32)
        for kb in range(k_blocks):
            s, lb = divmod(kb, q_blocks)
            live = info_ref[1 + (step * q_blocks + qb) * k_blocks + kb]

            @pl.when(live != 0)
            def _(s=s, lb=lb, kb=kb):
                entry = k_blocks - 1 - ((place_x ^ s) * q_blocks + lb - place_x * q_blocks - qb)
                keys = kv_refs[2 * s][0, pl.ds(lb * block, block), :]
                kept = segk_ref[0, pl.ds(kb * block, block), :] == seg_q
                for h in range(2):
                    score = dot_nn(keys, q_heads[h]) + table_ref[h, entry]
                    score = jnp.where(kept, score, NEGATIVE)
                    s_scr[h, kb] = score
                    m_scr[h] = jnp.maximum(m_scr[h], jnp.max(score, axis=0, keepdims=True))

        for kb in range(k_blocks):
            live = info_ref[1 + (step * q_blocks + qb) * k_blocks + kb]

            @pl.when(live != 0)
            def _(kb=kb):
                for h in range(2):
                    prob = jnp.exp(s_scr[h, kb] - m_scr[h])
                    l_scr[h] += jnp.sum(prob, axis=0, keepdims=True)
                    values_t = vt_scr[h * half : (h + 1) * half, kb * block : (kb + 1) * block]
                    acc_scr[h * half : (h + 1) * half] += dot_nn(values_t, prob.astype(BF16))

        for h in range(2):
            lse_ref[0, 0, h : h + 1, rows] = m_scr[h] + jnp.log(l_scr[h])
        context = jnp.concatenate(
            [acc_scr[:half] / l_scr[0], acc_scr[half:] / l_scr[1]], axis=0
        )
        ctx_ref[0, rows, :] = jnp.transpose(context, (1, 0)).astype(BF16)


def grad_kernel(sources, block, half, info_ref, q_ref, *refs):
    kv_refs = refs[: 2 * sources]
    refs = refs[2 * sources :]
    segq_ref, segk_ref, table_ref, ctx_ref, lse_ref, gctx_ref = refs[:6]
    dq_ref, gbias_ref = refs[6:8]
    dkv_refs = refs[8 : 8 + sources]
    dk_scr, dv_scr, dq_scr, kt_scr, db_scr = refs[8 + sources :]
    length = q_ref.shape[1]
    q_blocks = length // block
    k_blocks = q_blocks * sources
    place_x = info_ref[0]
    step = pl.program_id(1)
    lane = lax.broadcasted_iota(jnp.int32, (block, 2 * half), 1)

    @pl.when(step == 0)
    def _():
        db_scr[...] = jnp.zeros(db_scr.shape, F32)

    for s in range(sources):
        kt_scr[:, s * length : (s + 1) * length] = transposed(kv_refs[2 * s][0])
    dk_scr[...] = jnp.zeros(dk_scr.shape, F32)
    dv_scr[...] = jnp.zeros(dv_scr.shape, F32)
    for qb in range(q_blocks):
        rows = pl.ds(qb * block, block)
        query = q_ref[0, rows, :]
        grad_out = gctx_ref[0, rows, :]
        grad_out_t = jnp.transpose(grad_out.astype(F32), (1, 0))
        context_t = jnp.transpose(ctx_ref[0, rows, :].astype(F32), (1, 0))
        product = grad_out_t * context_t
        deltas = (
            jnp.sum(product[:half], axis=0, keepdims=True),
            jnp.sum(product[half:], axis=0, keepdims=True),
        )
        q_heads = halves(transposed(query), half)
        g_heads = halves(grad_out_t.astype(BF16), half)
        zero = jnp.zeros(query.shape, BF16)
        q_lanes = (jnp.where(lane < half, query, zero), jnp.where(lane < half, zero, query))
        g_lanes = (
            jnp.where(lane < half, grad_out, zero),
            jnp.where(lane < half, zero, grad_out),
        )
        seg_q = segq_ref[0, :, rows]
        dq_scr[...] = jnp.zeros(dq_scr.shape, F32)
        for kb in range(k_blocks):
            s, lb = divmod(kb, q_blocks)
            live = info_ref[1 + (step * q_blocks + qb) * k_blocks + kb]

            @pl.when(live != 0)
            def _(s=s, lb=lb, kb=kb):
                entry = k_blocks - 1 - ((place_x ^ s) * q_blocks + lb - place_x * q_blocks - qb)
                keys = kv_refs[2 * s][0, pl.ds(lb * block, block), :]
                values = kv_refs[2 * s + 1][0, pl.ds(lb * block, block), :]
                kept = segk_ref[0, pl.ds(kb * block, block), :] == seg_q
                key_rows = pl.ds(kb * block, block)
                key_grad = dk_scr[key_rows, :]
                value_grad = dv_scr[key_rows, :]
                for h in range(2):
                    score = dot_nn(keys, q_heads[h]) + table_ref[h, entry]
                    score = jnp.where(kept, score, NEGATIVE)
                    prob = jnp.exp(score - lse_ref[0, 0, h : h + 1, rows])
                    grad_prob = dot_nn(values, g_heads[h])
                    grad_score = prob * (grad_prob - deltas[h])
                    db_scr[h, entry] += grad_score
                    low = grad_score.astype(BF16)
                    key_grad = key_grad + dot_nn(low, q_lanes[h])
                    value_grad = value_grad + dot_nn(prob.astype(BF16), g_lanes[h])
                    keys_t = kt_scr[h * half : (h + 1) * half, kb * block : (kb + 1) * block]
                    dq_scr[h * half : (h + 1) * half] += dot_nn(keys_t, low)
                dk_scr[key_rows, :] = key_grad
                dv_scr[key_rows, :] = value_grad

        dq_ref[0, rows, :] = jnp.transpose(dq_scr[...], (1, 0)).astype(BF16)
    for s in range(sources):
        dkv_refs[s][0, 0] = dk_scr[s * length : (s + 1) * length, :].astype(BF16)
        dkv_refs[s][0, 1] = dv_scr[s * length : (s + 1) * length, :].astype(BF16)

    @pl.when(step == pl.num_programs(1) - 1)
    def _():
        for h in range(2):
            for entry in range(2 * k_blocks - 1):
                tile = db_scr[h, entry]
                tile = jnp.concatenate([tile, jnp.zeros_like(tile)], axis=1)
                count = block
                while count > 8:
                    count //= 2
                    tile = pltpu.roll(tile[:count], count, 1) + tile[count:]
                total = tile[7:8]
                for t in range(7):
                    total = total + pltpu.roll(tile[t : t + 1], 7 - t, 1)
                gbias_ref[h, entry] = total


def attention_specs(sources, length, block, pairs, width):
    k_blocks = length * sources // block
    entries = 2 * k_blocks - 1

    def column(offset):
        return pl.BlockSpec((1, length, width), lambda p, m, info: (m, 0, p + offset))

    kv_specs = [column(pairs), column(2 * pairs)]
    for _ in range(sources - 1):
        kv_specs += [column(0), column(pairs)]
    seg_specs = [
        pl.BlockSpec((1, 1, length), lambda p, m, info: (m, 0, 0)),
        pl.BlockSpec((1, length * sources, 1), lambda p, m, info: (m, 0, 0)),
    ]
    table_spec = pl.BlockSpec((2, entries, block, block), lambda p, m, info: (p, 0, 0, 0))
    lse_spec = pl.BlockSpec((1, 1, 8, length), lambda p, m, info: (m, p, 0, 0))
    return k_blocks, entries, column, kv_specs, seg_specs, table_spec, lse_spec


def kv_operands(qkv, others):
    operands = [qkv, qkv]
    for other in others:
        operands += [other, other]
    return operands


def attend(info, qkv, others, seg_q, seg_k, table, block, head_size):
    micro, length, total = qkv.shape
    sources = 1 + len(others)
    width = 2 * head_size
    pairs = total // (3 * width)
    k_blocks, entries, column, kv_specs, seg_specs, table_spec, lse_spec = attention_specs(
        sources, length, block, pairs, width
    )
    return pl.pallas_call(
        functools.partial(attend_kernel, sources, block, head_size),
        grid_spec=pltpu.PrefetchScalarGridSpec(
            num_scalar_prefetch=1,
            grid=(pairs, micro),
            in_specs=[column(0)] + kv_specs + seg_specs + [table_spec],
            out_specs=[column(0), lse_spec],
            scratch_shapes=[
                pltpu.VMEM((2, k_blocks, block, block), F32),
                pltpu.VMEM((2, 1, block), F32),
                pltpu.VMEM((2, 1, block), F32),
                pltpu.VMEM((width, block), F32),
                pltpu.VMEM((width, length * sources), BF16),
            ],
        ),
        out_shape=[
            jax.ShapeDtypeStruct((micro, length, pairs * width), BF16),
            jax.ShapeDtypeStruct((micro, pairs, 8, length), F32),
        ],
        compiler_params=pltpu.CompilerParams(vmem_limit_bytes=VMEM_BYTES),
        name="attend",
    )(info, qkv, *kv_operands(qkv, others), seg_q, seg_k, table)


def attend_grads(info, qkv, others, seg_q, seg_k, table, context, lse, grad_context, block, head_size):
    micro, length, total = qkv.shape
    sources = 1 + len(others)
    width = 2 * head_size
    pairs = total // (3 * width)
    k_blocks, entries, column, kv_specs, seg_specs, table_spec, lse_spec = attention_specs(
        sources, length, block, pairs, width
    )
    dkv_spec = pl.BlockSpec((1, 2, length, width), lambda p, m, info: (m, 0, 0, p))
    results = pl.pallas_call(
        functools.partial(grad_kernel, sources, block, head_size),
        grid_spec=pltpu.PrefetchScalarGridSpec(
            num_scalar_prefetch=1,
            grid=(pairs, micro),
            in_specs=[column(0)]
            + kv_specs
            + seg_specs
            + [table_spec, column(0), lse_spec, column(0)],
            out_specs=[
                column(0),
                pl.BlockSpec((2, entries, 1, 2 * block), lambda p, m, info: (p, 0, 0, 0)),
            ]
            + [dkv_spec] * sources,
            scratch_shapes=[
                pltpu.VMEM((length * sources, width), F32),
                pltpu.VMEM((length * sources, width), F32),
                pltpu.VMEM((width, block), F32),
                pltpu.VMEM((width, length * sources), BF16),
                pltpu.VMEM((2, entries, block, block), F32),
            ],
        ),
        out_shape=[
            jax.ShapeDtypeStruct((micro, length, pairs * width), BF16),
            jax.ShapeDtypeStruct((2 * pairs, entries, 1, 2 * block), F32),
        ]
        + [jax.ShapeDtypeStruct((micro, 2, length, pairs * width), BF16)] * sources,
        compiler_params=pltpu.CompilerParams(vmem_limit_bytes=VMEM_BYTES),
        name="attend_grads",
    )(
        info,
        qkv,
        *kv_operands(qkv, others),
        seg_q,
        seg_k,
        table,
        context,
        lse,
        grad_context,
    )
    return results[0], results[1], results[2:]


def gather_attention(shard, z, y, core, x):
    dp, mp = lax.axis_size("dp"), lax.axis_size("mp")
    depth = dp // 4
    rows, columns = shard.shape
    part = columns // (2 * mp)
    split = shard.reshape(rows, mp, 2, part)
    own_x = pick(split, x, 1)
    kept = pick(own_x, core, 1)
    got = swap_dp(pick(own_x, 1 - core, 1), 1)
    piece = place([kept, got], core, 0).reshape(2 * rows, part)
    column_y = place([piece] + [swap_dp(piece, 4 * k) for k in range(1, depth)], z, 0)
    both = place([column_y, swap_dp(column_y, 2)], y, 1)
    full = both.reshape(dp * rows, part)
    all_x = place([full] + [swap_mp(full, k) for k in range(1, mp)], x, 0)
    all_core = place([all_x, swap_dp(all_x, 1)], core, 1)
    return jnp.transpose(all_core, (2, 0, 1, 3)).reshape(dp * rows, columns)


def scatter_attention(grads, z, y, core, x):
    dp, mp = lax.axis_size("dp"), lax.axis_size("mp")
    depth = dp // 4
    wide, columns = grads.shape
    rows = wide // dp
    part = columns // (2 * mp)
    split = grads.reshape(wide, mp, 2, part)
    mine = add_low(pick(split, core, 2), swap_dp(pick(split, 1 - core, 2), 1))
    own = add_low(
        pick(mine, x, 1), *[swap_mp(pick(mine, x ^ k, 1), k) for k in range(1, mp)]
    ).reshape(depth, 2, 2 * rows, part)
    half = add_low(pick(own, y, 1), swap_dp(pick(own, 1 - y, 1), 2))
    piece = add_low(
        pick(half, z, 0), *[swap_dp(pick(half, z ^ k, 0), 4 * k) for k in range(1, depth)]
    )
    all_x = place([piece] + [swap_mp(piece, k) for k in range(1, mp)], x, 0)
    split_rows = all_x.reshape(mp, 2, rows, part)
    kept = pick(split_rows, core, 1)
    got = swap_dp(pick(split_rows, 1 - core, 1), 1)
    both = place([kept, got], core, 1)
    return jnp.transpose(both, (2, 0, 1, 3)).reshape(rows, columns)


def gather_ffn(piece, z, y, x_last):
    dp, mp = lax.axis_size("dp"), lax.axis_size("mp")
    depth = dp // 4
    kinds, rows, units = piece.shape
    column_y = place([piece] + [swap_dp(piece, 4 * k) for k in range(1, depth)], z, 1)
    if x_last:
        both = place([column_y, swap_dp(column_y, 2)], y, 2)
        full = both.reshape(kinds, dp // 2 * rows, units)
        return jnp.concatenate([full] + [swap_mp(full, k) for k in range(1, mp)], axis=2)
    wide = jnp.concatenate([column_y] + [swap_mp(column_y, k) for k in range(1, mp)], axis=3)
    both = place([wide, swap_dp(wide, 2)], y, 2)
    return both.reshape(kinds, dp // 2 * rows, mp * units)


def scatter_ffn(grads, z, y, x_last):
    dp, mp = lax.axis_size("dp"), lax.axis_size("mp")
    depth = dp // 4
    kinds, wide, total = grads.shape
    rows, units = wide // (dp // 2), total // mp
    own = grads.reshape(kinds, depth, 2, rows, mp, units)

    def sum_y(part):
        return add_low(pick(part, y, 2), swap_dp(pick(part, 1 - y, 2), 2))

    def sum_x(part):
        return add_low(part[..., 0, :], *[swap_mp(part[..., k, :], k) for k in range(1, mp)])

    half = sum_y(sum_x(own)) if x_last else sum_x(sum_y(own))
    return add_low(
        pick(half, z, 1), *[swap_dp(pick(half, z ^ k, 1), 4 * k) for k in range(1, depth)]
    )


def norm_factor(values):
    return lax.rsqrt(jnp.mean(values * values, axis=-1, keepdims=True) + EPSILON)


def norm_grads(values, factor, gain, grad):
    scaled = values * factor
    lifted = grad * gain
    inner = jnp.mean(lifted * scaled, axis=-1, keepdims=True)
    return factor * (lifted - scaled * inner), jnp.sum(grad * scaled, axis=0)


def matmul(left, right):
    return jnp.einsum("td,df->tf", left, right, preferred_element_type=F32)


def matmul_t(left, right):
    return jnp.einsum("tf,df->td", left, right, preferred_element_type=F32)


def outer(left, right):
    return jnp.einsum("td,tf->df", left, right, preferred_element_type=F32)


def body(
    inputs,
    cotangent,
    segments,
    rel_bucket,
    head_order,
    rel_table,
    norm1_gain,
    norm2_gain,
    w_query,
    w_key,
    w_value,
    output_weight,
    w_gate,
    w_up,
    w_down,
):
    mp = lax.axis_size("mp")
    x = lax.axis_index("mp")
    dp_place = lax.axis_index("dp")
    core, y, z = dp_place & 1, (dp_place >> 1) & 1, dp_place >> 2
    micro, rows, own_length, model = inputs.shape
    groups = micro * rows
    length = own_length * mp
    bucket_count, head_count = rel_table.shape
    inner = w_query.shape[1]
    head_size = inner // head_count
    block = min(256, own_length)
    q_blocks, k_blocks = own_length // block, length // block
    tokens = groups * own_length

    attention_shard = jnp.concatenate(
        [w_query, w_key, w_value, jnp.transpose(output_weight)], axis=1
    )
    attention_full = gather_attention(attention_shard, z, y, core, x)
    w_qkv, w_out_t = attention_full[:, : 3 * inner], attention_full[:, 3 * inner :]

    own_rows, own_units = w_gate.shape
    half_units = own_units // 2
    ffn_shard = jnp.stack([w_gate, w_up, jnp.transpose(w_down)])
    ffn_split = ffn_shard.reshape(3, own_rows, 2, half_units)
    kept = pick(ffn_split, core, 2)
    got = swap_dp(pick(ffn_split, 1 - core, 2), 1)
    ffn_piece = place([kept, got], core, 1).reshape(3, 2 * own_rows, half_units)
    first_units = half_units * 3 // 7
    chunks = (
        gather_ffn(ffn_piece[:, :, :first_units], z, y, True),
        gather_ffn(ffn_piece[:, :, first_units:], z, y, False),
    )

    bucket_rev = jnp.concatenate([rel_bucket[::-1], jnp.full((1,), -1, jnp.int32)])
    bucket_hot = (bucket_rev[:, None] == jnp.arange(bucket_count, dtype=jnp.int32)[None, :]).astype(F32)
    head_hot = (head_order[:, None] == jnp.arange(head_count, dtype=jnp.int32)[None, :]).astype(F32)
    offset_table = jnp.dot(bucket_hot, rel_table, precision=TOP_PRECISION)
    offset_bias = jnp.dot(head_hot, offset_table.T, precision=TOP_PRECISION)
    bias_blocks = offset_bias.reshape(head_count, 2 * k_blocks, block)
    windows = jnp.concatenate([bias_blocks[:, :-1], bias_blocks[:, 1:]], axis=2)
    table = bias_table(windows[:, :, None, :], block)

    seg_flat = segments.reshape(groups, length)
    seg_q = lax.dynamic_slice_in_dim(seg_flat, x * own_length, own_length, 1)
    seg_parts = seg_flat.reshape(groups, mp, own_length)
    seg_k = jnp.concatenate([pick(seg_parts, x ^ k, 1) for k in range(mp)], axis=1)
    q_edges = seg_q.reshape(groups, q_blocks, block)
    k_edges = seg_k.reshape(groups, k_blocks, block)
    live = (q_edges[:, :, None, 0] <= k_edges[:, None, :, -1]) & (
        k_edges[:, None, :, 0] <= q_edges[:, :, None, -1]
    )
    info = jnp.concatenate([x.reshape(1).astype(jnp.int32), live.reshape(-1).astype(jnp.int32)])
    seg_q_row = seg_q.reshape(groups, 1, own_length)
    seg_k_column = seg_k.reshape(groups, length, 1)

    layer_in = inputs.reshape(tokens, model).astype(F32)
    factor1 = norm_factor(layer_in)
    normed1 = (layer_in * factor1 * norm1_gain).astype(BF16)
    qkv = matmul(normed1, w_qkv).astype(BF16).reshape(groups, own_length, 3 * inner)
    own_kv = qkv[:, :, inner:]
    others = [swap_mp(own_kv, k) for k in range(1, mp)]
    context, lse = attend(info, qkv, others, seg_q_row, seg_k_column, table, block, head_size)
    context_flat = context.reshape(tokens, inner)
    middle = layer_in + matmul_t(context_flat, w_out_t)
    factor2 = norm_factor(middle)
    normed2 = (middle * factor2 * norm2_gain).astype(BF16)

    cot = cotangent.reshape(tokens, model)
    normed2_both = jnp.concatenate([normed2, swap_dp(normed2, 1)], axis=0)
    cot_both = jnp.concatenate([cot, swap_dp(cot, 1)], axis=0)
    ffn_sum = None
    back_sum = None
    reduced = []
    for chunk, weights in enumerate(chunks):
        gate = matmul(normed2_both, weights[0])
        upward = matmul(normed2_both, weights[1])
        grad_hidden = matmul(cot_both, weights[2])
        tanh = jnp.tanh(GELU_SCALE * (gate + 0.044715 * gate * gate * gate))
        gelu = 0.5 * gate * (1.0 + tanh)
        slope = 0.5 * (1.0 + tanh) + 0.5 * gate * (1.0 - tanh * tanh) * GELU_SCALE * (
            1.0 + 3.0 * 0.044715 * gate * gate
        )
        hidden = (gelu * upward).astype(BF16)
        grad_gate_in = (grad_hidden * upward * slope).astype(BF16)
        grad_up_in = (grad_hidden * gelu).astype(BF16)
        ffn_part = matmul_t(hidden, weights[2])
        back_part = matmul_t(grad_gate_in, weights[0]) + matmul_t(grad_up_in, weights[1])
        ffn_sum = ffn_part if ffn_sum is None else ffn_sum + ffn_part
        back_sum = back_part if back_sum is None else back_sum + back_part
        grads = jnp.stack(
            [
                outer(normed2_both, grad_gate_in).astype(BF16),
                outer(normed2_both, grad_up_in).astype(BF16),
                outer(cot_both, hidden).astype(BF16),
            ]
        )
        reduced.append(scatter_ffn(grads, z, y, chunk == 0))
    ffn_low = ffn_sum.astype(BF16)
    back_low = back_sum.astype(BF16)
    grad_normed2 = back_low[:tokens].astype(F32) + swap_dp(back_low[tokens:], 1).astype(F32)
    ffn_out = ffn_low[:tokens].astype(F32) + swap_dp(ffn_low[tokens:], 1).astype(F32)
    outputs = (middle + ffn_out).astype(BF16)

    grad_mid_norm, grad_gain2 = norm_grads(middle, factor2, norm2_gain, grad_normed2)
    grad_middle = cot.astype(F32) + grad_mid_norm
    grad_attn = grad_middle.astype(BF16)
    grad_context = matmul(grad_attn, w_out_t).astype(BF16)
    grad_q, bias_grads, dkv = attend_grads(
        info,
        qkv,
        others,
        seg_q_row,
        seg_k_column,
        table,
        context,
        lse,
        grad_context.reshape(groups, own_length, inner),
        block,
        head_size,
    )
    grad_kv = add_low(dkv[0], *[swap_mp(dkv[k], k) for k in range(1, mp)])
    grad_qkv = jnp.concatenate(
        [
            grad_q.reshape(tokens, inner),
            grad_kv[:, 0].reshape(tokens, inner),
            grad_kv[:, 1].reshape(tokens, inner),
        ],
        axis=1,
    )
    grad_normed1 = matmul_t(grad_qkv, w_qkv)
    grad_in_norm, grad_gain1 = norm_grads(layer_in, factor1, norm1_gain, grad_normed1)
    grad_inputs = (grad_middle + grad_in_norm).astype(BF16)
    attention_grads = jnp.concatenate(
        [outer(normed1, grad_qkv).astype(BF16), outer(grad_attn, context_flat).astype(BF16)], axis=1
    )
    attention_sum = scatter_attention(attention_grads, z, y, core, x).astype(F32)

    ffn_sums = jnp.concatenate(reduced, axis=2).reshape(3, 2, own_rows, half_units)
    kept = pick(ffn_sums, core, 1)
    got = swap_dp(pick(ffn_sums, 1 - core, 1), 1)
    ffn_grads = place([kept, got], core, 2).reshape(3, own_rows, own_units).astype(F32)

    bias_flat = bias_grads[:, :, 0, :]
    left = jnp.pad(bias_flat[:, :, :block], ((0, 0), (0, 1), (0, 0)))
    right = jnp.pad(bias_flat[:, :, block:], ((0, 0), (1, 0), (0, 0)))
    offsets_total = (left + right).reshape(head_count, 2 * k_blocks * block)
    bucket_part = jnp.dot(bucket_hot.T, offsets_total.T, precision=TOP_PRECISION)
    rel_part = jnp.dot(bucket_part, head_hot, precision=TOP_PRECISION)
    grad_norm1, grad_norm2, grad_rel = lax.psum((grad_gain1, grad_gain2, rel_part), ("dp", "mp"))
    shape = inputs.shape
    return (
        outputs.reshape(shape),
        grad_inputs.reshape(shape),
        grad_rel,
        grad_norm1,
        grad_norm2,
        attention_sum[:, :inner],
        attention_sum[:, inner : 2 * inner],
        attention_sum[:, 2 * inner : 3 * inner],
        jnp.transpose(attention_sum[:, 3 * inner :]),
        ffn_grads[0],
        ffn_grads[1],
        jnp.transpose(ffn_grads[2]),
    )


def solution(mesh):
    return jax.shard_map(
        body,
        mesh=mesh,
        in_specs=(
            P(None, "dp", "mp", None),
            P(None, "dp", "mp", None),
            P(None, "dp", None),
            P(),
            P(),
            P(),
            P(),
            P(),
            P("dp", None),
            P("dp", None),
            P("dp", None),
            P(None, "dp"),
            P("dp", "mp"),
            P("dp", "mp"),
            P("mp", "dp"),
        ),
        out_specs=(
            P(None, "dp", "mp", None),
            P(None, "dp", "mp", None),
            P(),
            P(),
            P(),
            P("dp", None),
            P("dp", None),
            P("dp", None),
            P(None, "dp"),
            P("dp", "mp"),
            P("dp", "mp"),
            P("mp", "dp"),
        ),
        check_vma=False,
    )
```

```python
import functools

import jax
import jax.numpy as jnp
from jax import lax
from jax.experimental import pallas as pl
from jax.experimental.pallas import tpu as pltpu
from jax.sharding import PartitionSpec as P

EPSILON = 1e-06
TOP_PRECISION = lax.Precision.HIGHEST
GELU_SCALE = 0.7978845608028654
GELU_CUBE = 0.044715
BF16 = jnp.bfloat16
F32 = jnp.float32
NEGATIVE = -1e30
VMEM_BYTES = 60 * 1024 * 1024
LANES = 128


def swap_dp(array, mask):
    count = lax.axis_size("dp")
    return lax.ppermute(array, "dp", [(i, i ^ mask) for i in range(count)])


def swap_mp(array, mask):
    count = lax.axis_size("mp")
    return lax.ppermute(array, "mp", [(i, i ^ mask) for i in range(count)])


def pick(array, index, axis):
    return lax.dynamic_index_in_dim(array, index, axis, keepdims=False)


def add_low(*terms):
    total = terms[0].astype(F32)
    for term in terms[1:]:
        total = total + term.astype(F32)
    return total.astype(BF16)


def either(flag, first, second):
    return jnp.where(flag == 0, first, second)


def gather_quads(piece):
    depth, mp = lax.axis_size("dp") // 4, lax.axis_size("mp")
    kinds, rows, columns = piece.shape
    parts = [piece] + [swap_dp(piece, 4 * k) for k in range(1, depth)]
    own = jnp.stack(parts, axis=1).reshape(kinds, depth * rows, columns)
    half = depth * rows // 2
    over_y = swap_dp(own, 2)
    quads = [(own, over_y)]
    for k in range(1, mp):
        over_x = swap_mp(own, k)
        quads.append(
            (over_x, swap_mp(over_y[:, :half], k), swap_dp(over_x[:, half:], 2))
        )
    return quads


def scatter_quads(quads):
    depth = lax.axis_size("dp") // 4
    own, to_y = quads[0]
    kinds, wide, columns = own.shape
    half = wide // 2
    low = to_y[:, :half]
    high = to_y[:, half:]
    terms = [own]
    for k, (to_x, first, second) in enumerate(quads[1:], 1):
        low = add_low(low, swap_mp(first, k))
        to_x = jnp.concatenate(
            [to_x[:, :half], add_low(to_x[:, half:], swap_dp(second, 2))], axis=1
        )
        terms.append(swap_mp(to_x, k))
    terms.append(swap_dp(jnp.concatenate([low, high], axis=1), 2))
    total = add_low(*terms).reshape(kinds, depth, wide // depth, columns)
    return add_low(total[:, 0], *[swap_dp(total[:, k], 4 * k) for k in range(1, depth)])


def sum_all(values):
    mask = 1
    while mask < lax.axis_size("dp"):
        values = values + swap_dp(values, mask)
        mask *= 2
    mask = 1
    while mask < lax.axis_size("mp"):
        values = values + swap_mp(values, mask)
        mask *= 2
    return values


def call(kernel, name, grid, in_specs, out_specs, out_shape, operands, flops=0, scratch=(), scalars=0):
    moved = sum(a.size * a.dtype.itemsize for a in operands)
    moved += sum(s.size * s.dtype.itemsize for s in out_shape)
    return pl.pallas_call(
        kernel,
        grid_spec=pltpu.PrefetchScalarGridSpec(
            num_scalar_prefetch=scalars,
            grid=grid,
            in_specs=in_specs,
            out_specs=out_specs,
            scratch_shapes=list(scratch),
        ),
        out_shape=out_shape,
        compiler_params=pltpu.CompilerParams(vmem_limit_bytes=VMEM_BYTES),
        cost_estimate=pl.CostEstimate(flops=flops, bytes_accessed=moved, transcendentals=0),
        name=name,
    )(*operands)


def whole(shape):
    return pl.BlockSpec(shape, lambda *_: (0,) * len(shape), pipeline_mode=pl.Buffered(1))


def slab(*shape):
    return pl.BlockSpec((1,) + shape, lambda m, *_: (m,) + (0,) * len(shape))


def dot_nn(left, right):
    return lax.dot_general(left, right, (((1,), (0,)), ((), ())), preferred_element_type=F32)


def dot_tn(left, right):
    return lax.dot_general(left, right, (((0,), (0,)), ((), ())), preferred_element_type=F32)


def dot_nt(left, right):
    return lax.dot_general(left, right, (((1,), (1,)), ((), ())), preferred_element_type=F32)


def transposed(value):
    return jnp.transpose(value.astype(F32), (1, 0)).astype(BF16)


def block_of(place, position, depth):
    z, y = place // 2, place % 2
    return (z ^ (position % depth)) * 2 + (y ^ (position // depth))


def reorder_kernel(outward, info_ref, in_ref, out_ref):
    blocks = in_ref.shape[1]
    for p in range(blocks):
        chip = block_of(info_ref[0], p, blocks // 2)
        if outward:
            out_ref[0, chip] = in_ref[0, p]
        else:
            out_ref[0, p] = in_ref[0, chip]


def reorder(array, place, blocks, outward):
    groups, wide, length = array.shape
    split = array.reshape(groups, blocks, wide // blocks, length)
    spec = slab(blocks, wide // blocks, length)
    return call(
        functools.partial(reorder_kernel, outward),
        "reorder",
        (groups,),
        [spec],
        [spec],
        [jax.ShapeDtypeStruct(split.shape, array.dtype)],
        [place, split],
        scalars=1,
    )[0].reshape(groups, wide, length)


def bias_kernel(window_ref, table_ref):
    count, block = table_ref.shape[1], table_ref.shape[-1]
    for entry in range(count):
        wide = jnp.broadcast_to(window_ref[0, entry], (block, 2 * block))
        rolled = pltpu.roll(wide, block + 1, 1, stride=1, stride_axis=0)
        table_ref[0, entry] = rolled[:, :block]


def bias_table(windows, block):
    heads, count = windows.shape[:2]
    return call(
        bias_kernel,
        "bias_table",
        (heads,),
        [slab(count, 1, 2 * block)],
        [slab(count, block, block)],
        [jax.ShapeDtypeStruct((heads, count, block, block), F32)],
        [windows],
    )[0]


def project_kernel(x_ref, gain_ref, w_ref, normed_ref, q_ref, kv_ref):
    values = x_ref[0].astype(F32)
    factor = lax.rsqrt(jnp.mean(values * values, axis=0, keepdims=True) + EPSILON)
    normed = (values * factor * gain_ref[...]).astype(BF16)
    normed_ref[0] = normed
    inner = q_ref.shape[1]
    q_ref[0] = dot_tn(w_ref[0], normed).astype(BF16)
    kv_ref[0, :inner] = dot_tn(w_ref[1], normed).astype(BF16)
    kv_ref[0, inner:] = dot_tn(w_ref[2], normed).astype(BF16)


def project(x, gain, weights):
    groups, wide, length = x.shape
    inner = weights.shape[2]
    return call(
        project_kernel,
        "project",
        (groups,),
        [slab(wide, length), whole((wide, 1)), whole(weights.shape)],
        [slab(wide, length), slab(inner, length), slab(2 * inner, length)],
        [
            jax.ShapeDtypeStruct((groups, wide, length), BF16),
            jax.ShapeDtypeStruct((groups, inner, length), BF16),
            jax.ShapeDtypeStruct((groups, 2 * inner, length), BF16),
        ],
        [x, gain, weights],
        flops=6 * groups * wide * length * inner,
    )


def middle_kernel(x_ref, context_ref, w_ref, gain_ref, middle_ref, normed_ref):
    values = x_ref[0].astype(F32) + dot_nn(w_ref[3], context_ref[0])
    middle_ref[0] = values
    factor = lax.rsqrt(jnp.mean(values * values, axis=0, keepdims=True) + EPSILON)
    normed_ref[0] = (values * factor * gain_ref[...]).astype(BF16)


def middle_layer(x, context, weights, gain):
    groups, wide, length = x.shape
    inner = weights.shape[2]
    return call(
        middle_kernel,
        "middle",
        (groups,),
        [slab(wide, length), slab(inner, length), whole(weights.shape), whole((wide, 1))],
        [slab(wide, length), slab(wide, length)],
        [
            jax.ShapeDtypeStruct((groups, wide, length), F32),
            jax.ShapeDtypeStruct((groups, wide, length), BF16),
        ],
        [x, context, weights, gain],
        flops=2 * groups * wide * length * inner,
    )


def lifted_grads(values, gain, grad):
    factor = lax.rsqrt(jnp.mean(values * values, axis=0, keepdims=True) + EPSILON)
    scaled = values * factor
    lifted = grad * gain
    inner = jnp.mean(lifted * scaled, axis=0, keepdims=True)
    return factor * (lifted - scaled * inner), jnp.sum(grad * scaled, axis=1, keepdims=True)


def turn_kernel(
    middle_ref, cot_ref, ffn0_ref, ffn1_ref, back0_ref, back1_ref, gain_ref, w_ref,
    out_ref, grad_ref, low_ref, context_ref, gain_grad_ref,
):
    middle = middle_ref[0]
    out_ref[0] = (middle + ffn0_ref[0].astype(F32) + ffn1_ref[0].astype(F32)).astype(BF16)
    grad = back0_ref[0].astype(F32) + back1_ref[0].astype(F32)
    normed_grad, gain_grad = lifted_grads(middle, gain_ref[...], grad)
    gain_grad_ref[0] = gain_grad
    total = cot_ref[0].astype(F32) + normed_grad
    grad_ref[0] = total
    low = total.astype(BF16)
    low_ref[0] = low
    context_ref[0] = dot_tn(w_ref[3], low).astype(BF16)


def turn(middle, cot, ffn, back, gain, weights):
    groups, wide, length = middle.shape
    inner = weights.shape[2]
    big = slab(wide, length)
    return call(
        turn_kernel,
        "turn",
        (groups,),
        [big] * 6 + [whole((wide, 1)), whole(weights.shape)],
        [big, big, big, slab(inner, length), slab(wide, 1)],
        [
            jax.ShapeDtypeStruct((groups, wide, length), BF16),
            jax.ShapeDtypeStruct((groups, wide, length), F32),
            jax.ShapeDtypeStruct((groups, wide, length), BF16),
            jax.ShapeDtypeStruct((groups, inner, length), BF16),
            jax.ShapeDtypeStruct((groups, wide, 1), F32),
        ],
        [middle, cot, *ffn, *back, gain, weights],
        flops=2 * groups * wide * length * inner,
    )


def attention_weights_kernel(normed_ref, low_ref, context_ref, dq_ref, dkv_ref, out_ref, sum_scr):
    step = pl.program_id(0)
    inner = dq_ref.shape[1]
    terms = (
        (normed_ref, dq_ref[0]),
        (normed_ref, dkv_ref[0, :inner]),
        (normed_ref, dkv_ref[0, inner:]),
        (low_ref, context_ref[0]),
    )
    for r, (left_ref, right) in enumerate(terms):
        product = dot_nt(left_ref[0], right)

        @pl.when(step == 0)
        def _(r=r, product=product):
            sum_scr[r] = product

        @pl.when(step > 0)
        def _(r=r, product=product):
            sum_scr[r] += product

    @pl.when(step == pl.num_programs(0) - 1)
    def _():
        out_ref[...] = sum_scr[...].astype(BF16)


def attention_weight_grads(normed, low, context, dq, dkv):
    groups, wide, length = normed.shape
    inner = context.shape[1]
    return call(
        attention_weights_kernel,
        "attention_weight_grads",
        (groups,),
        [slab(wide, length), slab(wide, length)]
        + [slab(inner, length), slab(inner, length), slab(2 * inner, length)],
        [whole((4, wide, inner))],
        [jax.ShapeDtypeStruct((4, wide, inner), BF16)],
        [normed, low, context, dq, dkv],
        flops=8 * groups * wide * length * inner,
        scratch=[pltpu.VMEM((4, wide, inner), F32)],
    )[0]


def input_kernel(x_ref, grad_ref, dq_ref, dkv_ref, gain_ref, w_ref, out_ref, gain_grad_ref):
    inner = dq_ref.shape[1]
    grad = (
        dot_nn(w_ref[0], dq_ref[0])
        + dot_nn(w_ref[1], dkv_ref[0, :inner])
        + dot_nn(w_ref[2], dkv_ref[0, inner:])
    )
    normed_grad, gain_grad = lifted_grads(x_ref[0].astype(F32), gain_ref[...], grad)
    gain_grad_ref[0] = gain_grad
    out_ref[0] = (grad_ref[0] + normed_grad).astype(BF16)


def input_grads(x, grad, dq, dkv, gain, weights):
    groups, wide, length = x.shape
    inner = weights.shape[2]
    return call(
        input_kernel,
        "input_grads",
        (groups,),
        [slab(wide, length), slab(wide, length), slab(inner, length), slab(2 * inner, length)]
        + [whole((wide, 1)), whole(weights.shape)],
        [slab(wide, length), slab(wide, 1)],
        [
            jax.ShapeDtypeStruct((groups, wide, length), BF16),
            jax.ShapeDtypeStruct((groups, wide, 1), F32),
        ],
        [x, grad, dq, dkv, gain, weights],
        flops=6 * groups * wide * length * inner,
    )


def halves(value_t, half):
    zero = jnp.zeros((half, value_t.shape[1]), value_t.dtype)
    return (
        jnp.concatenate([value_t[:half], zero], axis=0),
        jnp.concatenate([zero, value_t[half:]], axis=0),
    )


def attend_kernel(sources, block, half, info_ref, q_ref, *refs):
    kv_refs = refs[: 2 * sources]
    segq_ref, segk_ref, table_ref, ctx_ref, lse_ref = refs[2 * sources : 2 * sources + 5]
    s_scr, m_scr, l_scr, acc_scr, k_scr = refs[2 * sources + 5 :]
    length = q_ref.shape[2]
    q_blocks = length // block
    k_blocks = q_blocks * sources
    place_x = info_ref[0]
    step = pl.program_id(1)
    for s in range(sources):
        k_scr[s * length : (s + 1) * length, :] = transposed(kv_refs[2 * s][0])
    for qb in range(q_blocks):
        rows = pl.ds(qb * block, block)
        q_heads = halves(q_ref[0, :, rows], half)
        seg_q = segq_ref[0, :, rows]
        m_scr[...] = jnp.full(m_scr.shape, NEGATIVE, F32)
        l_scr[...] = jnp.zeros(l_scr.shape, F32)
        acc_scr[...] = jnp.zeros(acc_scr.shape, F32)
        for kb in range(k_blocks):
            s, lb = divmod(kb, q_blocks)
            live = info_ref[1 + (step * q_blocks + qb) * k_blocks + kb]

            @pl.when(live != 0)
            def _(s=s, lb=lb, kb=kb):
                entry = k_blocks - 1 - ((place_x ^ s) * q_blocks + lb - place_x * q_blocks - qb)
                keys = k_scr[pl.ds(kb * block, block), :]
                kept = segk_ref[0, pl.ds(kb * block, block), :] == seg_q
                for h in range(2):
                    score = dot_nn(keys, q_heads[h]) + table_ref[h, entry]
                    score = jnp.where(kept, score, NEGATIVE)
                    s_scr[h, kb] = score
                    m_scr[h] = jnp.maximum(m_scr[h], jnp.max(score, axis=0, keepdims=True))

        for kb in range(k_blocks):
            s, lb = divmod(kb, q_blocks)
            live = info_ref[1 + (step * q_blocks + qb) * k_blocks + kb]

            @pl.when(live != 0)
            def _(s=s, lb=lb, kb=kb):
                for h in range(2):
                    prob = jnp.exp(s_scr[h, kb] - m_scr[h])
                    l_scr[h] += jnp.sum(prob, axis=0, keepdims=True)
                    values_t = kv_refs[2 * s + 1][
                        0, h * half : (h + 1) * half, lb * block : (lb + 1) * block
                    ]
                    acc_scr[h * half : (h + 1) * half] += dot_nn(values_t, prob.astype(BF16))

        for h in range(2):
            lse_ref[0, 0, h : h + 1, rows] = m_scr[h] + jnp.log(l_scr[h])
            ctx_ref[0, h * half : (h + 1) * half, rows] = (
                acc_scr[h * half : (h + 1) * half] / l_scr[h]
            ).astype(BF16)


def grad_kernel(sources, block, half, info_ref, q_ref, *refs):
    kv_refs = refs[: 2 * sources]
    refs = refs[2 * sources :]
    segq_ref, segk_ref, table_ref, ctx_ref, lse_ref, gctx_ref = refs[:6]
    dq_ref, gbias_ref = refs[6:8]
    dkv_refs = refs[8 : 8 + sources]
    dk_scr, dv_scr, dq_scr, k_scr, v_scr, db_scr = refs[8 + sources :]
    length = q_ref.shape[2]
    q_blocks = length // block
    k_blocks = q_blocks * sources
    place_x = info_ref[0]
    step = pl.program_id(1)
    lane = lax.broadcasted_iota(jnp.int32, (block, 2 * half), 1)

    @pl.when(step == 0)
    def _():
        db_scr[...] = jnp.zeros(db_scr.shape, F32)

    for s in range(sources):
        k_scr[s * length : (s + 1) * length, :] = transposed(kv_refs[2 * s][0])
        v_scr[s * length : (s + 1) * length, :] = transposed(kv_refs[2 * s + 1][0])
    dk_scr[...] = jnp.zeros(dk_scr.shape, F32)
    dv_scr[...] = jnp.zeros(dv_scr.shape, F32)
    for qb in range(q_blocks):
        rows = pl.ds(qb * block, block)
        query_t = q_ref[0, :, rows]
        grad_out_t = gctx_ref[0, :, rows]
        product = grad_out_t.astype(F32) * ctx_ref[0, :, rows].astype(F32)
        deltas = (
            jnp.sum(product[:half], axis=0, keepdims=True),
            jnp.sum(product[half:], axis=0, keepdims=True),
        )
        q_heads = halves(query_t, half)
        g_heads = halves(grad_out_t, half)
        query, grad_out = transposed(query_t), transposed(grad_out_t)
        zero = jnp.zeros(query.shape, BF16)
        q_lanes = (jnp.where(lane < half, query, zero), jnp.where(lane < half, zero, query))
        g_lanes = (
            jnp.where(lane < half, grad_out, zero),
            jnp.where(lane < half, zero, grad_out),
        )
        seg_q = segq_ref[0, :, rows]
        dq_scr[...] = jnp.zeros(dq_scr.shape, F32)
        for kb in range(k_blocks):
            s, lb = divmod(kb, q_blocks)
            live = info_ref[1 + (step * q_blocks + qb) * k_blocks + kb]

            @pl.when(live != 0)
            def _(s=s, lb=lb, kb=kb):
                entry = k_blocks - 1 - ((place_x ^ s) * q_blocks + lb - place_x * q_blocks - qb)
                key_rows = pl.ds(kb * block, block)
                keys = k_scr[key_rows, :]
                values = v_scr[key_rows, :]
                kept = segk_ref[0, key_rows, :] == seg_q
                key_grad = dk_scr[key_rows, :]
                value_grad = dv_scr[key_rows, :]
                for h in range(2):
                    score = dot_nn(keys, q_heads[h]) + table_ref[h, entry]
                    score = jnp.where(kept, score, NEGATIVE)
                    prob = jnp.exp(score - lse_ref[0, 0, h : h + 1, rows])
                    grad_prob = dot_nn(values, g_heads[h])
                    grad_score = prob * (grad_prob - deltas[h])
                    db_scr[h, entry] += grad_score
                    low = grad_score.astype(BF16)
                    key_grad = key_grad + dot_nn(low, q_lanes[h])
                    value_grad = value_grad + dot_nn(prob.astype(BF16), g_lanes[h])
                    keys_t = kv_refs[2 * s][
                        0, h * half : (h + 1) * half, lb * block : (lb + 1) * block
                    ]
                    dq_scr[h * half : (h + 1) * half] += dot_nn(keys_t, low)
                dk_scr[key_rows, :] = key_grad
                dv_scr[key_rows, :] = value_grad

        dq_ref[0, :, rows] = dq_scr[...].astype(BF16)
    for s in range(sources):
        rows = slice(s * length, (s + 1) * length)
        dkv_refs[s][0, 0] = jnp.transpose(dk_scr[rows, :], (1, 0)).astype(BF16)
        dkv_refs[s][0, 1] = jnp.transpose(dv_scr[rows, :], (1, 0)).astype(BF16)

    @pl.when(step == pl.num_programs(1) - 1)
    def _():
        for h in range(2):
            for entry in range(2 * k_blocks - 1):
                tile = db_scr[h, entry]
                tile = jnp.concatenate([tile, jnp.zeros_like(tile)], axis=1)
                count = block
                while count > 8:
                    count //= 2
                    tile = pltpu.roll(tile[:count], count, 1) + tile[count:]
                total = tile[7:8]
                for t in range(7):
                    total = total + pltpu.roll(tile[t : t + 1], 7 - t, 1)
                gbias_ref[h, entry] = total


def attention_specs(sources, length, block, pairs, width):
    k_blocks = length * sources // block
    entries = 2 * k_blocks - 1

    def rows(offset):
        return pl.BlockSpec((1, width, length), lambda p, m, info: (m, p + offset, 0))

    kv_specs = [rows(0), rows(pairs)] * sources
    seg_specs = [
        pl.BlockSpec((1, 1, length), lambda p, m, info: (m, 0, 0)),
        pl.BlockSpec((1, length * sources, 1), lambda p, m, info: (m, 0, 0)),
    ]
    table_spec = pl.BlockSpec((2, entries, block, block), lambda p, m, info: (p, 0, 0, 0))
    lse_spec = pl.BlockSpec((1, 1, 8, length), lambda p, m, info: (m, p, 0, 0))
    return k_blocks, entries, rows, kv_specs, seg_specs, table_spec, lse_spec


def attend(info, q, kvs, seg_q, seg_k, table, block, head_size):
    micro, inner, length = q.shape
    sources = len(kvs)
    width = 2 * head_size
    pairs = inner // width
    k_blocks, entries, rows, kv_specs, seg_specs, table_spec, lse_spec = attention_specs(
        sources, length, block, pairs, width
    )
    return call(
        functools.partial(attend_kernel, sources, block, head_size),
        "attend",
        (pairs, micro),
        [rows(0)] + kv_specs + seg_specs + [table_spec],
        [rows(0), lse_spec],
        [
            jax.ShapeDtypeStruct((micro, inner, length), BF16),
            jax.ShapeDtypeStruct((micro, pairs, 8, length), F32),
        ],
        [info, q, *[kv for kv in kvs for _ in range(2)], seg_q, seg_k, table],
        flops=16 * micro * inner * length * length * sources,
        scratch=[
            pltpu.VMEM((2, k_blocks, block, block), F32),
            pltpu.VMEM((2, 1, block), F32),
            pltpu.VMEM((2, 1, block), F32),
            pltpu.VMEM((width, block), F32),
            pltpu.VMEM((length * sources, width), BF16),
        ],
        scalars=1,
    )


def attend_grads(info, q, kvs, seg_q, seg_k, table, context, lse, grad_context, block, head_size):
    micro, inner, length = q.shape
    sources = len(kvs)
    width = 2 * head_size
    pairs = inner // width
    k_blocks, entries, rows, kv_specs, seg_specs, table_spec, lse_spec = attention_specs(
        sources, length, block, pairs, width
    )
    dkv_spec = pl.BlockSpec((1, 2, width, length), lambda p, m, info: (m, 0, p, 0))
    results = call(
        functools.partial(grad_kernel, sources, block, head_size),
        "attend_grads",
        (pairs, micro),
        [rows(0)] + kv_specs + seg_specs + [table_spec, rows(0), lse_spec, rows(0)],
        [
            rows(0),
            pl.BlockSpec((2, entries, 1, 2 * block), lambda p, m, info: (p, 0, 0, 0)),
        ]
        + [dkv_spec] * sources,
        [
            jax.ShapeDtypeStruct((micro, inner, length), BF16),
            jax.ShapeDtypeStruct((2 * pairs, entries, 1, 2 * block), F32),
        ]
        + [jax.ShapeDtypeStruct((micro, 2, inner, length), BF16)] * sources,
        [info, q, *[kv for kv in kvs for _ in range(2)], seg_q, seg_k, table]
        + [context, lse, grad_context],
        flops=32 * micro * inner * length * length * sources,
        scratch=[
            pltpu.VMEM((length * sources, width), F32),
            pltpu.VMEM((length * sources, width), F32),
            pltpu.VMEM((width, block), F32),
            pltpu.VMEM((length * sources, width), BF16),
            pltpu.VMEM((length * sources, width), BF16),
            pltpu.VMEM((2, entries, block, block), F32),
        ],
        scalars=1,
    )
    return results[0], results[1], results[2:]


def gelu_terms(gate, upward, grad_hidden):
    square = gate * gate
    tanh = jnp.tanh(GELU_SCALE * gate * (1.0 + GELU_CUBE * square))
    half = 0.5 + 0.5 * tanh
    gelu = gate * half
    slope = half + 0.5 * gate * (1.0 - tanh * tanh) * (
        GELU_SCALE + 3.0 * GELU_CUBE * GELU_SCALE * square
    )
    return (
        (gelu * upward).astype(BF16),
        (grad_hidden * upward * slope).astype(BF16),
        (grad_hidden * gelu).astype(BF16),
    )


def joined(parts, axis):
    return parts[0] if len(parts) == 1 else jnp.concatenate(parts, axis=axis)


def source_rows(refs, kind, columns):
    return joined([ref[kind][:, columns] for ref in refs], 0)


def batches_of(sources, tile):
    if tile % LANES:
        return [[s] for s in range(sources)]
    return [list(range(s, min(s + 2, sources))) for s in range(0, sources, 2)]


def split_refs(refs, counts):
    result, start = [], 0
    for count in counts:
        result.append(refs[start : start + count])
        start += count
    return result, refs[start:]


def ffn_kernel(counts, *refs):
    sources, refs = split_refs(refs, counts)
    (normed_own, normed_far, cot_own, cot_far, hid_ref, ggi_ref, gui_ref), refs = refs[:7], refs[7:]
    grads, _ = split_refs(refs, counts)
    tile = sources[0][0].shape[2]
    micro = normed_own.shape[0]
    normed = [(ref, m) for ref in (normed_own, normed_far) for m in range(micro)]
    cot = [(ref, m) for ref in (cot_own, cot_far) for m in range(micro)]
    start = 0
    for batch in batches_of(len(sources), tile):
        units = tile * len(batch)
        rows = slice(start, start + units)
        start += units
        weights = [
            joined([source_rows(sources[s], kind, slice(None)) for s in batch], 1)
            for kind in range(3)
        ]
        for g in range(2 * micro):
            ref, m = normed[g]
            gate = dot_tn(weights[0], ref[m])
            upward = dot_tn(weights[1], ref[m])
            ref, m = cot[g]
            grad_hidden = dot_tn(weights[2], ref[m])
            hidden, grad_gate, grad_up = gelu_terms(gate, upward, grad_hidden)
            hid_ref[g, rows] = hidden
            ggi_ref[g, rows] = grad_gate
            gui_ref[g, rows] = grad_up
        for kind, (left, right_ref) in enumerate(((normed, ggi_ref), (normed, gui_ref), (cot, hid_ref))):
            total = None
            for g in range(2 * micro):
                ref, m = left[g]
                product = dot_nt(ref[m], right_ref[g, rows])
                total = product if total is None else total + product
            total = total.astype(BF16)
            for n, s in enumerate(batch):
                row = 0
                for ref in grads[s]:
                    depth = ref.shape[1]
                    ref[kind] = total[row : row + depth, n * tile : (n + 1) * tile]
                    row += depth


def tile_of(columns):
    return LANES if columns % LANES == 0 else columns


def ffn_chunk(quads, normed_own, normed_far, cot_own, cot_far):
    micro, wide, length = normed_own.shape
    columns = quads[0][0].shape[2]
    tile = tile_of(columns)
    counts = [len(parts) for parts in quads]
    flat = [part for parts in quads for part in parts]
    part_specs = [
        pl.BlockSpec((3, part.shape[1], tile), lambda j: (0, 0, j)) for part in flat
    ]
    units = len(quads) * tile
    act_spec = pl.BlockSpec((2 * micro, units, length), lambda j: (0, j, 0))
    act_shape = jax.ShapeDtypeStruct((2 * micro, len(quads) * columns, length), BF16)
    results = call(
        functools.partial(ffn_kernel, counts),
        "ffn_chunk",
        (columns // tile,),
        part_specs + [whole(normed_own.shape)] * 4,
        [act_spec] * 3 + part_specs,
        [act_shape] * 3 + [jax.ShapeDtypeStruct(part.shape, BF16) for part in flat],
        [*flat, normed_own, normed_far, cot_own, cot_far],
        flops=24 * micro * length * wide * len(quads) * columns,
    )
    grads, _ = split_refs(results[3:], counts)
    return results[:3], grads


def down_kernel(layout, *refs):
    chunks = []
    for counts in layout:
        sources, refs = split_refs(refs, counts)
        acts, refs = refs[:3], refs[3:]
        chunks.append((sources, acts))
    ffn_own, ffn_far, back_own, back_far = refs
    group = pl.program_id(0)
    micro = pl.num_programs(0) // 2
    totals = [None, None]
    for sources, acts in chunks:
        columns = sources[0][0].shape[2]
        tile = tile_of(columns)
        pieces = [(j, s) for j in range(columns // tile) for s in range(len(sources))]
        if tile % LANES == 0:
            pieces = [pieces]
        else:
            pieces = [[piece] for piece in pieces]
        for kind, act, which in ((2, 0, 0), (0, 1, 1), (1, 2, 1)):
            row = 0
            for group_of in pieces:
                left = joined(
                    [
                        source_rows(sources[s], kind, slice(j * tile, (j + 1) * tile))
                        for j, s in group_of
                    ],
                    1,
                )
                right = acts[act][0, row : row + left.shape[1]]
                row += left.shape[1]
                product = dot_nn(left, right)
                totals[which] = product if totals[which] is None else totals[which] + product

    @pl.when(group < micro)
    def _():
        ffn_own[0] = totals[0].astype(BF16)
        back_own[0] = totals[1].astype(BF16)

    @pl.when(group >= micro)
    def _():
        ffn_far[0] = totals[0].astype(BF16)
        back_far[0] = totals[1].astype(BF16)


def down(chunk_quads, chunk_acts, wide):
    groups, _, length = chunk_acts[0][0].shape
    micro = groups // 2
    operands, specs, layout = [], [], []
    flops = 0
    for quads, acts in zip(chunk_quads, chunk_acts):
        layout.append([len(parts) for parts in quads])
        flat = [part for parts in quads for part in parts]
        operands += flat + list(acts)
        specs += [whole(part.shape) for part in flat]
        specs += [slab(act.shape[1], length) for act in acts]
        flops += 6 * groups * length * wide * acts[0].shape[1]
    own_spec = pl.BlockSpec((1, wide, length), lambda g: (jnp.minimum(g, micro - 1), 0, 0))
    far_spec = pl.BlockSpec((1, wide, length), lambda g: (jnp.maximum(g - micro, 0), 0, 0))
    return call(
        functools.partial(down_kernel, layout),
        "down",
        (groups,),
        specs,
        [own_spec, far_spec, own_spec, far_spec],
        [jax.ShapeDtypeStruct((micro, wide, length), BF16)] * 4,
        operands,
        flops=flops,
    )


def body(
    inputs,
    cotangent,
    segments,
    rel_bucket,
    head_order,
    rel_table,
    norm1_gain,
    norm2_gain,
    w_query,
    w_key,
    w_value,
    output_weight,
    w_gate,
    w_up,
    w_down,
):
    dp, mp = lax.axis_size("dp"), lax.axis_size("mp")
    x = lax.axis_index("mp")
    dp_place = lax.axis_index("dp")
    core, chip = dp_place & 1, dp_place >> 1
    chips, depth = dp // 2, dp // 4
    micro, rows, own_length, model = inputs.shape
    groups = micro * rows
    length = own_length * mp
    bucket_count, head_count = rel_table.shape
    inner = w_query.shape[1]
    head_size = inner // head_count
    block = min(256, own_length)
    q_blocks, k_blocks = own_length // block, length // block
    own_rows, own_units = w_gate.shape
    half_units = own_units // 2
    chip_rows = 2 * own_rows
    place = chip.reshape(1).astype(jnp.int32)

    def inward(array):
        return reorder(array, place, chips, False)

    def feature_major(array):
        return jnp.transpose(array.reshape(groups, own_length, model), (0, 2, 1))

    part = 4 * inner // (2 * mp)
    shard = jnp.concatenate([w_query, w_key, w_value, jnp.transpose(output_weight)], axis=1)
    kept = lax.dynamic_slice_in_dim(shard, (2 * x + core) * part, part, 1)
    sent = lax.dynamic_slice_in_dim(shard, (2 * x + 1 - core) * part, part, 1)
    got = swap_dp(sent, 1)
    attention_piece = either(
        core, jnp.concatenate([kept, got], axis=0), jnp.concatenate([got, kept], axis=0)
    )[None]
    attention_quads = gather_quads(attention_piece)
    near = jnp.concatenate([jnp.concatenate(parts, axis=1) for parts in attention_quads], axis=0)
    far = swap_dp(near, 1)
    parts_all = jnp.stack([near, far], axis=1).reshape(2 * mp, model, part)
    ordered = jnp.concatenate(
        [
            lax.dynamic_slice_in_dim(parts_all, (2 * x + core) ^ r, 1, 0)
            for r in range(2 * mp)
        ],
        axis=0,
    )
    attention_weights = jnp.transpose(
        ordered.reshape(4, inner // part, model, part), (0, 2, 1, 3)
    ).reshape(4, model, inner)

    ffn_shard = jnp.stack([w_gate, w_up, jnp.transpose(w_down)])
    low_half, high_half = ffn_shard[:, :, :half_units], ffn_shard[:, :, half_units:]
    kept = either(core, low_half, high_half)
    got = swap_dp(either(core, high_half, low_half), 1)
    ffn_piece = either(
        core, jnp.concatenate([kept, got], axis=1), jnp.concatenate([got, kept], axis=1)
    )
    if half_units % LANES == 0:
        first = half_units // LANES * 3 // 7 * LANES
        bounds = [0, first, half_units] if first else [0, half_units]
    else:
        bounds = [0, half_units]
    spans = list(zip(bounds[:-1], bounds[1:]))
    chunk_quads = [gather_quads(ffn_piece[:, :, a:b]) for a, b in spans]

    bucket_rev = jnp.concatenate([rel_bucket[::-1], jnp.full((1,), -1, jnp.int32)])
    bucket_hot = (bucket_rev[:, None] == jnp.arange(bucket_count, dtype=jnp.int32)[None, :]).astype(F32)
    head_hot = (head_order[:, None] == jnp.arange(head_count, dtype=jnp.int32)[None, :]).astype(F32)
    offset_table = jnp.dot(bucket_hot, rel_table, precision=TOP_PRECISION)
    offset_bias = jnp.dot(head_hot, offset_table.T, precision=TOP_PRECISION)
    bias_blocks = offset_bias.reshape(head_count, 2 * k_blocks, block)
    windows = jnp.concatenate([bias_blocks[:, :-1], bias_blocks[:, 1:]], axis=2)
    table = bias_table(windows[:, :, None, :], block)

    seg_flat = segments.reshape(groups, length)
    seg_q = lax.dynamic_slice_in_dim(seg_flat, x * own_length, own_length, 1)
    seg_parts = seg_flat.reshape(groups, mp, own_length)
    seg_k = jnp.concatenate([pick(seg_parts, x ^ k, 1) for k in range(mp)], axis=1)
    q_edges = seg_q.reshape(groups, q_blocks, block)
    k_edges = seg_k.reshape(groups, k_blocks, block)
    live = (q_edges[:, :, None, 0] <= k_edges[:, None, :, -1]) & (
        k_edges[:, None, :, 0] <= q_edges[:, :, None, -1]
    )
    info = jnp.concatenate([x.reshape(1).astype(jnp.int32), live.reshape(-1).astype(jnp.int32)])
    seg_q_row = seg_q.reshape(groups, 1, own_length)
    seg_k_column = seg_k.reshape(groups, length, 1)

    gains = inward(jnp.stack([norm1_gain, norm2_gain], axis=1)[None])[0]
    gain1, gain2 = gains[:, :1], gains[:, 1:]
    layer_in = inward(feature_major(inputs))
    cot = inward(feature_major(cotangent))
    cot_far = swap_dp(cot, 1)
    normed1, q, own_kv = project(layer_in, gain1, attention_weights)
    kvs = [own_kv] + [swap_mp(own_kv, k) for k in range(1, mp)]
    context, lse = attend(info, q, kvs, seg_q_row, seg_k_column, table, block, head_size)
    middle, normed2 = middle_layer(layer_in, context, attention_weights, gain2)
    normed2_far = swap_dp(normed2, 1)

    chunk_acts, reduced = [], []
    for quads in chunk_quads:
        acts, grads = ffn_chunk(quads, normed2, normed2_far, cot, cot_far)
        chunk_acts.append(acts)
        reduced.append(scatter_quads(grads))
    ffn_own, ffn_far, back_own, back_far = down(chunk_quads, chunk_acts, model)
    back = (back_own, swap_dp(back_far, 1))
    ffn = (ffn_own, swap_dp(ffn_far, 1))

    outputs, grad_middle, grad_attn, grad_context, gain2_grads = turn(
        middle, cot, ffn, back, gain2, attention_weights
    )
    grad_q, bias_grads, dkv = attend_grads(
        info,
        q,
        kvs,
        seg_q_row,
        seg_k_column,
        table,
        context,
        lse,
        grad_context,
        block,
        head_size,
    )
    grad_kv = add_low(dkv[0], *[swap_mp(dkv[k], k) for k in range(1, mp)])
    grad_kv = grad_kv.reshape(groups, 2 * inner, own_length)
    weight_grads = attention_weight_grads(normed1, grad_attn, context, grad_q, grad_kv)
    grad_inputs, gain1_grads = input_grads(
        layer_in, grad_middle, grad_q, grad_kv, gain1, attention_weights
    )

    by_part = jnp.transpose(
        weight_grads.reshape(4, model, inner // part, part), (0, 2, 1, 3)
    ).reshape(mp, 2, model, part)
    near = add_low(pick(by_part, core, 1), swap_dp(pick(by_part, 1 - core, 1), 1))
    half = model // 2
    quads = []
    for k in range(mp):
        matrix = pick(near, x ^ k, 0)[None]
        if k == 0:
            quads.append((matrix[:, :half], matrix[:, half:]))
        else:
            quads.append(
                (matrix[:, :half], matrix[:, half : half + half // 2], matrix[:, half + half // 2 :])
            )
    piece = scatter_quads(quads)[0]
    over_x = jnp.stack([piece] + [swap_mp(piece, k) for k in range(1, mp)])
    kept = either(core, over_x[:, :own_rows], over_x[:, own_rows:])
    got = swap_dp(either(core, over_x[:, own_rows:], over_x[:, :own_rows]), 1)
    both = jnp.stack([kept, got], axis=1).reshape(2 * mp, own_rows, part)
    final = jnp.concatenate(
        [pick(both, (2 * x + core) ^ r, 0) for r in range(2 * mp)], axis=1
    ).astype(F32)

    sums = jnp.concatenate(reduced, axis=2)
    kept = either(core, sums[:, :own_rows], sums[:, own_rows:])
    got = swap_dp(either(core, sums[:, own_rows:], sums[:, :own_rows]), 1)
    ffn_grads = either(
        core, jnp.concatenate([kept, got], axis=2), jnp.concatenate([got, kept], axis=2)
    ).astype(F32)

    bias_flat = bias_grads[:, :, 0, :]
    left = jnp.pad(bias_flat[:, :, :block], ((0, 0), (0, 1), (0, 0)))
    right = jnp.pad(bias_flat[:, :, block:], ((0, 0), (1, 0), (0, 0)))
    offsets_total = (left + right).reshape(head_count, 2 * k_blocks * block)
    bucket_part = jnp.dot(bucket_hot.T, offsets_total.T, precision=TOP_PRECISION)
    rel_part = jnp.dot(bucket_part, head_hot, precision=TOP_PRECISION)
    gain_parts = jnp.stack([jnp.sum(gain1_grads[..., 0], 0), jnp.sum(gain2_grads[..., 0], 0)], axis=1)
    gain_parts = reorder(gain_parts[None], place, chips, True)[0]
    small = jnp.concatenate([gain_parts[:, 0], gain_parts[:, 1], rel_part.reshape(-1)])
    small = sum_all(small)

    shape = inputs.shape

    def placed(array):
        array = reorder(array, place, chips, True)
        return jnp.transpose(array, (0, 2, 1)).reshape(shape)

    return (
        placed(outputs),
        placed(grad_inputs),
        small[2 * model :].reshape(rel_table.shape),
        small[:model],
        small[model : 2 * model],
        final[:, :inner],
        final[:, inner : 2 * inner],
        final[:, 2 * inner : 3 * inner],
        jnp.transpose(final[:, 3 * inner :]),
        ffn_grads[0],
        ffn_grads[1],
        jnp.transpose(ffn_grads[2]),
    )


def solution(mesh):
    return jax.shard_map(
        body,
        mesh=mesh,
        in_specs=(
            P(None, "dp", "mp", None),
            P(None, "dp", "mp", None),
            P(None, "dp", None),
            P(),
            P(),
            P(),
            P(),
            P(),
            P("dp", None),
            P("dp", None),
            P("dp", None),
            P(None, "dp"),
            P("dp", "mp"),
            P("dp", "mp"),
            P("mp", "dp"),
        ),
        out_specs=(
            P(None, "dp", "mp", None),
            P(None, "dp", "mp", None),
            P(),
            P(),
            P(),
            P("dp", None),
            P("dp", None),
            P("dp", None),
            P(None, "dp"),
            P("dp", "mp"),
            P("dp", "mp"),
            P("mp", "dp"),
        ),
        check_vma=False,
    )
```

```python
import functools

import jax
import jax.numpy as jnp
from jax import lax
from jax.experimental import pallas as pl
from jax.experimental.pallas import tpu as pltpu
from jax.sharding import PartitionSpec as P

EPSILON = 1e-06
TOP_PRECISION = lax.Precision.HIGHEST
GELU_SCALE = 0.7978845608028654
GELU_CUBE = 0.044715
BF16 = jnp.bfloat16
F32 = jnp.float32
NEGATIVE = -1e30
VMEM_BYTES = 60 * 1024 * 1024
LANES = 128
COST_SHARE = 0.05


DP = ("chip", "core")


def dp_size():
    return lax.axis_size("chip") * lax.axis_size("core")


def swap_dp(array, mask):
    return lax.ppermute(array, DP, [(i, i ^ mask) for i in range(dp_size())])


def swap_mp(array, mask):
    count = lax.axis_size("mp")
    return lax.ppermute(array, "mp", [(i, i ^ mask) for i in range(count)])


def pick(array, index, axis):
    return lax.dynamic_index_in_dim(array, index, axis, keepdims=False)


def add_low(*terms):
    total = terms[0].astype(F32)
    for term in terms[1:]:
        total = total + term.astype(F32)
    return total.astype(BF16)


def first_of(parts):
    return parts[0] if isinstance(parts, tuple) else parts


def either(flag, first, second):
    return jnp.where(flag == 0, first, second)


def hold(value, *tokens):
    return lax.optimization_barrier((value, *tokens))[0] if tokens else value


def z_masks():
    masks, mask = [], dp_size() // 2
    while mask > 2:
        masks.append(mask)
        mask //= 2
    return masks


def x_masks():
    return range(1, lax.axis_size("mp"))


def merged(parts):
    kinds, rows, columns = parts[0].shape
    return jnp.stack(parts, axis=1).reshape(kinds, len(parts) * rows, columns)


def gather_xy(own, first=(), then=()):
    own = hold(own, *first)
    return hold((swap_dp(own, 2), [swap_mp(own, k) for k in x_masks()]), *then)


def gather_corner(over_y, over_x, first=(), then=()):
    half = over_y.shape[1] // 2
    low = hold(rows_of(over_y, 0, half), *first)
    result = []
    for k, other in zip(x_masks(), over_x):
        high = hold(rows_of(other, half, half), *first)
        result.append((swap_mp(low, k), swap_dp(high, 2)))
    return hold(result, *then)


def quads_of(own, over_y, over_x, corner):
    return [(own, over_y)] + [(other, *parts) for other, parts in zip(over_x, corner)]


def scatter_corner(quads, first=(), then=()):
    own, to_y = quads[0]
    got = []
    for k, (_, low, high) in zip(x_masks(), quads[1:]):
        got.append((swap_mp(hold(low, *first), k), swap_dp(hold(high, *first), 2)))
    got = hold(got, *then)
    if len(got) == 1:
        to_y, to_x = add_corner(to_y, got[0][0], quads[1][0], got[0][1])
        return own, to_y, [to_x]
    half = own.shape[1] // 2
    low = add_low(to_y[:, :half], *[part for part, _ in got])
    to_x = [
        jnp.concatenate([parts[0][:, :half], add_low(parts[0][:, half:], part)], axis=1)
        for parts, (_, part) in zip(quads[1:], got)
    ]
    return own, jnp.concatenate([low, to_y[:, half:]], axis=1), to_x


def scatter_xy(own, to_y, to_x, then=()):
    got = [swap_dp(to_y, 2)] + [swap_mp(other, k) for k, other in zip(x_masks(), to_x)]
    return sum_rows([own, *hold(got, *then)], 2)


def scatter_z(pair, stage, then=()):
    masks = z_masks()
    mask = masks[len(masks) - 1 - stage]
    got = hold(swap_dp(pair[1], mask), *then)
    return sum_rows([pair[0], got], 1 if stage == len(masks) - 1 else 2)


def sum_all(values, late):
    mask = 1
    while mask < lax.axis_size("mp"):
        values = values + swap_mp(values, mask)
        mask *= 2
    mask = 1
    while mask < dp_size():
        values = values + swap_dp(hold(values, *late) if mask > 2 else values, mask)
        mask *= 2
    return values


def call(
    kernel, name, grid, in_specs, out_specs, out_shape, operands, flops=0, scratch=(), scalars=0, after=(),
    aliases=None,
):
    moved = sum(a.size * a.dtype.itemsize for a in operands)
    moved += sum(s.size * s.dtype.itemsize for s in out_shape)
    count = len(operands)

    def run(*refs):
        kernel(*refs[:count], *refs[count + len(after) :])

    return pl.pallas_call(
        run,
        grid_spec=pltpu.PrefetchScalarGridSpec(
            num_scalar_prefetch=scalars,
            grid=grid,
            in_specs=list(in_specs) + [pl.BlockSpec(memory_space=pl.ANY)] * len(after),
            out_specs=out_specs,
            scratch_shapes=list(scratch),
        ),
        out_shape=out_shape,
        input_output_aliases=aliases or {},
        compiler_params=pltpu.CompilerParams(vmem_limit_bytes=VMEM_BYTES),
        cost_estimate=pl.CostEstimate(
            flops=int(flops * COST_SHARE),
            bytes_accessed=int(moved * COST_SHARE),
            transcendentals=0,
        ),
        name=name,
    )(*operands, *after)


def whole(shape):
    return pl.BlockSpec(shape, lambda *_: (0,) * len(shape), pipeline_mode=pl.Buffered(1))


def slab(*shape):
    return pl.BlockSpec((1,) + shape, lambda m, *_: (m,) + (0,) * len(shape))


def columns(wide, step):
    return pl.BlockSpec((wide, step), lambda j, *_: (0, j))


def lane_step(length):
    return 256 if length % 256 == 0 else length


def dot_nn(left, right):
    return lax.dot_general(left, right, (((1,), (0,)), ((), ())), preferred_element_type=F32)


def dot_tn(left, right):
    return lax.dot_general(left, right, (((0,), (0,)), ((), ())), preferred_element_type=F32)


def dot_nt(left, right):
    return lax.dot_general(left, right, (((1,), (1,)), ((), ())), preferred_element_type=F32)


def transposed(value):
    return jnp.transpose(value.astype(F32), (1, 0)).astype(BF16)


def block_of(place, position, depth):
    z, y = place // 2, place % 2
    masks, left, mask = 0, position % depth, depth
    while mask > 1:
        mask //= 2
        masks += mask * (left % 2)
        left //= 2
    return (z ^ masks) * 2 + (y ^ (position // depth))


def reorder_kernel(outward, info_ref, in_ref, out_ref):
    blocks = out_ref.shape[0]
    for p in range(blocks):
        chip = block_of(info_ref[0], p, blocks // 2)
        if outward:
            out_ref[chip] = in_ref[0, p]
        else:
            out_ref[p] = in_ref[0, chip]


def reorder(array, group, place, blocks, outward, after=()):
    groups, wide, length = array.shape
    split = array.reshape(groups, blocks, wide // blocks, length)
    return call(
        functools.partial(reorder_kernel, outward),
        "reorder",
        (1,),
        [pl.BlockSpec((1,) + split.shape[1:], lambda *_: (group, 0, 0, 0))],
        [pl.BlockSpec(split.shape[1:], lambda *_: (0, 0, 0))],
        [jax.ShapeDtypeStruct(split.shape[1:], array.dtype)],
        [place, split],
        scalars=1,
        after=after,
    )[0].reshape(wide, length)


def bias_kernel(window_ref, table_ref):
    count, block = table_ref.shape[1], table_ref.shape[-1]
    for entry in range(count):
        wide = jnp.broadcast_to(window_ref[0, entry], (block, 2 * block))
        rolled = pltpu.roll(wide, block + 1, 1, stride=1, stride_axis=0)
        table_ref[0, entry] = rolled[:, :block]


def bias_table(windows, block, after):
    heads, count = windows.shape[:2]
    return call(
        bias_kernel,
        "bias_table",
        (heads,),
        [slab(count, 1, 2 * block)],
        [slab(count, block, block)],
        [jax.ShapeDtypeStruct((heads, count, block, block), F32)],
        [windows],
        after=after,
    )[0]


def project_kernel(counts, limit, info_ref, x_ref, gain_ref, *refs):
    matrices, (normed_ref, out_ref, kv_ref) = split_refs(refs, counts)
    first = kv_ref.shape[0] // 2
    values = x_ref[...].astype(F32)
    factor = lax.rsqrt(jnp.mean(values * values, axis=0, keepdims=True) + EPSILON)
    normed = (values * factor * gain_ref[...]).astype(BF16)
    normed_ref[...] = normed
    for r, parts in enumerate(matrices):
        place = info_ref[0] ^ r

        @pl.when(place < limit)
        def _(parts=parts, place=place):
            weights = joined([ref[0] for ref in parts], 0)
            product = dot_tn(weights, normed).astype(BF16)
            out_ref[place] = product

            @pl.when(place >= first)
            def _():
                kv_ref[place - first] = product


def project(place, x, gain, matrices, after):
    wide, length = x.shape
    part = matrices[0][0].shape[2]
    limit = len(matrices) * 3 // 4
    step = lane_step(length)
    counts = [len(parts) for parts in matrices]
    flat = [ref for parts in matrices for ref in parts]
    return call(
        functools.partial(project_kernel, counts, limit),
        "project",
        (length // step,),
        [columns(wide, step), whole((wide, 1))] + [whole(ref.shape) for ref in flat],
        [
            columns(wide, step),
            pl.BlockSpec((len(matrices), part, step), lambda j, *_: (0, 0, j)),
            pl.BlockSpec((len(matrices) // 2, part, step), lambda j, *_: (0, 0, j)),
        ],
        [
            jax.ShapeDtypeStruct((wide, length), BF16),
            jax.ShapeDtypeStruct((len(matrices), part, length), BF16),
            jax.ShapeDtypeStruct((len(matrices) // 2, part, length), BF16),
        ],
        [place, x, gain, *flat],
        flops=2 * wide * length * limit * part,
        scalars=1,
        after=after,
    )


def assemble_kernel(counts, info_ref, *refs):
    matrices, (out_ref,) = split_refs(refs, counts)
    for r, parts in enumerate(matrices):
        place, row = info_ref[0] ^ r, 0
        for ref in parts:
            rows = ref.shape[1]
            out_ref[place, row : row + rows] = ref[0]
            row += rows


def assemble(place, matrices, inner, after):
    part = matrices[0][0].shape[2]
    counts = [len(parts) for parts in matrices]
    flat = [ref for parts in matrices for ref in parts]
    wide = sum(ref.shape[1] for ref in matrices[0])
    shape = (len(matrices), wide, part)
    ordered = call(
        functools.partial(assemble_kernel, counts),
        "assemble",
        (1,),
        [whole(ref.shape) for ref in flat],
        [pl.BlockSpec(shape, lambda *_: (0, 0, 0))],
        [jax.ShapeDtypeStruct(shape, BF16)],
        [place, *flat],
        scalars=1,
        after=after,
    )[0]
    return jnp.transpose(ordered.reshape(4, inner // part, wide, part), (0, 2, 1, 3)).reshape(
        4, wide, inner
    )


def middle_kernel(x_ref, context_ref, w_ref, gain_ref, normed_ref):
    values = x_ref[...].astype(F32) + dot_nn(w_ref[0], context_ref[...])
    factor = lax.rsqrt(jnp.mean(values * values, axis=0, keepdims=True) + EPSILON)
    normed_ref[...] = (values * factor * gain_ref[...]).astype(BF16)


def out_weights(weights):
    return pl.BlockSpec(
        (1,) + weights.shape[1:], lambda *_: (3, 0, 0), pipeline_mode=pl.Buffered(1)
    )


def middle_layer(x, context, weights, gain, after):
    wide, length = x.shape
    inner = weights.shape[2]
    step = lane_step(length)
    return call(
        middle_kernel,
        "middle",
        (length // step,),
        [columns(wide, step), columns(inner, step), out_weights(weights), whole((wide, 1))],
        [columns(wide, step)],
        [jax.ShapeDtypeStruct((wide, length), BF16)],
        [x, context, weights, gain],
        flops=2 * wide * length * inner,
        after=after,
    )[0]


def lifted_grads(values, gain, grad):
    factor = lax.rsqrt(jnp.mean(values * values, axis=0, keepdims=True) + EPSILON)
    scaled = values * factor
    lifted = grad * gain
    inner = jnp.mean(lifted * scaled, axis=0, keepdims=True)
    return factor * (lifted - scaled * inner), jnp.sum(grad * scaled, axis=1, keepdims=True)


def add_up(ref, value):
    first = pl.program_id(0) == 0

    @pl.when(first)
    def _():
        ref[...] = value

    @pl.when(jnp.logical_not(first))
    def _():
        ref[...] += value


def turn_kernel(
    x_ref, context_ref, cot_ref, back0_ref, back1_ref, gain_ref, w_ref, low_ref, grad_ref, gain_grad_ref
):
    middle = x_ref[...].astype(F32) + dot_nn(w_ref[0], context_ref[...])
    grad = back0_ref[0].astype(F32) + back1_ref[0].astype(F32)
    normed_grad, gain_grad = lifted_grads(middle, gain_ref[...], grad)
    add_up(gain_grad_ref, gain_grad)
    low = (cot_ref[...].astype(F32) + normed_grad).astype(BF16)
    low_ref[...] = low
    grad_ref[...] = dot_tn(w_ref[0], low).astype(BF16)


def turn(group, x, context, cot, back, gain, weights, after):
    wide, length = x.shape
    inner = weights.shape[2]
    step = lane_step(length)
    big = columns(wide, step)
    part = pl.BlockSpec((1, wide, step), lambda j, *_: (group, 0, j))
    return call(
        turn_kernel,
        "turn",
        (length // step,),
        [big, columns(inner, step), big, part, part, whole((wide, 1)), out_weights(weights)],
        [big, columns(inner, step), pl.BlockSpec((wide, 1), lambda *_: (0, 0))],
        [
            jax.ShapeDtypeStruct((wide, length), BF16),
            jax.ShapeDtypeStruct((inner, length), BF16),
            jax.ShapeDtypeStruct((wide, 1), F32),
        ],
        [x, context, cot, *back, gain, weights],
        flops=4 * wide * length * inner,
        after=after,
    )


def put_blocks(info_ref, out_ref, values):
    if len(out_ref.shape) == 3:
        out_ref[0] = values.astype(out_ref.dtype)
        return
    blocks, rows = out_ref.shape[1:3]
    for p in range(blocks):
        chip = block_of(info_ref[0], p, blocks // 2)
        out_ref[0, chip] = values[p * rows : (p + 1) * rows].astype(out_ref.dtype)


def outward_spec(groups, wide, length, blocks, step):
    rows, steps = wide // blocks, length // step
    if rows % 8:
        spec = pl.BlockSpec((1, wide, step), lambda j, *_: (j // steps, 0, j % steps))
        return spec, jax.ShapeDtypeStruct((groups, wide, length), BF16)
    return (
        pl.BlockSpec((1, blocks, rows, step), lambda j, *_: (j // steps, 0, 0, j % steps)),
        jax.ShapeDtypeStruct((groups, blocks, rows, length), BF16),
    )


def outward(array, place, blocks):
    if array.ndim == 4:
        return array.reshape(array.shape[0], -1, array.shape[3])
    return jnp.stack([reorder(array, m, place, blocks, True) for m in range(array.shape[0])])


def group_columns(group, steps, *shape):
    def index(j, *_):
        return (0,) * (len(shape) - 1) + (jnp.clip(j - group * steps, 0, steps - 1),)

    return pl.BlockSpec(shape, index)


def in_groups(kernel, counts, steps, *refs):
    lead, each, groups = counts
    group = pl.program_id(0) // steps
    shared, rest = refs[:lead], refs[lead:]
    parts, tail = rest[: each * groups], rest[each * groups :]
    for m in range(groups):

        @pl.when(group == m)
        def _(m=m):
            kernel(*shared, *parts[each * m : each * (m + 1)], *tail)


def finish_kernel(info_ref, x_ref, context_ref, ffn0_ref, ffn1_ref, w_ref, out_ref):
    middle = x_ref[...].astype(F32) + dot_nn(w_ref[0], context_ref[...])
    total = middle + (ffn0_ref[0].astype(F32) + ffn1_ref[0].astype(F32))
    put_blocks(info_ref, out_ref, total)


def finish(place, terms, ffn, weights, blocks, after):
    wide, length = terms[0][0].shape
    inner = weights.shape[2]
    step = lane_step(length)
    groups, steps = len(terms), length // step
    spec, shape = outward_spec(groups, wide, length, blocks, step)
    specs = []
    for m in range(groups):
        specs += [group_columns(m, steps, wide, step), group_columns(m, steps, inner, step)]
    part = pl.BlockSpec((1, wide, step), lambda j, *_: (j // steps, 0, j % steps))
    result = call(
        functools.partial(in_groups, finish_kernel, (1, 2, groups), steps),
        "finish",
        (groups * steps,),
        specs + [part, part, out_weights(weights)],
        [spec],
        [shape],
        [place, *[array for term in terms for array in term], *ffn, weights],
        flops=2 * groups * wide * length * inner,
        scalars=1,
        after=after,
    )[0]
    return outward(result, place, blocks)


def outer_kernel(count, info_ref, *refs):
    out_ref = refs[-1]
    step = pl.program_id(0)
    for r in range(len(refs) // (2 * count)):
        pairs = refs[2 * count * r : 2 * count * (r + 1)]

        @pl.when(step == r)
        def _(pairs=pairs):
            total = dot_nt(pairs[0][...], matrix_of(pairs[1]))
            for m in range(1, count):
                total = total + dot_nt(pairs[2 * m][...], matrix_of(pairs[2 * m + 1]))
            out_ref[0] = total.astype(BF16)


def matrix_of(ref):
    return ref[0] if len(ref.shape) == 3 else ref[...]


def outer_products(place, roles, matrices, into, after):
    count = len(matrices[0])
    wide, length = matrices[0][0][0].shape
    low, high = roles
    operands, specs = [], []
    for left, right in [pair for pairs in matrices for pair in pairs]:
        right, number = right if isinstance(right, tuple) else (right, None)
        inner = right.shape[-2]
        operands += [left, right]
        specs.append(whole(left.shape))
        if number is None:
            specs.append(whole(right.shape))
        else:
            specs.append(
                pl.BlockSpec(
                    (1, inner, length),
                    lambda *_, n=number: (n, 0, 0),
                    pipeline_mode=pl.Buffered(1),
                )
            )

    def index(step, info):
        return (jnp.where(step == 0, low, high) ^ info[0], 0, 0)

    if into is not None:
        operands.append(into)
        specs.append(pl.BlockSpec(memory_space=pl.ANY))

    def kernel(info_ref, *refs):
        if into is not None:
            refs = refs[:-2] + refs[-1:]
        outer_kernel(count, info_ref, *refs)

    return call(
        kernel,
        "outer_products",
        (len(matrices),),
        specs,
        [pl.BlockSpec((1, wide, inner), index)],
        [jax.ShapeDtypeStruct((4, wide, inner), BF16)],
        [place, *operands],
        flops=2 * wide * inner * length * count * len(matrices),
        scalars=1,
        after=after,
        aliases=None if into is None else {len(operands): 0},
    )[0]


def input_kernel(info_ref, x_ref, low_ref, dq_ref, dkv_ref, gain_ref, w_ref, out_ref, gain_grad_ref):
    grad = (
        dot_nn(w_ref[0], dq_ref[...]) + dot_nn(w_ref[1], dkv_ref[0]) + dot_nn(w_ref[2], dkv_ref[1])
    )
    normed_grad, gain_grad = lifted_grads(x_ref[...].astype(F32), gain_ref[...], grad)
    add_up(gain_grad_ref, gain_grad)
    put_blocks(info_ref, out_ref, low_ref[...].astype(F32) + normed_grad)


def input_grads(place, terms, gain, weights, blocks, after):
    wide, length = terms[0][0].shape
    inner = weights.shape[2]
    step = lane_step(length)
    groups, steps = len(terms), length // step
    spec, shape = outward_spec(groups, wide, length, blocks, step)
    specs = []
    for m in range(groups):
        big = group_columns(m, steps, wide, step)
        specs += [big, big, group_columns(m, steps, inner, step), group_columns(m, steps, 2, inner, step)]
    result, gain_grads = call(
        functools.partial(in_groups, input_kernel, (1, 4, groups), steps),
        "input_grads",
        (groups * steps,),
        specs
        + [
            whole((wide, 1)),
            pl.BlockSpec((3,) + weights.shape[1:], lambda *_: (0, 0, 0), pipeline_mode=pl.Buffered(1)),
        ],
        [spec, pl.BlockSpec((wide, 1), lambda *_: (0, 0))],
        [shape, jax.ShapeDtypeStruct((wide, 1), F32)],
        [place, *[array for term in terms for array in term], gain, weights],
        flops=6 * groups * wide * length * inner,
        scalars=1,
        after=after,
    )
    return outward(result, place, blocks), gain_grads


def rows_kernel(in_ref, out_ref):
    out_ref[...] = in_ref[...]


def rows_of(array, start, rows):
    kinds, _, width = array.shape
    if rows % 16:
        return array[:, start : start + rows]
    return call(
        rows_kernel,
        "rows",
        (kinds,),
        [pl.BlockSpec((1, rows, width), lambda k: (k, start // rows, 0))],
        [pl.BlockSpec((1, rows, width), lambda k: (k, 0, 0))],
        [jax.ShapeDtypeStruct((kinds, rows, width), array.dtype)],
        [array],
    )[0]


def merge_kernel(first_ref, second_ref, out_ref):
    parts = [first_ref[0].astype(F32), second_ref[0].astype(F32)]
    out_ref[0] = jnp.concatenate(parts, axis=0).astype(out_ref.dtype)


def merge(first, second):
    kinds, rows, width = first.shape
    if rows % 8:
        return jnp.concatenate([first, second], axis=1)
    return call(
        merge_kernel,
        "merge",
        (kinds,),
        [slab(rows, width), slab(rows, width)],
        [slab(2 * rows, width)],
        [jax.ShapeDtypeStruct((kinds, 2 * rows, width), first.dtype)],
        [first, second],
    )[0]


def sum_kernel(count, *refs):
    total = refs[0][0].astype(F32)
    for ref in refs[1:count]:
        total = total + ref[0].astype(F32)
    row = 0
    for ref in refs[count:]:
        rows = ref.shape[1]
        ref[0] = total[row : row + rows].astype(BF16)
        row += rows


def sum_rows(terms, parts, starts=None, kinds=None, after=()):
    starts = starts or [0] * len(terms)
    kinds = kinds or terms[0].shape[0]
    rows, width = terms[0].shape[1:]
    sizes = [rows // parts] * parts if isinstance(parts, int) else list(parts)
    if sizes[0] % 8:
        total = add_low(*[term[a : a + kinds] for term, a in zip(terms, starts)])
        results, row = [], 0
        for size in sizes:
            results.append(total[:, row : row + size])
            row += size
    else:
        results = call(
            functools.partial(sum_kernel, len(terms)),
            "sum_rows",
            (kinds,),
            [pl.BlockSpec((1, rows, width), lambda k, a=a: (a + k, 0, 0)) for a in starts],
            [slab(size, width) for size in sizes],
            [jax.ShapeDtypeStruct((kinds, size, width), BF16) for size in sizes],
            terms,
            after=after,
        )
    return results[0] if len(sizes) == 1 else tuple(results)


def corner_kernel(y_ref, first_ref, x_ref, second_ref, y_out, x_out):
    y_out[...] = (y_ref[...].astype(F32) + first_ref[...].astype(F32)).astype(BF16)
    x_out[...] = (x_ref[...].astype(F32) + second_ref[...].astype(F32)).astype(BF16)


def add_corner(to_y, first, to_x, second):
    kinds, half, width = first.shape
    upper = pl.BlockSpec((1, half, width), lambda k: (k, 0, 0))
    lower = pl.BlockSpec((1, half, width), lambda k: (k, 1, 0))
    return call(
        corner_kernel,
        "add_corner",
        (kinds,),
        [upper, upper, lower, upper],
        [upper, lower],
        [jax.ShapeDtypeStruct(to_y.shape, BF16), jax.ShapeDtypeStruct(to_x.shape, BF16)],
        [to_y, first, to_x, second],
        aliases={0: 0, 2: 1},
    )


def halves(value_t, half):
    zero = jnp.zeros((half, value_t.shape[1]), value_t.dtype)
    return (
        jnp.concatenate([value_t[:half], zero], axis=0),
        jnp.concatenate([zero, value_t[half:]], axis=0),
    )


def attend_kernel(sources, block, half, info_ref, q_ref, *refs):
    kv_refs = refs[: 2 * sources]
    segq_ref, segk_ref, table_ref, ctx_ref, lse_ref = refs[2 * sources : 2 * sources + 5]
    s_scr, m_scr, l_scr, acc_scr, k_scr = refs[2 * sources + 5 :]
    length = q_ref.shape[1]
    q_blocks = length // block
    k_blocks = q_blocks * sources
    place_x = info_ref[0]
    for s in range(sources):
        k_scr[s * length : (s + 1) * length, :] = transposed(kv_refs[2 * s][...])
    for qb in range(q_blocks):
        rows = pl.ds(qb * block, block)
        q_heads = halves(q_ref[:, rows], half)
        seg_q = segq_ref[:, rows]
        m_scr[...] = jnp.full(m_scr.shape, NEGATIVE, F32)
        l_scr[...] = jnp.zeros(l_scr.shape, F32)
        acc_scr[...] = jnp.zeros(acc_scr.shape, F32)
        for kb in range(k_blocks):
            s, lb = divmod(kb, q_blocks)
            live = info_ref[1 + qb * k_blocks + kb]

            @pl.when(live != 0)
            def _(s=s, lb=lb, kb=kb):
                entry = k_blocks - 1 - ((place_x ^ s) * q_blocks + lb - place_x * q_blocks - qb)
                keys = k_scr[pl.ds(kb * block, block), :]
                kept = segk_ref[pl.ds(kb * block, block), :] == seg_q
                for h in range(2):
                    score = dot_nn(keys, q_heads[h]) + table_ref[h, entry]
                    score = jnp.where(kept, score, NEGATIVE)
                    s_scr[h, kb] = score
                    m_scr[h] = jnp.maximum(m_scr[h], jnp.max(score, axis=0, keepdims=True))

        for kb in range(k_blocks):
            s, lb = divmod(kb, q_blocks)
            live = info_ref[1 + qb * k_blocks + kb]

            @pl.when(live != 0)
            def _(s=s, lb=lb, kb=kb):
                for h in range(2):
                    prob = jnp.exp(s_scr[h, kb] - m_scr[h])
                    l_scr[h] += jnp.sum(prob, axis=0, keepdims=True)
                    values_t = kv_refs[2 * s + 1][
                        h * half : (h + 1) * half, lb * block : (lb + 1) * block
                    ]
                    acc_scr[h * half : (h + 1) * half] += dot_nn(values_t, prob.astype(BF16))

        for h in range(2):
            lse_ref[0, h : h + 1, rows] = m_scr[h] + jnp.log(l_scr[h])
            ctx_ref[h * half : (h + 1) * half, rows] = (
                acc_scr[h * half : (h + 1) * half] / l_scr[h]
            ).astype(BF16)


def grad_kernel(sources, block, half, info_ref, q_ref, *refs):
    kv_refs = refs[: 2 * sources]
    refs = refs[2 * sources :]
    segq_ref, segk_ref, table_ref, ctx_ref, lse_ref, gctx_ref = refs[:6]
    dq_ref, gbias_ref = refs[6:8]
    dkv_refs = refs[8 : 8 + sources]
    dk_scr, dv_scr, dq_scr, k_scr, v_scr, db_scr = refs[8 + sources :]
    length = q_ref.shape[1]
    q_blocks = length // block
    k_blocks = q_blocks * sources
    place_x = info_ref[0]
    lane = lax.broadcasted_iota(jnp.int32, (block, 2 * half), 1)

    db_scr[...] = jnp.zeros(db_scr.shape, F32)
    for s in range(sources):
        k_scr[s * length : (s + 1) * length, :] = transposed(kv_refs[2 * s][...])
        v_scr[s * length : (s + 1) * length, :] = transposed(kv_refs[2 * s + 1][...])
    dk_scr[...] = jnp.zeros(dk_scr.shape, F32)
    dv_scr[...] = jnp.zeros(dv_scr.shape, F32)
    for qb in range(q_blocks):
        rows = pl.ds(qb * block, block)
        query_t = q_ref[:, rows]
        grad_out_t = gctx_ref[:, rows]
        product = grad_out_t.astype(F32) * ctx_ref[:, rows].astype(F32)
        deltas = (
            jnp.sum(product[:half], axis=0, keepdims=True),
            jnp.sum(product[half:], axis=0, keepdims=True),
        )
        q_heads = halves(query_t, half)
        g_heads = halves(grad_out_t, half)
        query, grad_out = transposed(query_t), transposed(grad_out_t)
        zero = jnp.zeros(query.shape, BF16)
        q_lanes = (jnp.where(lane < half, query, zero), jnp.where(lane < half, zero, query))
        g_lanes = (
            jnp.where(lane < half, grad_out, zero),
            jnp.where(lane < half, zero, grad_out),
        )
        seg_q = segq_ref[:, rows]
        dq_scr[...] = jnp.zeros(dq_scr.shape, F32)
        for kb in range(k_blocks):
            s, lb = divmod(kb, q_blocks)
            live = info_ref[1 + qb * k_blocks + kb]

            @pl.when(live != 0)
            def _(s=s, lb=lb, kb=kb):
                entry = k_blocks - 1 - ((place_x ^ s) * q_blocks + lb - place_x * q_blocks - qb)
                key_rows = pl.ds(kb * block, block)
                keys = k_scr[key_rows, :]
                values = v_scr[key_rows, :]
                kept = segk_ref[key_rows, :] == seg_q
                key_grad = dk_scr[key_rows, :]
                value_grad = dv_scr[key_rows, :]
                for h in range(2):
                    score = dot_nn(keys, q_heads[h]) + table_ref[h, entry]
                    score = jnp.where(kept, score, NEGATIVE)
                    prob = jnp.exp(score - lse_ref[0, h : h + 1, rows])
                    grad_prob = dot_nn(values, g_heads[h])
                    grad_score = prob * (grad_prob - deltas[h])
                    db_scr[h, s, q_blocks - 1 - lb + qb] += grad_score
                    low = grad_score.astype(BF16)
                    key_grad = key_grad + dot_nn(low, q_lanes[h])
                    value_grad = value_grad + dot_nn(prob.astype(BF16), g_lanes[h])
                    keys_t = kv_refs[2 * s][
                        h * half : (h + 1) * half, lb * block : (lb + 1) * block
                    ]
                    dq_scr[h * half : (h + 1) * half] += dot_nn(keys_t, low)
                dk_scr[key_rows, :] = key_grad
                dv_scr[key_rows, :] = value_grad

        dq_ref[:, rows] = dq_scr[...].astype(BF16)
    for s in range(sources):
        rows = slice(s * length, (s + 1) * length)
        dkv_refs[s][0] = jnp.transpose(dk_scr[rows, :], (1, 0)).astype(BF16)
        dkv_refs[s][1] = jnp.transpose(dv_scr[rows, :], (1, 0)).astype(BF16)

    for h in range(2):
        for s in range(sources):
            for n in range(2 * q_blocks - 1):
                gbias_ref[h, s, n] = diagonal_sums(db_scr[h, s, n])


def diagonal_sums(tile):
    block = tile.shape[0]
    count = block
    if block == 2 * LANES:
        zero = jnp.zeros((LANES, LANES), F32)
        tile = jnp.concatenate(
            [
                tile[LANES:, :LANES],
                tile[LANES:, LANES:] + tile[:LANES, :LANES],
                tile[:LANES, LANES:],
                zero,
            ],
            axis=1,
        )
        count = LANES
    else:
        tile = jnp.concatenate([tile, jnp.zeros_like(tile)], axis=1)
    while count > 8:
        count //= 2
        tile = pltpu.roll(tile[:count], count, 1) + tile[count:]
    return tile


def attention_specs(sources, length, block, pairs, width):
    k_blocks = length * sources // block
    entries = 2 * k_blocks - 1

    def rows(offset):
        return pl.BlockSpec((width, length), lambda p, info: (p + offset, 0))

    kv_specs = [rows(pairs), rows(2 * pairs)] + [rows(0), rows(pairs)] * (sources - 1)
    seg_specs = [whole((1, length)), whole((length * sources, 1))]
    table_spec = pl.BlockSpec((2, entries, block, block), lambda p, info: (p, 0, 0, 0))
    lse_spec = pl.BlockSpec((1, 8, length), lambda p, info: (p, 0, 0))
    return k_blocks, entries, rows, kv_specs, seg_specs, table_spec, lse_spec


def attend(info, qkv, others, seg_q, seg_k, table, block, head_size, inner, after):
    length = qkv.shape[1]
    sources = 1 + len(others)
    width = 2 * head_size
    pairs = inner // width
    k_blocks, entries, rows, kv_specs, seg_specs, table_spec, lse_spec = attention_specs(
        sources, length, block, pairs, width
    )
    kvs = [qkv, qkv] + [kv for kv in others for _ in range(2)]
    return call(
        functools.partial(attend_kernel, sources, block, head_size),
        "attend",
        (pairs,),
        [rows(0)] + kv_specs + seg_specs + [table_spec],
        [rows(0), lse_spec],
        [
            jax.ShapeDtypeStruct((inner, length), BF16),
            jax.ShapeDtypeStruct((pairs, 8, length), F32),
        ],
        [info, qkv, *kvs, seg_q, seg_k, table],
        flops=16 * inner * length * length * sources,
        scratch=[
            pltpu.VMEM((2, k_blocks, block, block), F32),
            pltpu.VMEM((2, 1, block), F32),
            pltpu.VMEM((2, 1, block), F32),
            pltpu.VMEM((width, block), F32),
            pltpu.VMEM((length * sources, width), BF16),
        ],
        scalars=1,
        after=after,
    )


def attend_grads(
    info, qkv, others, seg_q, seg_k, table, context, lse, grad_context, block, head_size, after
):
    inner, length = context.shape
    sources = 1 + len(others)
    width = 2 * head_size
    pairs = inner // width
    k_blocks, entries, rows, kv_specs, seg_specs, table_spec, lse_spec = attention_specs(
        sources, length, block, pairs, width
    )
    dkv_spec = pl.BlockSpec((2, width, length), lambda p, info: (0, p, 0))
    tiles = (sources, 2 * (length // block) - 1)
    kvs = [qkv, qkv] + [kv for kv in others for _ in range(2)]
    results = call(
        functools.partial(grad_kernel, sources, block, head_size),
        "attend_grads",
        (pairs,),
        [rows(0)] + kv_specs + seg_specs + [table_spec, rows(0), lse_spec, rows(0)],
        [rows(0), pl.BlockSpec((2,) + tiles + (8, 2 * block), lambda p, info: (p, 0, 0, 0, 0))]
        + [dkv_spec] * sources,
        [
            jax.ShapeDtypeStruct((inner, length), BF16),
            jax.ShapeDtypeStruct((2 * pairs,) + tiles + (8, 2 * block), F32),
        ]
        + [jax.ShapeDtypeStruct((2, inner, length), BF16)] * sources,
        [info, qkv, *kvs, seg_q, seg_k, table, context, lse, grad_context],
        flops=32 * inner * length * length * sources,
        scratch=[
            pltpu.VMEM((length * sources, width), F32),
            pltpu.VMEM((length * sources, width), F32),
            pltpu.VMEM((width, block), F32),
            pltpu.VMEM((length * sources, width), BF16),
            pltpu.VMEM((length * sources, width), BF16),
            pltpu.VMEM((2,) + tiles + (block, block), F32),
        ],
        scalars=1,
        after=after,
    )
    return results[0], results[1], results[2:]


def gelu_terms(gate, upward, grad_hidden):
    square = gate * gate
    tanh = jnp.tanh(GELU_SCALE * gate * (1.0 + GELU_CUBE * square))
    half = 0.5 + 0.5 * tanh
    gelu = gate * half
    slope = half + 0.5 * gate * (1.0 - tanh * tanh) * (
        GELU_SCALE + 3.0 * GELU_CUBE * GELU_SCALE * square
    )
    return (
        (gelu * upward).astype(BF16),
        (grad_hidden * upward * slope).astype(BF16),
        (grad_hidden * gelu).astype(BF16),
    )


def joined(parts, axis):
    return parts[0] if len(parts) == 1 else jnp.concatenate(parts, axis=axis)


def source_rows(refs, kind, columns):
    return joined([ref[kind][:, columns] for ref in refs], 0)


def batches_of(sources, tile):
    if tile % LANES:
        return [[s] for s in range(sources)]
    return [list(range(s, min(s + 2, sources))) for s in range(0, sources, 2)]


def split_refs(refs, counts):
    result, start = [], 0
    for count in counts:
        result.append(refs[start : start + count])
        start += count
    return result, refs[start:]


def ffn_kernel(counts, groups, gathered, info_ref, *refs):
    if gathered:
        stacks, refs = refs[:3], refs[3:]
        blocks = stacks[0].shape[0] // len(counts)
        tile = stacks[0].shape[2]
    else:
        sources, refs = refs[: len(counts)], refs[len(counts) :]
        tile = sources[0].shape[2]
    acts_hbm, refs = refs[: 2 * groups], refs[2 * groups :]
    (hid_ref, ggi_ref, gui_ref, w_ref), refs = refs[:4], refs[4:]
    grads, (acts, sems) = split_refs(refs, counts)
    first = pl.program_id(0) == 0

    def fetch(n):
        return pltpu.make_async_copy(acts_hbm[n], acts.at[n], sems.at[n])

    def matrix(kind, source):
        if not gathered:
            return sources[source][kind]
        places = [
            (info_ref[1] ^ source) * blocks + block_of(info_ref[0], p, blocks // 2)
            for p in range(blocks)
        ]
        rows = [stacks[kind][place].astype(F32) for place in places]
        return jnp.concatenate(rows, axis=0).astype(BF16)

    @pl.when(first)
    def _():
        for g in range(groups):
            fetch(g).start()
            fetch(groups + g).start()

    start = 0
    for number, batch in enumerate(batches_of(len(counts), tile)):
        units = tile * len(batch)
        rows = slice(start, start + units)
        start += units
        for kind in range(3):
            w_ref[kind, :, rows] = joined([matrix(kind, s) for s in batch], 1)
        for g in range(groups):
            if number == 0:

                @pl.when(first)
                def _(g=g):
                    fetch(g).wait()
                    fetch(groups + g).wait()

            gate = dot_tn(w_ref[0, :, rows], acts[g])
            upward = dot_tn(w_ref[1, :, rows], acts[g])
            grad_hidden = dot_tn(w_ref[2, :, rows], acts[groups + g])
            hidden, grad_gate, grad_up = gelu_terms(gate, upward, grad_hidden)
            hid_ref[g, rows] = hidden
            ggi_ref[g, rows] = grad_gate
            gui_ref[g, rows] = grad_up
        for kind, (left, right_ref) in enumerate(((0, ggi_ref), (0, gui_ref), (groups, hid_ref))):
            total = None
            for g in range(groups):
                product = dot_nt(acts[left + g], right_ref[g, rows])
                total = product if total is None else total + product
            total = total.astype(BF16)
            for n, s in enumerate(batch):
                row = 0
                for ref in grads[s]:
                    depth = ref.shape[1]
                    ref[kind] = total[row : row + depth, n * tile : (n + 1) * tile]
                    row += depth


def tile_of(width):
    return LANES if width % LANES == 0 else width


def ffn_chunk(info, weights, width, normed, cot, after):
    groups = len(normed)
    wide, length = normed[0].shape
    gathered = not isinstance(weights, list)
    sources = lax.axis_size("mp")
    tile = tile_of(width)
    steps = width // tile
    half = wide // 2
    counts = [2] + [3] * (sources - 1)
    shapes = [(3, half, width)] * 2
    for _ in range(sources - 1):
        shapes += [(3, half, width)] + [(3, half // 2, width)] * 2
    if gathered:
        weight_specs = [
            pl.BlockSpec(weights.shape[:2] + (tile,), lambda j, *_, n=n: (0, 0, n * steps + j))
            for n in range(3)
        ]
        operands = [weights] * 3
    else:
        weight_specs = [pl.BlockSpec((3, wide, tile), lambda j, *_: (0, 0, j))] * sources
        operands = list(weights)
    units = sources * tile
    act_spec = pl.BlockSpec((groups, units, length), lambda j, *_: (0, j, 0))
    act_shape = jax.ShapeDtypeStruct((groups, sources * width, length), BF16)
    results = call(
        functools.partial(ffn_kernel, counts, groups, gathered),
        "ffn_chunk",
        (steps,),
        weight_specs + [pl.BlockSpec(memory_space=pl.ANY)] * (2 * groups),
        [act_spec] * 3
        + [pl.BlockSpec((3, wide, units), lambda j, *_: (0, 0, j))]
        + [pl.BlockSpec(shape[:2] + (tile,), lambda j, *_: (0, 0, j)) for shape in shapes],
        [act_shape] * 3
        + [jax.ShapeDtypeStruct((3, wide, sources * width), BF16)]
        + [jax.ShapeDtypeStruct(shape, BF16) for shape in shapes],
        [info, *operands, *normed, *cot],
        flops=12 * groups * length * wide * sources * width,
        scratch=[
            pltpu.VMEM((2 * groups, wide, length), BF16),
            pltpu.SemaphoreType.DMA((2 * groups,)),
        ],
        scalars=1,
        after=after,
    )
    grads, _ = split_refs(results[4:], counts)
    return results[:3], results[3], grads


def down_kernel(chunks, kinds, *refs):
    total = None
    for _ in range(chunks):
        matrices, acts, refs = refs[:kinds], refs[kinds : 2 * kinds], refs[2 * kinds :]
        for matrix, act in zip(matrices, acts):
            product = dot_nn(matrix[0], act[0])
            total = product if total is None else total + product
    (out_ref,) = refs
    out_ref[0] = total.astype(BF16)


def down(chunk_weights, chunk_acts, first, kinds, start, count, after):
    length = chunk_acts[0][0].shape[2]
    wide = chunk_weights[0].shape[1]
    operands, specs = [], []
    flops = 0
    for weights, acts in zip(chunk_weights, chunk_acts):
        acts = acts[1:] if kinds == 2 else acts[:1]
        operands += [weights] * kinds + list(acts)
        specs += [
            pl.BlockSpec(
                (1,) + weights.shape[1:], lambda g, n=n: (n, 0, 0), pipeline_mode=pl.Buffered(1)
            )
            for n in range(first, first + kinds)
        ]
        specs += [
            pl.BlockSpec((1, act.shape[1], length), lambda g: (start + g, 0, 0)) for act in acts
        ]
        flops += 2 * kinds * count * length * wide * acts[0].shape[1]
    return call(
        functools.partial(down_kernel, len(chunk_acts), kinds),
        "down",
        (count,),
        specs,
        [slab(wide, length)],
        [jax.ShapeDtypeStruct((count, wide, length), BF16)],
        operands,
        flops=flops,
        after=after,
    )[0]


def body(
    inputs,
    cotangent,
    segments,
    rel_bucket,
    head_order,
    rel_table,
    norm1_gain,
    norm2_gain,
    w_query,
    w_key,
    w_value,
    output_weight,
    w_gate,
    w_up,
    w_down,
):
    dp, mp = dp_size(), lax.axis_size("mp")
    x = lax.axis_index("mp")
    core, chip = lax.axis_index("core"), lax.axis_index("chip")
    chips, depth = dp // 2, dp // 4
    micro, rows, own_length, model = inputs.shape
    groups = micro * rows
    length = own_length * mp
    bucket_count, head_count = rel_table.shape
    inner = w_query.shape[1]
    head_size = inner // head_count
    block = min(256, own_length)
    q_blocks, k_blocks = own_length // block, length // block
    own_rows, own_units = w_gate.shape
    half_units = own_units // 2
    chip_rows = 2 * own_rows
    place = chip.reshape(1).astype(jnp.int32)

    micros = range(groups)
    own_place = (2 * x + core).reshape(1).astype(jnp.int32)
    role_place = own_place & 3

    def feature_major(array):
        return jnp.transpose(array.reshape(groups, own_length, model), (0, 2, 1))

    bucket_rev = jnp.concatenate([rel_bucket[::-1], jnp.full((1,), -1, jnp.int32)])
    bucket_hot = (bucket_rev[:, None] == jnp.arange(bucket_count, dtype=jnp.int32)[None, :]).astype(F32)
    head_hot = (head_order[:, None] == jnp.arange(head_count, dtype=jnp.int32)[None, :]).astype(F32)
    offset_table = jnp.dot(bucket_hot, rel_table, precision=TOP_PRECISION)
    offset_bias = jnp.dot(head_hot, offset_table.T, precision=TOP_PRECISION)
    bias_blocks = offset_bias.reshape(head_count, 2 * k_blocks, block)
    windows = jnp.concatenate([bias_blocks[:, :-1], bias_blocks[:, 1:]], axis=2)

    part = 4 * inner // (2 * mp)
    shard = jnp.concatenate([w_query, w_key, w_value, jnp.transpose(output_weight)], axis=1)
    kept = lax.dynamic_slice_in_dim(shard, (2 * x + core) * part, part, 1)
    sent = lax.dynamic_slice_in_dim(shard, (2 * x + 1 - core) * part, part, 1)
    got = swap_dp(sent, 1)
    attention_piece = either(
        core, jnp.concatenate([kept, got], axis=0), jnp.concatenate([got, kept], axis=0)
    )[None]
    ffn_shard = jnp.stack([w_gate, w_up, jnp.transpose(w_down)])
    low_half, high_half = ffn_shard[:, :, :half_units], ffn_shard[:, :, half_units:]
    kept = either(core, low_half, high_half)
    got = swap_dp(either(core, high_half, low_half), 1)
    ffn_piece = either(
        core, jnp.concatenate([kept, got], axis=1), jnp.concatenate([got, kept], axis=1)
    )
    if half_units % (7 * LANES) == 0:
        bounds = [0, half_units // 7 * 4, half_units]
    elif half_units > LANES:
        bounds = [0, LANES, half_units]
    else:
        bounds = [0, half_units]
    widths = [b - a for a, b in zip(bounds[:-1], bounds[1:])]
    chunk_stacks = []
    for a, width in zip(bounds, widths):
        flat = jnp.concatenate([ffn_piece[n, :, a : a + width] for n in range(3)], axis=1)
        chunk_stacks.append(lax.all_gather(flat, ("mp", "chip")))

    far_masks = z_masks()

    def gather_z(piece, masks, first=(), then=()):
        for mask in masks:
            piece = merge(piece, hold(swap_dp(hold(piece, *first), mask), *then))
        return piece

    own = gather_z(attention_piece, far_masks)
    arrays = feature_major(inputs)
    layer_in = [reorder(arrays, m, place, chips, False) for m in micros]
    arrays = feature_major(cotangent)
    cots = [reorder(arrays, m, place, chips, False, [*layer_in, own]) for m in micros]
    cots_far = [swap_dp(cot, 1) for cot in cots]
    table = bias_table(windows[:, :, None, :], block, cots)
    over_y, over_x = gather_xy(own, layer_in, [table])
    corner = gather_corner(over_y, over_x)
    quads = quads_of(own, over_y, over_x, corner)
    matrices = []
    for parts in quads:
        matrices += [parts, tuple(swap_dp(ref, 1) for ref in parts)]

    seg_flat = segments.reshape(groups, length)
    seg_q = lax.dynamic_slice_in_dim(seg_flat, x * own_length, own_length, 1)
    seg_parts = seg_flat.reshape(groups, mp, own_length)
    seg_k = jnp.concatenate([pick(seg_parts, x ^ k, 1) for k in range(mp)], axis=1)
    q_edges = seg_q.reshape(groups, q_blocks, block)
    k_edges = seg_k.reshape(groups, k_blocks, block)
    live = (q_edges[:, :, None, 0] <= k_edges[:, None, :, -1]) & (
        k_edges[:, None, :, 0] <= q_edges[:, :, None, -1]
    )
    infos = [
        jnp.concatenate([x.reshape(1).astype(jnp.int32), live[m].reshape(-1).astype(jnp.int32)])
        for m in micros
    ]
    seg_q_rows = [seg_q[m][None, :] for m in micros]
    seg_k_columns = [seg_k[m][:, None] for m in micros]

    gains = reorder(jnp.stack([norm1_gain, norm2_gain], axis=1)[None], 0, place, chips, False)
    gain1, gain2 = gains[:, :1], gains[:, 1:]
    normed1, qkvs, others = [], [], []
    last = cots_far
    for m in micros:
        normed, qkv, kv = project(own_place, layer_in[m], gain1, matrices, last)
        last = [normed]
        normed1.append(normed)
        qkvs.append(qkv.reshape(4 * inner, own_length))
        others.append([swap_mp(kv, k).reshape(2 * inner, own_length) for k in x_masks()])
    weights = assemble(own_place, matrices, inner, [normed1[-1]])
    last = [weights]
    contexts, lses, normed2, normed2_far = [], [], [], []
    for m in micros:
        context, lse = attend(
            infos[m], qkvs[m], others[m], seg_q_rows[m], seg_k_columns[m], table,
            block, head_size, inner, last,
        )
        contexts.append(context)
        lses.append(lse)
        last = [context]
        normed = middle_layer(layer_in[m], context, weights, gain2, last)
        last = [normed]
        normed2.append(normed)
        normed2_far.append(swap_dp(normed, 1))

    ffn_info = jnp.concatenate([place, x.reshape(1).astype(jnp.int32)])
    chunk_acts, chunk_weights, corners = [], [], []
    for stack, width in zip(chunk_stacks, widths):
        if own_rows % 4 or width % LANES:
            ordered = jnp.stack(
                [
                    jnp.stack([pick(stack, (x ^ k) * chips + block_of(chip, p, depth), 0) for p in range(chips)])
                    for k in range(mp)
                ]
            ).reshape(mp, model, 3, width)
            stack = [jnp.transpose(ordered[k], (1, 0, 2)) for k in range(mp)]
        acts, matrices_in, grads = ffn_chunk(
            ffn_info, stack, width, normed2 + normed2_far, cots + cots_far, last
        )
        last = [acts[0]] + [c[1] for c in corners]
        chunk_acts.append(acts)
        chunk_weights.append(matrices_in)
        corners.append(scatter_corner(grads, [], [acts[0]] if len(widths) == 1 else []))
    corners[0] = hold(corners[0], chunk_acts[-1][0])
    back_far = down(chunk_weights, chunk_acts, 0, 2, groups, groups, chunk_acts[-1][:1])
    from_far = swap_dp(back_far, 1)
    back_own = down(chunk_weights, chunk_acts, 0, 2, 0, groups, [back_far])
    last = [back_own]

    z_count = len(far_masks)
    grad_attn, grad_q, grad_kv, bias_grads, gain2_grads = [], [], [], [], []
    for m in micros:
        low, grad_context, gain_grads = turn(
            m, layer_in[m], contexts[m], cots[m], (back_own, from_far), gain2, weights, last
        )
        last = [low]
        grad_attn.append(low)
        gain2_grads.append(gain_grads)
        dq, bias_grad, dkv = attend_grads(
            infos[m], qkvs[m], others[m], seg_q_rows[m], seg_k_columns[m], table,
            contexts[m], lses[m], grad_context, block, head_size, last,
        )
        last = [dq]
        grad_q.append(dq)
        bias_grads.append(bias_grad)
        grad_kv.append((dkv[0], [swap_mp(dkv[k], k) for k in x_masks()]))
        if m == micros[0]:
            sums = [scatter_xy(*corners[0], [dq])]
            waiting = [hold(corner, dq) for corner in corners[1:]]
            last += [sums[0][0]] + [corner[1] for corner in waiting]
    sums[0] = scatter_z(sums[0], 0, [dq])
    last.append(sums[0][0])
    weight_grads = outer_products(
        role_place,
        (0, 3),
        [
            [(normed1[m], grad_q[m]) for m in micros],
            [(grad_attn[m], contexts[m]) for m in micros],
        ],
        None,
        last,
    )
    ffn_far = down(chunk_weights, chunk_acts, 2, 1, groups, groups, [weight_grads])
    ffn_from = swap_dp(ffn_far, 1)
    ffn_own = down(chunk_weights, chunk_acts, 2, 1, 0, groups, [ffn_far])
    sums[0] = scatter_z(sums[0], 1, [ffn_own])
    last = [ffn_own, first_of(sums[0])]
    grad_kv = [sum_rows([own, *hold(got, ffn_own)], 1, after=[ffn_own]) for own, got in grad_kv]
    weight_grads = outer_products(
        role_place,
        (1, 2),
        [[(normed1[m], (grad_kv[m], n)) for m in micros] for n in range(2)],
        weight_grads,
        last,
    )
    sums += [scatter_xy(*corner, [weight_grads]) for corner in waiting]

    half = model // 2
    split = [half, half // 2, half // 2]
    if part == inner:
        got = [swap_dp(weight_grads[2 * k + 1 : 2 * k + 2], 1) for k in range(mp)]
        quads = [
            sum_rows([weight_grads, got[k]], 2 if k == 0 else split, [2 * k, 0], 1)
            for k in range(mp)
        ]
    else:
        ordered = jnp.concatenate(
            [lax.dynamic_slice_in_dim(weight_grads, role_place[0] ^ r, 1, 0) for r in range(4)]
        )
        by_part = jnp.transpose(
            ordered.reshape(4, model, inner // part, part), (0, 2, 1, 3)
        ).reshape(mp, 2, model, part)
        near = add_low(pick(by_part, core, 1), swap_dp(pick(by_part, 1 - core, 1), 1))
        quads = []
        for k in range(mp):
            matrix = pick(near, x ^ k, 0)[None]
            sizes = [half, half] if k == 0 else split
            starts = [sum(sizes[:n]) for n in range(len(sizes))]
            quads.append(tuple(matrix[:, a : a + n] for a, n in zip(starts, sizes)))
    grad_inputs, gain1_grads = input_grads(
        place,
        [(layer_in[m], grad_attn[m], grad_q[m], grad_kv[m]) for m in micros],
        gain1,
        weights,
        chips,
        [quads[0][0]] + [parts[0] for parts in sums[1:]],
    )
    corner = scatter_corner(quads, [], [gain1_grads])
    last = [gain1_grads, corner[1]]
    sums[1:] = [scatter_z(parts, 0, [gain1_grads]) for parts in sums[1:]]
    last += [parts[0] for parts in sums[1:]]
    outputs = finish(
        place,
        [(layer_in[m], contexts[m]) for m in micros],
        (ffn_own, ffn_from),
        weights,
        chips,
        last,
    )
    sums[1:] = [scatter_z(parts, 1, [outputs]) for parts in sums[1:]]
    total = scatter_xy(*corner, [outputs])
    for stage in range(z_count):
        total = scatter_z(total, stage)
    piece = total[0]
    for stage in range(2, z_count):
        sums = [scatter_z(parts, stage) for parts in sums]
    over_x = jnp.stack([piece] + [swap_mp(piece, k) for k in x_masks()])
    kept = either(core, over_x[:, :own_rows], over_x[:, own_rows:])
    got = swap_dp(either(core, over_x[:, own_rows:], over_x[:, :own_rows]), 1)
    both = jnp.stack([kept, got], axis=1).reshape(2 * mp, own_rows, part)
    final = jnp.concatenate(
        [pick(both, (2 * x + core) ^ r, 0) for r in range(2 * mp)], axis=1
    ).astype(F32)

    sums = jnp.concatenate(sums, axis=2)
    kept = either(core, sums[:, :own_rows], sums[:, own_rows:])
    got = swap_dp(either(core, sums[:, own_rows:], sums[:, :own_rows]), 1)
    ffn_grads = either(
        core, jnp.concatenate([kept, got], axis=2), jnp.concatenate([got, kept], axis=2)
    ).astype(F32)

    bias_rows = sum(bias_grads)
    bias_tiles = sum(
        jnp.pad(bias_rows[:, :, :, t, : 2 * block - 7 + t], ((0, 0),) * 3 + ((7 - t, 0),))
        for t in range(8)
    )
    run = 2 * q_blocks - 1
    bias_flat = jnp.zeros((head_count, 2 * k_blocks - 1, 2 * block), F32)
    for k in range(mp):
        first = k_blocks - q_blocks - ((x ^ k) - x) * q_blocks
        held = lax.dynamic_slice_in_dim(bias_flat, first, run, 1)
        bias_flat = lax.dynamic_update_slice_in_dim(bias_flat, held + bias_tiles[:, k], first, 1)
    left = jnp.pad(bias_flat[:, :, :block], ((0, 0), (0, 1), (0, 0)))
    right = jnp.pad(bias_flat[:, :, block:], ((0, 0), (1, 0), (0, 0)))
    offsets_total = (left + right).reshape(head_count, 2 * k_blocks * block)
    bucket_part = jnp.dot(bucket_hot.T, offsets_total.T, precision=TOP_PRECISION)
    rel_part = jnp.dot(bucket_part, head_hot, precision=TOP_PRECISION)
    gain_parts = jnp.concatenate([gain1_grads, sum(gain2_grads)], axis=1)
    gain_parts = reorder(gain_parts[None], 0, place, chips, True)
    small = jnp.concatenate([gain_parts[:, 0], gain_parts[:, 1], rel_part.reshape(-1)])
    small = sum_all(small, [outputs])

    shape = inputs.shape

    def placed(array):
        return jnp.transpose(array, (0, 2, 1)).reshape(shape)

    return (
        placed(outputs),
        placed(grad_inputs),
        small[2 * model :].reshape(rel_table.shape),
        small[:model],
        small[model : 2 * model],
        final[:, :inner],
        final[:, inner : 2 * inner],
        final[:, 2 * inner : 3 * inner],
        jnp.transpose(final[:, 3 * inner :]),
        ffn_grads[0],
        ffn_grads[1],
        jnp.transpose(ffn_grads[2]),
    )


def solution(mesh):
    devices = mesh.devices.reshape(-1, 2, mesh.shape["mp"])
    return jax.shard_map(
        body,
        mesh=jax.sharding.Mesh(devices, DP + ("mp",)),
        in_specs=(
            P(None, DP, "mp", None),
            P(None, DP, "mp", None),
            P(None, DP, None),
            P(),
            P(),
            P(),
            P(),
            P(),
            P(DP, None),
            P(DP, None),
            P(DP, None),
            P(None, DP),
            P(DP, "mp"),
            P(DP, "mp"),
            P("mp", DP),
        ),
        out_specs=(
            P(None, DP, "mp", None),
            P(None, DP, "mp", None),
            P(),
            P(),
            P(),
            P(DP, None),
            P(DP, None),
            P(DP, None),
            P(None, DP),
            P(DP, "mp"),
            P(DP, "mp"),
            P("mp", DP),
        ),
        check_vma=False,
    )
```

```python
import functools

import jax
import jax.numpy as jnp
from jax import lax
from jax.experimental import pallas as pl
from jax.experimental.pallas import tpu as pltpu
from jax.sharding import PartitionSpec as P

EPSILON = 1e-06
TOP_PRECISION = lax.Precision.HIGHEST
GELU_SCALE = 0.7978845608028654
GELU_CUBE = 0.044715
BF16 = jnp.bfloat16
F32 = jnp.float32
NEGATIVE = -1e30
VMEM_BYTES = 60 * 1024 * 1024
LANES = 128
COST_SHARE = 1.0
FIRST_SEVENTHS = 4


DP = ("chip", "core")


def dp_size():
    return lax.axis_size("chip") * lax.axis_size("core")


def swap_dp(array, mask):
    return lax.ppermute(array, DP, [(i, i ^ mask) for i in range(dp_size())])


def swap_mp(array, mask):
    count = lax.axis_size("mp")
    return lax.ppermute(array, "mp", [(i, i ^ mask) for i in range(count)])


def pick(array, index, axis):
    return lax.dynamic_index_in_dim(array, index, axis, keepdims=False)


def add_low(*terms):
    total = terms[0].astype(F32)
    for term in terms[1:]:
        total = total + term.astype(F32)
    return total.astype(BF16)


def trade_rows(array, core, rows):
    low, high = array[:, :rows], array[:, rows:]
    return either(core, low, high), swap_dp(either(core, high, low), 1)


def first_of(parts):
    return parts[0] if isinstance(parts, tuple) else parts


def either(flag, first, second):
    return jnp.where(flag == 0, first, second)


def hold(value, *tokens):
    return lax.optimization_barrier((value, *tokens))[0] if tokens else value


def z_masks():
    masks, mask = [], dp_size() // 2
    while mask > 2:
        masks.append(mask)
        mask //= 2
    return masks


def x_masks():
    return range(1, lax.axis_size("mp"))


def merged(parts):
    kinds, rows, columns = parts[0].shape
    return jnp.stack(parts, axis=1).reshape(kinds, len(parts) * rows, columns)


def gather_xy(own, first=(), then=()):
    own = hold(own, *first)
    return hold((swap_dp(own, 2), [swap_mp(own, k) for k in x_masks()]), *then)


def gather_corner(over_y, over_x, first=(), then=()):
    half = over_y.shape[1] // 2
    low = hold(rows_of(over_y, 0, half), *first)
    result = []
    for k, other in zip(x_masks(), over_x):
        high = hold(rows_of(other, half, half), *first)
        result.append((swap_mp(low, k), swap_dp(high, 2)))
    return hold(result, *then)


def quads_of(own, over_y, over_x, corner):
    return [(own, over_y)] + [(other, *parts) for other, parts in zip(over_x, corner)]


def scatter_corner(quads, first=(), then=()):
    own, to_y = quads[0]
    got = []
    for k, (_, low, high) in zip(x_masks(), quads[1:]):
        got.append((swap_mp(hold(low, *first), k), swap_dp(hold(high, *first), 2)))
    got = hold(got, *then)
    if len(got) == 1:
        to_y, to_x = add_corner(to_y, got[0][0], quads[1][0], got[0][1], then)
        return own, to_y, [to_x]
    half = own.shape[1] // 2
    low = add_low(to_y[:, :half], *[part for part, _ in got])
    to_x = [
        jnp.concatenate([parts[0][:, :half], add_low(parts[0][:, half:], part)], axis=1)
        for parts, (_, part) in zip(quads[1:], got)
    ]
    return own, jnp.concatenate([low, to_y[:, half:]], axis=1), to_x


def scatter_xy(own, to_y, to_x, then=()):
    got = [swap_dp(to_y, 2)] + [swap_mp(other, k) for k, other in zip(x_masks(), to_x)]
    return sum_rows([own, *hold(got, *then)], 2, after=then)


def scatter_z(pair, stage, then=()):
    masks = z_masks()
    mask = masks[len(masks) - 1 - stage]
    got = hold(swap_dp(pair[1], mask), *then)
    return sum_rows([pair[0], got], 1 if stage == len(masks) - 1 else 2, after=then)


def doubling(count):
    masks, mask = [], 1
    while mask < count:
        masks.append(mask)
        mask *= 2
    return masks


def beside(got, values, steps):
    if not steps:
        return got, values
    swap, mask = steps.pop(0)
    got, other = lax.optimization_barrier((got, swap(values, mask)))
    return got, values + other


def call(
    kernel, name, grid, in_specs, out_specs, out_shape, operands, flops=0, scratch=(), scalars=0, after=(),
    aliases=None,
):
    moved = sum(a.size * a.dtype.itemsize for a in operands)
    moved += sum(s.size * s.dtype.itemsize for s in out_shape)
    count = len(operands)

    def run(*refs):
        kernel(*refs[:count], *refs[count + len(after) :])

    return pl.pallas_call(
        run,
        grid_spec=pltpu.PrefetchScalarGridSpec(
            num_scalar_prefetch=scalars,
            grid=grid,
            in_specs=list(in_specs) + [pl.BlockSpec(memory_space=pl.ANY)] * len(after),
            out_specs=out_specs,
            scratch_shapes=list(scratch),
        ),
        out_shape=out_shape,
        input_output_aliases=aliases or {},
        compiler_params=pltpu.CompilerParams(vmem_limit_bytes=VMEM_BYTES),
        cost_estimate=pl.CostEstimate(
            flops=int(flops * COST_SHARE),
            bytes_accessed=int(moved * COST_SHARE),
            transcendentals=0,
        ),
        name=name,
    )(*operands, *after)


def whole(shape):
    return pl.BlockSpec(shape, lambda *_: (0,) * len(shape), pipeline_mode=pl.Buffered(1))


def slab(*shape):
    return pl.BlockSpec((1,) + shape, lambda m, *_: (m,) + (0,) * len(shape))


def columns(wide, step):
    return pl.BlockSpec((wide, step), lambda j, *_: (0, j))


def lane_step(length):
    return 256 if length % 256 == 0 else length


def dot_nn(left, right):
    return lax.dot_general(left, right, (((1,), (0,)), ((), ())), preferred_element_type=F32)


def dot_tn(left, right):
    return lax.dot_general(left, right, (((0,), (0,)), ((), ())), preferred_element_type=F32)


def dot_nt(left, right):
    return lax.dot_general(left, right, (((1,), (1,)), ((), ())), preferred_element_type=F32)


def transposed(value):
    return jnp.transpose(value.astype(F32), (1, 0)).astype(BF16)


def block_of(place, position, depth):
    z, y = place // 2, place % 2
    masks, left, mask = 0, position % depth, depth
    while mask > 1:
        mask //= 2
        masks += mask * (left % 2)
        left //= 2
    return (z ^ masks) * 2 + (y ^ (position // depth))


def reorder_kernel(outward, info_ref, in_ref, out_ref):
    blocks = out_ref.shape[0]
    for p in range(blocks):
        chip = block_of(info_ref[0], p, blocks // 2)
        if outward:
            out_ref[chip] = in_ref[0, p]
        else:
            out_ref[p] = in_ref[0, chip]


def reorder(array, group, place, blocks, outward, after=()):
    groups, wide, length = array.shape
    split = array.reshape(groups, blocks, wide // blocks, length)
    return call(
        functools.partial(reorder_kernel, outward),
        "reorder",
        (1,),
        [pl.BlockSpec((1,) + split.shape[1:], lambda *_: (group, 0, 0, 0))],
        [pl.BlockSpec(split.shape[1:], lambda *_: (0, 0, 0))],
        [jax.ShapeDtypeStruct(split.shape[1:], array.dtype)],
        [place, split],
        scalars=1,
        after=after,
    )[0].reshape(wide, length)


def bias_kernel(window_ref, table_ref):
    count, block = table_ref.shape[1], table_ref.shape[-1]
    for entry in range(count):
        wide = jnp.broadcast_to(window_ref[0, entry], (block, 2 * block))
        rolled = pltpu.roll(wide, block + 1, 1, stride=1, stride_axis=0)
        table_ref[0, entry] = rolled[:, :block]


def bias_table(windows, block, after):
    heads, count = windows.shape[:2]
    return call(
        bias_kernel,
        "bias_table",
        (heads,),
        [slab(count, 1, 2 * block)],
        [slab(count, block, block)],
        [jax.ShapeDtypeStruct((heads, count, block, block), F32)],
        [windows],
        after=after,
    )[0]


def project_kernel(counts, limit, info_ref, x_ref, gain_ref, *refs):
    matrices, (normed_ref, out_ref, kv_ref) = split_refs(refs, counts)
    first = kv_ref.shape[0] // 2
    values = x_ref[...].astype(F32)
    factor = lax.rsqrt(jnp.mean(values * values, axis=0, keepdims=True) + EPSILON)
    normed = (values * factor * gain_ref[...]).astype(BF16)
    normed_ref[...] = normed
    for r, parts in enumerate(matrices):
        place = info_ref[0] ^ r

        @pl.when(place < limit)
        def _(parts=parts, place=place):
            weights = joined([ref[0] for ref in parts], 0)
            product = dot_tn(weights, normed).astype(BF16)
            out_ref[place] = product

            @pl.when(place >= first)
            def _():
                kv_ref[place - first] = product


def project(place, x, gain, matrices, after):
    wide, length = x.shape
    part = matrices[0][0].shape[2]
    limit = len(matrices) * 3 // 4
    step = lane_step(length)
    counts = [len(parts) for parts in matrices]
    flat = [ref for parts in matrices for ref in parts]
    return call(
        functools.partial(project_kernel, counts, limit),
        "project",
        (length // step,),
        [columns(wide, step), whole((wide, 1))] + [whole(ref.shape) for ref in flat],
        [
            columns(wide, step),
            pl.BlockSpec((len(matrices), part, step), lambda j, *_: (0, 0, j)),
            pl.BlockSpec((len(matrices) // 2, part, step), lambda j, *_: (0, 0, j)),
        ],
        [
            jax.ShapeDtypeStruct((wide, length), BF16),
            jax.ShapeDtypeStruct((len(matrices), part, length), BF16),
            jax.ShapeDtypeStruct((len(matrices) // 2, part, length), BF16),
        ],
        [place, x, gain, *flat],
        flops=2 * wide * length * limit * part,
        scalars=1,
        after=after,
    )


def assemble_kernel(counts, info_ref, *refs):
    matrices, (out_ref,) = split_refs(refs, counts)
    for r, parts in enumerate(matrices):
        place, row = info_ref[0] ^ r, 0
        for ref in parts:
            rows = ref.shape[1]
            out_ref[place, row : row + rows] = ref[0]
            row += rows


def assemble(place, matrices, inner, after):
    part = matrices[0][0].shape[2]
    counts = [len(parts) for parts in matrices]
    flat = [ref for parts in matrices for ref in parts]
    wide = sum(ref.shape[1] for ref in matrices[0])
    shape = (len(matrices), wide, part)
    ordered = call(
        functools.partial(assemble_kernel, counts),
        "assemble",
        (1,),
        [whole(ref.shape) for ref in flat],
        [pl.BlockSpec(shape, lambda *_: (0, 0, 0))],
        [jax.ShapeDtypeStruct(shape, BF16)],
        [place, *flat],
        scalars=1,
        after=after,
    )[0]
    return jnp.transpose(ordered.reshape(4, inner // part, wide, part), (0, 2, 1, 3)).reshape(
        4, wide, inner
    )


def middle_kernel(x_ref, context_ref, w_ref, gain_ref, normed_ref):
    values = x_ref[...].astype(F32) + dot_nn(w_ref[0], context_ref[...])
    factor = lax.rsqrt(jnp.mean(values * values, axis=0, keepdims=True) + EPSILON)
    normed_ref[...] = (values * factor * gain_ref[...]).astype(BF16)


def out_weights(weights):
    return pl.BlockSpec(
        (1,) + weights.shape[1:], lambda *_: (3, 0, 0), pipeline_mode=pl.Buffered(1)
    )


def middle_layer(x, context, weights, gain, after):
    wide, length = x.shape
    inner = weights.shape[2]
    step = lane_step(length)
    return call(
        middle_kernel,
        "middle",
        (length // step,),
        [columns(wide, step), columns(inner, step), out_weights(weights), whole((wide, 1))],
        [columns(wide, step)],
        [jax.ShapeDtypeStruct((wide, length), BF16)],
        [x, context, weights, gain],
        flops=2 * wide * length * inner,
        after=after,
    )[0]


def lifted_grads(values, gain, grad):
    factor = lax.rsqrt(jnp.mean(values * values, axis=0, keepdims=True) + EPSILON)
    scaled = values * factor
    lifted = grad * gain
    inner = jnp.mean(lifted * scaled, axis=0, keepdims=True)
    return factor * (lifted - scaled * inner), jnp.sum(grad * scaled, axis=1, keepdims=True)


def add_up(ref, value):
    first = pl.program_id(0) == 0

    @pl.when(first)
    def _():
        ref[...] = value

    @pl.when(jnp.logical_not(first))
    def _():
        ref[...] += value


def turn_kernel(
    x_ref, context_ref, cot_ref, back0_ref, back1_ref, gain_ref, w_ref, low_ref, grad_ref, gain_grad_ref
):
    middle = x_ref[...].astype(F32) + dot_nn(w_ref[0], context_ref[...])
    grad = back0_ref[0].astype(F32) + back1_ref[0].astype(F32)
    normed_grad, gain_grad = lifted_grads(middle, gain_ref[...], grad)
    add_up(gain_grad_ref, gain_grad)
    low = (cot_ref[...].astype(F32) + normed_grad).astype(BF16)
    low_ref[...] = low
    grad_ref[...] = dot_tn(w_ref[0], low).astype(BF16)


def turn(group, x, context, cot, back, gain, weights, after):
    wide, length = x.shape
    inner = weights.shape[2]
    step = lane_step(length)
    big = columns(wide, step)
    part = pl.BlockSpec((1, wide, step), lambda j, *_: (group, 0, j))
    return call(
        turn_kernel,
        "turn",
        (length // step,),
        [big, columns(inner, step), big, part, part, whole((wide, 1)), out_weights(weights)],
        [big, columns(inner, step), pl.BlockSpec((wide, 1), lambda *_: (0, 0))],
        [
            jax.ShapeDtypeStruct((wide, length), BF16),
            jax.ShapeDtypeStruct((inner, length), BF16),
            jax.ShapeDtypeStruct((wide, 1), F32),
        ],
        [x, context, cot, *back, gain, weights],
        flops=4 * wide * length * inner,
        after=after,
    )


def put_blocks(info_ref, out_ref, values):
    if len(out_ref.shape) == 3:
        out_ref[0] = values.astype(out_ref.dtype)
        return
    blocks, rows = out_ref.shape[1:3]
    for p in range(blocks):
        chip = block_of(info_ref[0], p, blocks // 2)
        out_ref[0, chip] = values[p * rows : (p + 1) * rows].astype(out_ref.dtype)


def outward_spec(groups, wide, length, blocks, step):
    rows, steps = wide // blocks, length // step
    if rows % 8:
        spec = pl.BlockSpec((1, wide, step), lambda j, *_: (j // steps, 0, j % steps))
        return spec, jax.ShapeDtypeStruct((groups, wide, length), BF16)
    return (
        pl.BlockSpec((1, blocks, rows, step), lambda j, *_: (j // steps, 0, 0, j % steps)),
        jax.ShapeDtypeStruct((groups, blocks, rows, length), BF16),
    )


def outward(array, place, blocks):
    if array.ndim == 4:
        return array.reshape(array.shape[0], -1, array.shape[3])
    return jnp.stack([reorder(array, m, place, blocks, True) for m in range(array.shape[0])])


def group_columns(group, steps, *shape):
    def index(j, *_):
        return (0,) * (len(shape) - 1) + (jnp.clip(j - group * steps, 0, steps - 1),)

    return pl.BlockSpec(shape, index)


def in_groups(kernel, counts, steps, *refs):
    lead, each, groups = counts
    group = pl.program_id(0) // steps
    shared, rest = refs[:lead], refs[lead:]
    parts, tail = rest[: each * groups], rest[each * groups :]
    for m in range(groups):

        @pl.when(group == m)
        def _(m=m):
            kernel(*shared, *parts[each * m : each * (m + 1)], *tail)


def finish_kernel(info_ref, x_ref, context_ref, ffn0_ref, ffn1_ref, w_ref, out_ref):
    middle = x_ref[...].astype(F32) + dot_nn(w_ref[0], context_ref[...])
    total = middle + (ffn0_ref[0].astype(F32) + ffn1_ref[0].astype(F32))
    put_blocks(info_ref, out_ref, total)


def finish(place, terms, ffn, weights, blocks, after):
    wide, length = terms[0][0].shape
    inner = weights.shape[2]
    step = lane_step(length)
    groups, steps = len(terms), length // step
    spec, shape = outward_spec(groups, wide, length, blocks, step)
    specs = []
    for m in range(groups):
        specs += [group_columns(m, steps, wide, step), group_columns(m, steps, inner, step)]
    part = pl.BlockSpec((1, wide, step), lambda j, *_: (j // steps, 0, j % steps))
    result = call(
        functools.partial(in_groups, finish_kernel, (1, 2, groups), steps),
        "finish",
        (groups * steps,),
        specs + [part, part, out_weights(weights)],
        [spec],
        [shape],
        [place, *[array for term in terms for array in term], *ffn, weights],
        flops=2 * groups * wide * length * inner,
        scalars=1,
        after=after,
    )[0]
    return outward(result, place, blocks)


def outer_kernel(count, info_ref, *refs):
    out_ref = refs[-1]
    step = pl.program_id(0)
    for r in range(len(refs) // (2 * count)):
        pairs = refs[2 * count * r : 2 * count * (r + 1)]

        @pl.when(step == r)
        def _(pairs=pairs):
            total = dot_nt(pairs[0][...], matrix_of(pairs[1]))
            for m in range(1, count):
                total = total + dot_nt(pairs[2 * m][...], matrix_of(pairs[2 * m + 1]))
            out_ref[0] = total.astype(BF16)


def matrix_of(ref):
    return ref[0] if len(ref.shape) == 3 else ref[...]


def outer_products(place, roles, matrices, into, after):
    count = len(matrices[0])
    wide, length = matrices[0][0][0].shape
    low, high = roles
    operands, specs = [], []
    for left, right in [pair for pairs in matrices for pair in pairs]:
        right, number = right if isinstance(right, tuple) else (right, None)
        inner = right.shape[-2]
        operands += [left, right]
        specs.append(whole(left.shape))
        if number is None:
            specs.append(whole(right.shape))
        else:
            specs.append(
                pl.BlockSpec(
                    (1, inner, length),
                    lambda *_, n=number: (n, 0, 0),
                    pipeline_mode=pl.Buffered(1),
                )
            )

    def index(step, info):
        return (jnp.where(step == 0, low, high) ^ info[0], 0, 0)

    if into is not None:
        operands.append(into)
        specs.append(pl.BlockSpec(memory_space=pl.ANY))

    def kernel(info_ref, *refs):
        if into is not None:
            refs = refs[:-2] + refs[-1:]
        outer_kernel(count, info_ref, *refs)

    return call(
        kernel,
        "outer_products",
        (len(matrices),),
        specs,
        [pl.BlockSpec((1, wide, inner), index)],
        [jax.ShapeDtypeStruct((4, wide, inner), BF16)],
        [place, *operands],
        flops=2 * wide * inner * length * count * len(matrices),
        scalars=1,
        after=after,
        aliases=None if into is None else {len(operands): 0},
    )[0]


def input_kernel(info_ref, x_ref, low_ref, dq_ref, dkv_ref, gain_ref, w_ref, out_ref, gain_grad_ref):
    grad = (
        dot_nn(w_ref[0], dq_ref[...]) + dot_nn(w_ref[1], dkv_ref[0]) + dot_nn(w_ref[2], dkv_ref[1])
    )
    normed_grad, gain_grad = lifted_grads(x_ref[...].astype(F32), gain_ref[...], grad)
    add_up(gain_grad_ref, gain_grad)
    put_blocks(info_ref, out_ref, low_ref[...].astype(F32) + normed_grad)


def input_grads(place, terms, gain, weights, blocks, after):
    wide, length = terms[0][0].shape
    inner = weights.shape[2]
    step = lane_step(length)
    groups, steps = len(terms), length // step
    spec, shape = outward_spec(groups, wide, length, blocks, step)
    specs = []
    for m in range(groups):
        big = group_columns(m, steps, wide, step)
        specs += [big, big, group_columns(m, steps, inner, step), group_columns(m, steps, 2, inner, step)]
    result, gain_grads = call(
        functools.partial(in_groups, input_kernel, (1, 4, groups), steps),
        "input_grads",
        (groups * steps,),
        specs
        + [
            whole((wide, 1)),
            pl.BlockSpec((3,) + weights.shape[1:], lambda *_: (0, 0, 0), pipeline_mode=pl.Buffered(1)),
        ],
        [spec, pl.BlockSpec((wide, 1), lambda *_: (0, 0))],
        [shape, jax.ShapeDtypeStruct((wide, 1), F32)],
        [place, *[array for term in terms for array in term], gain, weights],
        flops=6 * groups * wide * length * inner,
        scalars=1,
        after=after,
    )
    return outward(result, place, blocks), gain_grads


def rows_kernel(in_ref, out_ref):
    out_ref[...] = in_ref[...]


def rows_of(array, start, rows):
    kinds, _, width = array.shape
    if rows % 16:
        return array[:, start : start + rows]
    return call(
        rows_kernel,
        "rows",
        (kinds,),
        [pl.BlockSpec((1, rows, width), lambda k: (k, start // rows, 0))],
        [pl.BlockSpec((1, rows, width), lambda k: (k, 0, 0))],
        [jax.ShapeDtypeStruct((kinds, rows, width), array.dtype)],
        [array],
    )[0]


def merge_kernel(first_ref, second_ref, out_ref):
    parts = [first_ref[0].astype(F32), second_ref[0].astype(F32)]
    out_ref[0] = jnp.concatenate(parts, axis=0).astype(out_ref.dtype)


def merge(first, second):
    kinds, rows, width = first.shape
    if rows % 8:
        return jnp.concatenate([first, second], axis=1)
    return call(
        merge_kernel,
        "merge",
        (kinds,),
        [slab(rows, width), slab(rows, width)],
        [slab(2 * rows, width)],
        [jax.ShapeDtypeStruct((kinds, 2 * rows, width), first.dtype)],
        [first, second],
    )[0]


def sum_kernel(count, *refs):
    total = refs[0][0].astype(F32)
    for ref in refs[1:count]:
        total = total + ref[0].astype(F32)
    row = 0
    for ref in refs[count:]:
        rows = ref.shape[1]
        ref[0] = total[row : row + rows].astype(BF16)
        row += rows


def sum_rows(terms, parts, starts=None, kinds=None, after=()):
    starts = starts or [0] * len(terms)
    kinds = kinds or terms[0].shape[0]
    rows, width = terms[0].shape[1:]
    sizes = [rows // parts] * parts if isinstance(parts, int) else list(parts)
    if sizes[0] % 8:
        total = add_low(*[term[a : a + kinds] for term, a in zip(terms, starts)])
        results, row = [], 0
        for size in sizes:
            results.append(total[:, row : row + size])
            row += size
    else:
        results = call(
            functools.partial(sum_kernel, len(terms)),
            "sum_rows",
            (kinds,),
            [pl.BlockSpec((1, rows, width), lambda k, a=a: (a + k, 0, 0)) for a in starts],
            [slab(size, width) for size in sizes],
            [jax.ShapeDtypeStruct((kinds, size, width), BF16) for size in sizes],
            terms,
            after=after,
        )
    return results[0] if len(sizes) == 1 else tuple(results)


def corner_kernel(y_ref, first_ref, x_ref, second_ref, y_out, x_out):
    y_out[...] = (y_ref[...].astype(F32) + first_ref[...].astype(F32)).astype(BF16)
    x_out[...] = (x_ref[...].astype(F32) + second_ref[...].astype(F32)).astype(BF16)


def add_corner(to_y, first, to_x, second, after):
    kinds, half, width = first.shape
    upper = pl.BlockSpec((1, half, width), lambda k: (k, 0, 0))
    lower = pl.BlockSpec((1, half, width), lambda k: (k, 1, 0))
    return call(
        corner_kernel,
        "add_corner",
        (kinds,),
        [upper, upper, lower, upper],
        [upper, lower],
        [jax.ShapeDtypeStruct(to_y.shape, BF16), jax.ShapeDtypeStruct(to_x.shape, BF16)],
        [to_y, first, to_x, second],
        aliases={0: 0, 2: 1},
        after=after,
    )


def halves(value_t, half):
    zero = jnp.zeros((half, value_t.shape[1]), value_t.dtype)
    return (
        jnp.concatenate([value_t[:half], zero], axis=0),
        jnp.concatenate([zero, value_t[half:]], axis=0),
    )


def attend_kernel(sources, block, half, info_ref, q_ref, *refs):
    kv_refs = refs[: 2 * sources]
    segq_ref, segk_ref, table_ref, ctx_ref, lse_ref = refs[2 * sources : 2 * sources + 5]
    s_scr, m_scr, l_scr, acc_scr, k_scr = refs[2 * sources + 5 :]
    length = q_ref.shape[1]
    q_blocks = length // block
    k_blocks = q_blocks * sources
    place_x = info_ref[0]
    for s in range(sources):
        k_scr[s * length : (s + 1) * length, :] = transposed(kv_refs[2 * s][...])
    for qb in range(q_blocks):
        rows = pl.ds(qb * block, block)
        q_heads = halves(q_ref[:, rows], half)
        seg_q = segq_ref[:, rows]
        m_scr[...] = jnp.full(m_scr.shape, NEGATIVE, F32)
        l_scr[...] = jnp.zeros(l_scr.shape, F32)
        acc_scr[...] = jnp.zeros(acc_scr.shape, F32)
        for kb in range(k_blocks):
            s, lb = divmod(kb, q_blocks)
            live = info_ref[1 + qb * k_blocks + kb]

            @pl.when(live != 0)
            def _(s=s, lb=lb, kb=kb):
                entry = k_blocks - 1 - ((place_x ^ s) * q_blocks + lb - place_x * q_blocks - qb)
                keys = k_scr[pl.ds(kb * block, block), :]
                kept = segk_ref[pl.ds(kb * block, block), :] == seg_q
                for h in range(2):
                    score = dot_nn(keys, q_heads[h]) + table_ref[h, entry]
                    score = jnp.where(kept, score, NEGATIVE)
                    s_scr[h, kb] = score
                    m_scr[h] = jnp.maximum(m_scr[h], jnp.max(score, axis=0, keepdims=True))

        for kb in range(k_blocks):
            s, lb = divmod(kb, q_blocks)
            live = info_ref[1 + qb * k_blocks + kb]

            @pl.when(live != 0)
            def _(s=s, lb=lb, kb=kb):
                for h in range(2):
                    prob = jnp.exp(s_scr[h, kb] - m_scr[h])
                    l_scr[h] += jnp.sum(prob, axis=0, keepdims=True)
                    values_t = kv_refs[2 * s + 1][
                        h * half : (h + 1) * half, lb * block : (lb + 1) * block
                    ]
                    acc_scr[h * half : (h + 1) * half] += dot_nn(values_t, prob.astype(BF16))

        for h in range(2):
            lse_ref[0, h : h + 1, rows] = m_scr[h] + jnp.log(l_scr[h])
            ctx_ref[h * half : (h + 1) * half, rows] = (
                acc_scr[h * half : (h + 1) * half] / l_scr[h]
            ).astype(BF16)


def grad_kernel(sources, block, half, info_ref, q_ref, *refs):
    kv_refs = refs[: 2 * sources]
    refs = refs[2 * sources :]
    segq_ref, segk_ref, table_ref, ctx_ref, lse_ref, gctx_ref = refs[:6]
    dq_ref, gbias_ref = refs[6:8]
    dkv_refs = refs[8 : 8 + sources]
    dk_scr, dv_scr, dq_scr, k_scr, v_scr, db_scr = refs[8 + sources :]
    length = q_ref.shape[1]
    q_blocks = length // block
    k_blocks = q_blocks * sources
    place_x = info_ref[0]
    db_scr[...] = jnp.zeros(db_scr.shape, F32)
    for s in range(sources):
        k_scr[s * length : (s + 1) * length, :] = transposed(kv_refs[2 * s][...])
        v_scr[s * length : (s + 1) * length, :] = transposed(kv_refs[2 * s + 1][...])
    dk_scr[...] = jnp.zeros(dk_scr.shape, F32)
    dv_scr[...] = jnp.zeros(dv_scr.shape, F32)
    for qb in range(q_blocks):
        rows = pl.ds(qb * block, block)
        query_t = q_ref[:, rows]
        grad_out_t = gctx_ref[:, rows]
        product = grad_out_t.astype(F32) * ctx_ref[:, rows].astype(F32)
        deltas = (
            jnp.sum(product[:half], axis=0, keepdims=True),
            jnp.sum(product[half:], axis=0, keepdims=True),
        )
        q_heads = halves(query_t, half)
        g_heads = halves(grad_out_t, half)
        seg_q = segq_ref[:, rows]
        dq_scr[...] = jnp.zeros(dq_scr.shape, F32)
        for kb in range(k_blocks):
            s, lb = divmod(kb, q_blocks)
            live = info_ref[1 + qb * k_blocks + kb]

            @pl.when(live != 0)
            def _(s=s, lb=lb, kb=kb):
                entry = k_blocks - 1 - ((place_x ^ s) * q_blocks + lb - place_x * q_blocks - qb)
                key_rows = pl.ds(kb * block, block)
                keys = k_scr[key_rows, :]
                values = v_scr[key_rows, :]
                kept = segk_ref[key_rows, :] == seg_q
                for h in range(2):
                    score = dot_nn(keys, q_heads[h]) + table_ref[h, entry]
                    score = jnp.where(kept, score, NEGATIVE)
                    prob = jnp.exp(score - lse_ref[0, h : h + 1, rows])
                    grad_prob = dot_nn(values, g_heads[h])
                    grad_score = prob * (grad_prob - deltas[h])
                    db_scr[h, s, q_blocks - 1 - lb + qb] += grad_score
                    low = grad_score.astype(BF16)
                    head = slice(h * half, (h + 1) * half)
                    key_lanes = slice(kb * block, (kb + 1) * block)
                    dk_scr[head, key_lanes] += dot_nt(query_t[head], low)
                    dv_scr[head, key_lanes] += dot_nt(grad_out_t[head], prob.astype(BF16))
                    keys_t = kv_refs[2 * s][head, lb * block : (lb + 1) * block]
                    dq_scr[head] += dot_nn(keys_t, low)

        dq_ref[:, rows] = dq_scr[...].astype(BF16)
    for s in range(sources):
        lanes = slice(s * length, (s + 1) * length)
        dkv_refs[s][0] = dk_scr[:, lanes].astype(BF16)
        dkv_refs[s][1] = dv_scr[:, lanes].astype(BF16)

    for h in range(2):
        for s in range(sources):
            for n in range(2 * q_blocks - 1):
                gbias_ref[h, s, n] = diagonal_sums(db_scr[h, s, n])


def diagonal_sums(tile):
    block = tile.shape[0]
    count = block
    if block == 2 * LANES:
        zero = jnp.zeros((LANES, LANES), F32)
        tile = jnp.concatenate(
            [
                tile[LANES:, :LANES],
                tile[LANES:, LANES:] + tile[:LANES, :LANES],
                tile[:LANES, LANES:],
                zero,
            ],
            axis=1,
        )
        count = LANES
    else:
        tile = jnp.concatenate([tile, jnp.zeros_like(tile)], axis=1)
    while count > 8:
        count //= 2
        tile = pltpu.roll(tile[:count], count, 1) + tile[count:]
    return tile


def attention_specs(sources, length, block, pairs, width):
    k_blocks = length * sources // block
    entries = 2 * k_blocks - 1

    def rows(offset):
        return pl.BlockSpec((width, length), lambda p, info: (p + offset, 0))

    kv_specs = [rows(pairs), rows(2 * pairs)] + [rows(0), rows(pairs)] * (sources - 1)
    seg_specs = [whole((1, length)), whole((length * sources, 1))]
    table_spec = pl.BlockSpec((2, entries, block, block), lambda p, info: (p, 0, 0, 0))
    lse_spec = pl.BlockSpec((1, 8, length), lambda p, info: (p, 0, 0))
    return k_blocks, entries, rows, kv_specs, seg_specs, table_spec, lse_spec


def attend(info, qkv, others, seg_q, seg_k, table, block, head_size, inner, after):
    length = qkv.shape[1]
    sources = 1 + len(others)
    width = 2 * head_size
    pairs = inner // width
    k_blocks, entries, rows, kv_specs, seg_specs, table_spec, lse_spec = attention_specs(
        sources, length, block, pairs, width
    )
    kvs = [qkv, qkv] + [kv for kv in others for _ in range(2)]
    return call(
        functools.partial(attend_kernel, sources, block, head_size),
        "attend",
        (pairs,),
        [rows(0)] + kv_specs + seg_specs + [table_spec],
        [rows(0), lse_spec],
        [
            jax.ShapeDtypeStruct((inner, length), BF16),
            jax.ShapeDtypeStruct((pairs, 8, length), F32),
        ],
        [info, qkv, *kvs, seg_q, seg_k, table],
        flops=16 * inner * length * length * sources,
        scratch=[
            pltpu.VMEM((2, k_blocks, block, block), F32),
            pltpu.VMEM((2, 1, block), F32),
            pltpu.VMEM((2, 1, block), F32),
            pltpu.VMEM((width, block), F32),
            pltpu.VMEM((length * sources, width), BF16),
        ],
        scalars=1,
        after=after,
    )


def attend_grads(
    info, qkv, others, seg_q, seg_k, table, context, lse, grad_context, block, head_size, after
):
    inner, length = context.shape
    sources = 1 + len(others)
    width = 2 * head_size
    pairs = inner // width
    k_blocks, entries, rows, kv_specs, seg_specs, table_spec, lse_spec = attention_specs(
        sources, length, block, pairs, width
    )
    dkv_spec = pl.BlockSpec((2, width, length), lambda p, info: (0, p, 0))
    tiles = (sources, 2 * (length // block) - 1)
    kvs = [qkv, qkv] + [kv for kv in others for _ in range(2)]
    results = call(
        functools.partial(grad_kernel, sources, block, head_size),
        "attend_grads",
        (pairs,),
        [rows(0)] + kv_specs + seg_specs + [table_spec, rows(0), lse_spec, rows(0)],
        [rows(0), pl.BlockSpec((2,) + tiles + (8, 2 * block), lambda p, info: (p, 0, 0, 0, 0))]
        + [dkv_spec] * sources,
        [
            jax.ShapeDtypeStruct((inner, length), BF16),
            jax.ShapeDtypeStruct((2 * pairs,) + tiles + (8, 2 * block), F32),
        ]
        + [jax.ShapeDtypeStruct((2, inner, length), BF16)] * sources,
        [info, qkv, *kvs, seg_q, seg_k, table, context, lse, grad_context],
        flops=32 * inner * length * length * sources,
        scratch=[
            pltpu.VMEM((width, length * sources), F32),
            pltpu.VMEM((width, length * sources), F32),
            pltpu.VMEM((width, block), F32),
            pltpu.VMEM((length * sources, width), BF16),
            pltpu.VMEM((length * sources, width), BF16),
            pltpu.VMEM((2,) + tiles + (block, block), F32),
        ],
        scalars=1,
        after=after,
    )
    return results[0], results[1], results[2:]


def gelu_terms(gate, upward, grad_hidden):
    square = gate * gate
    tanh = jnp.tanh(GELU_SCALE * gate * (1.0 + GELU_CUBE * square))
    half = 0.5 + 0.5 * tanh
    gelu = gate * half
    slope = half + 0.5 * gate * (1.0 - tanh * tanh) * (
        GELU_SCALE + 3.0 * GELU_CUBE * GELU_SCALE * square
    )
    return (
        (gelu * upward).astype(BF16),
        (grad_hidden * upward * slope).astype(BF16),
        (grad_hidden * gelu).astype(BF16),
    )


def joined(parts, axis):
    return parts[0] if len(parts) == 1 else jnp.concatenate(parts, axis=axis)


def source_rows(refs, kind, columns):
    return joined([ref[kind][:, columns] for ref in refs], 0)


def batches_of(sources, tile):
    if tile % LANES:
        return [[s] for s in range(sources)]
    return [list(range(s, min(s + 2, sources))) for s in range(0, sources, 2)]


def split_refs(refs, counts):
    result, start = [], 0
    for count in counts:
        result.append(refs[start : start + count])
        start += count
    return result, refs[start:]


def ffn_kernel(counts, groups, gathered, stacked, info_ref, *refs):
    if gathered:
        stacks, refs = refs[:3], refs[3:]
        blocks = stacks[0].shape[0] // len(counts)
        tile = stacks[0].shape[2]
    else:
        sources, refs = refs[: len(counts)], refs[len(counts) :]
        tile = sources[0].shape[2]
    acts_hbm, refs = refs[: 2 * groups], refs[2 * groups :]
    (hid_ref, ggi_ref, gui_ref, w_ref), refs = refs[:4], refs[4:]
    if stacked:
        grads_ref, acts, sems = refs
    else:
        grads, (acts, sems) = split_refs(refs, counts)
    first = pl.program_id(0) == 0

    def fetch(n):
        return pltpu.make_async_copy(acts_hbm[n], acts.at[n], sems.at[n])

    def places(source):
        return [
            (info_ref[1] ^ source) * blocks + block_of(info_ref[0], p, blocks // 2)
            for p in range(blocks)
        ]

    def matrix(kind, source):
        if not gathered:
            return sources[source][kind]
        rows = [stacks[kind][place].astype(F32) for place in places(source)]
        return jnp.concatenate(rows, axis=0).astype(BF16)

    @pl.when(first)
    def _():
        for g in range(groups):
            fetch(g).start()
            fetch(groups + g).start()

    start = 0
    for number, batch in enumerate(batches_of(len(counts), tile)):
        units = tile * len(batch)
        rows = slice(start, start + units)
        start += units
        for kind in range(3):
            w_ref[kind, :, rows] = joined([matrix(kind, s) for s in batch], 1)
        for g in range(groups):
            if number == 0:

                @pl.when(first)
                def _(g=g):
                    fetch(g).wait()
                    fetch(groups + g).wait()

            gate = dot_tn(w_ref[0, :, rows], acts[g])
            upward = dot_tn(w_ref[1, :, rows], acts[g])
            grad_hidden = dot_tn(w_ref[2, :, rows], acts[groups + g])
            hidden, grad_gate, grad_up = gelu_terms(gate, upward, grad_hidden)
            hid_ref[g, rows] = hidden
            ggi_ref[g, rows] = grad_gate
            gui_ref[g, rows] = grad_up
        for kind, (left, right_ref) in enumerate(((0, ggi_ref), (0, gui_ref), (groups, hid_ref))):
            total = None
            for g in range(groups):
                product = dot_nt(acts[left + g], right_ref[g, rows])
                total = product if total is None else total + product
            if not stacked:
                total = total.astype(BF16)
            for n, s in enumerate(batch):
                row = 0
                if stacked:
                    depth = grads_ref.shape[2]
                    for place in places(s):
                        part = total[row : row + depth, n * tile : (n + 1) * tile]
                        grads_ref[place, kind] = part.astype(BF16)
                        row += depth
                    continue
                for ref in grads[s]:
                    depth = ref.shape[1]
                    ref[kind] = total[row : row + depth, n * tile : (n + 1) * tile]
                    row += depth


def tile_of(width):
    return LANES if width % LANES == 0 else width


def ffn_chunk(info, weights, width, stacked, normed, cot, after):
    groups = len(normed)
    wide, length = normed[0].shape
    gathered = not isinstance(weights, list)
    sources = lax.axis_size("mp")
    tile = tile_of(width)
    steps = width // tile
    half = wide // 2
    counts = [2] + [3] * (sources - 1)
    shapes = [(3, half, width)] * 2
    for _ in range(sources - 1):
        shapes += [(3, half, width)] + [(3, half // 2, width)] * 2
    grad_specs = [pl.BlockSpec(shape[:2] + (tile,), lambda j, *_: (0, 0, j)) for shape in shapes]
    if stacked:
        shapes = [(weights.shape[0], 3, weights.shape[1], width)]
        grad_specs = [pl.BlockSpec(shapes[0][:3] + (tile,), lambda j, *_: (0, 0, 0, j))]
    if gathered:
        weight_specs = [
            pl.BlockSpec(weights.shape[:2] + (tile,), lambda j, *_, n=n: (0, 0, n * steps + j))
            for n in range(3)
        ]
        operands = [weights] * 3
    else:
        weight_specs = [pl.BlockSpec((3, wide, tile), lambda j, *_: (0, 0, j))] * sources
        operands = list(weights)
    units = sources * tile
    act_spec = pl.BlockSpec((groups, units, length), lambda j, *_: (0, j, 0))
    act_shape = jax.ShapeDtypeStruct((groups, sources * width, length), BF16)
    results = call(
        functools.partial(ffn_kernel, counts, groups, gathered, stacked),
        "ffn_chunk",
        (steps,),
        weight_specs + [pl.BlockSpec(memory_space=pl.ANY)] * (2 * groups),
        [act_spec] * 3
        + [pl.BlockSpec((3, wide, units), lambda j, *_: (0, 0, j))]
        + grad_specs,
        [act_shape] * 3
        + [jax.ShapeDtypeStruct((3, wide, sources * width), BF16)]
        + [jax.ShapeDtypeStruct(shape, BF16) for shape in shapes],
        [info, *operands, *normed, *cot],
        flops=12 * groups * length * wide * sources * width,
        scratch=[
            pltpu.VMEM((2 * groups, wide, length), BF16),
            pltpu.SemaphoreType.DMA((2 * groups,)),
        ],
        scalars=1,
        after=after,
    )
    grads = results[4] if stacked else split_refs(results[4:], counts)[0]
    return results[:3], results[3], grads


def down_kernel(chunks, kinds, with_prior, *refs):
    total = None
    if with_prior:
        total, refs = refs[0][0].astype(F32), refs[1:]
    for _ in range(chunks):
        matrices, acts, refs = refs[:kinds], refs[kinds : 2 * kinds], refs[2 * kinds :]
        for matrix, act in zip(matrices, acts):
            product = dot_nn(matrix[0], act[0])
            total = product if total is None else total + product
    (out_ref,) = refs
    out_ref[0] = total.astype(BF16)


def down(chunk_weights, chunk_acts, first, kinds, start, count, after, prior=None):
    length = chunk_acts[0][0].shape[2]
    wide = chunk_weights[0].shape[1]
    operands, specs = [], []
    if prior is not None:
        operands.append(prior)
        specs.append(pl.BlockSpec((1, wide, length), lambda g: (start + g, 0, 0)))
    flops = 0
    for weights, acts in zip(chunk_weights, chunk_acts):
        acts = acts[1:] if kinds == 2 else acts[:1]
        operands += [weights] * kinds + list(acts)
        specs += [
            pl.BlockSpec(
                (1,) + weights.shape[1:], lambda g, n=n: (n, 0, 0), pipeline_mode=pl.Buffered(1)
            )
            for n in range(first, first + kinds)
        ]
        specs += [
            pl.BlockSpec((1, act.shape[1], length), lambda g: (start + g, 0, 0)) for act in acts
        ]
        flops += 2 * kinds * count * length * wide * acts[0].shape[1]
    return call(
        functools.partial(down_kernel, len(chunk_acts), kinds, prior is not None),
        "down",
        (count,),
        specs,
        [slab(wide, length)],
        [jax.ShapeDtypeStruct((count, wide, length), BF16)],
        operands,
        flops=flops,
        after=after,
    )[0]


def body(
    inputs,
    cotangent,
    segments,
    rel_bucket,
    head_order,
    rel_table,
    norm1_gain,
    norm2_gain,
    w_query,
    w_key,
    w_value,
    output_weight,
    w_gate,
    w_up,
    w_down,
):
    dp, mp = dp_size(), lax.axis_size("mp")
    x = lax.axis_index("mp")
    core, chip = lax.axis_index("core"), lax.axis_index("chip")
    chips, depth = dp // 2, dp // 4
    micro, rows, own_length, model = inputs.shape
    groups = micro * rows
    length = own_length * mp
    bucket_count, head_count = rel_table.shape
    inner = w_query.shape[1]
    head_size = inner // head_count
    block = min(256, own_length)
    q_blocks, k_blocks = own_length // block, length // block
    own_rows, own_units = w_gate.shape
    half_units = own_units // 2
    chip_rows = 2 * own_rows
    place = chip.reshape(1).astype(jnp.int32)

    micros = range(groups)
    own_place = (2 * x + core).reshape(1).astype(jnp.int32)
    role_place = own_place & 3

    def feature_major(array):
        return jnp.transpose(array.reshape(groups, own_length, model), (0, 2, 1))

    bucket_rev = jnp.concatenate([rel_bucket[::-1], jnp.full((1,), -1, jnp.int32)])
    bucket_hot = (bucket_rev[:, None] == jnp.arange(bucket_count, dtype=jnp.int32)[None, :]).astype(F32)
    head_hot = (head_order[:, None] == jnp.arange(head_count, dtype=jnp.int32)[None, :]).astype(F32)
    offset_table = jnp.dot(bucket_hot, rel_table, precision=TOP_PRECISION)
    offset_bias = jnp.dot(head_hot, offset_table.T, precision=TOP_PRECISION)
    bias_blocks = offset_bias.reshape(head_count, 2 * k_blocks, block)
    windows = jnp.concatenate([bias_blocks[:, :-1], bias_blocks[:, 1:]], axis=2)

    part = 4 * inner // (2 * mp)
    shard = jnp.concatenate([w_query, w_key, w_value, jnp.transpose(output_weight)], axis=1)
    kept = lax.dynamic_slice_in_dim(shard, (2 * x + core) * part, part, 1)
    sent = lax.dynamic_slice_in_dim(shard, (2 * x + 1 - core) * part, part, 1)
    got = swap_dp(sent, 1)
    attention_piece = either(
        core, jnp.concatenate([kept, got], axis=0), jnp.concatenate([got, kept], axis=0)
    )[None]
    ffn_shard = jnp.stack([w_gate, w_up, jnp.transpose(w_down)])
    low_half, high_half = ffn_shard[:, :, :half_units], ffn_shard[:, :, half_units:]
    kept = either(core, low_half, high_half)
    got = swap_dp(either(core, high_half, low_half), 1)
    ffn_piece = either(
        core, jnp.concatenate([kept, got], axis=1), jnp.concatenate([got, kept], axis=1)
    )
    if half_units % (7 * LANES) == 0:
        bounds = [0, half_units // 7 * FIRST_SEVENTHS, half_units]
    elif half_units > LANES:
        bounds = [0, LANES, half_units]
    else:
        bounds = [0, half_units]
    widths = [b - a for a, b in zip(bounds[:-1], bounds[1:])]
    chunk_stacks = []
    for a, width in zip(bounds, widths):
        flat = jnp.concatenate([ffn_piece[n, :, a : a + width] for n in range(3)], axis=1)
        chunk_stacks.append(lax.all_gather(flat, ("mp", "chip")))

    far_masks = z_masks()

    def gather_z(piece, masks, first=(), then=()):
        for mask in masks:
            piece = merge(piece, hold(swap_dp(hold(piece, *first), mask), *then))
        return piece

    own = gather_z(attention_piece, far_masks)
    arrays = feature_major(inputs)
    layer_in = [reorder(arrays, m, place, chips, False) for m in micros]
    arrays = feature_major(cotangent)
    cots = [reorder(arrays, m, place, chips, False, [*layer_in, own]) for m in micros]
    cots_far = [swap_dp(cot, 1) for cot in cots]
    table = bias_table(windows[:, :, None, :], block, cots)
    over_y, over_x = gather_xy(own, layer_in, [table])
    corner = gather_corner(over_y, over_x)
    quads = quads_of(own, over_y, over_x, corner)
    matrices = []
    for parts in quads:
        matrices += [parts, tuple(swap_dp(ref, 1) for ref in parts)]

    seg_flat = segments.reshape(groups, length)
    seg_q = lax.dynamic_slice_in_dim(seg_flat, x * own_length, own_length, 1)
    seg_parts = seg_flat.reshape(groups, mp, own_length)
    seg_k = jnp.concatenate([pick(seg_parts, x ^ k, 1) for k in range(mp)], axis=1)
    q_edges = seg_q.reshape(groups, q_blocks, block)
    k_edges = seg_k.reshape(groups, k_blocks, block)
    live = (q_edges[:, :, None, 0] <= k_edges[:, None, :, -1]) & (
        k_edges[:, None, :, 0] <= q_edges[:, :, None, -1]
    )
    infos = [
        jnp.concatenate([x.reshape(1).astype(jnp.int32), live[m].reshape(-1).astype(jnp.int32)])
        for m in micros
    ]
    seg_q_rows = [seg_q[m][None, :] for m in micros]
    seg_k_columns = [seg_k[m][:, None] for m in micros]

    gains = reorder(jnp.stack([norm1_gain, norm2_gain], axis=1)[None], 0, place, chips, False)
    gain1, gain2 = gains[:, :1], gains[:, 1:]
    normed1, qkvs, others = [], [], []
    last = cots_far
    for m in micros:
        normed, qkv, kv = project(own_place, layer_in[m], gain1, matrices, last)
        last = [normed]
        normed1.append(normed)
        qkvs.append(qkv.reshape(4 * inner, own_length))
        others.append([swap_mp(kv, k).reshape(2 * inner, own_length) for k in x_masks()])
    weights = assemble(own_place, matrices, inner, [normed1[-1]])
    last = [weights]
    contexts, lses, normed2, normed2_far = [], [], [], []
    for m in micros:
        context, lse = attend(
            infos[m], qkvs[m], others[m], seg_q_rows[m], seg_k_columns[m], table,
            block, head_size, inner, last,
        )
        contexts.append(context)
        lses.append(lse)
        last = [context]
        normed = middle_layer(layer_in[m], context, weights, gain2, last)
        last = [normed]
        normed2.append(normed)
        normed2_far.append(swap_dp(normed, 1))

    ffn_info = jnp.concatenate([place, x.reshape(1).astype(jnp.int32)])
    chunk_acts, chunk_weights, chunk_grads = [], [], []
    prior = prior_ffn = None
    sums = []
    for stack, width in zip(chunk_stacks, widths):
        stacked = len(chunk_acts) + 1 < len(widths)
        if own_rows % 4 or width % LANES:
            ordered = jnp.stack(
                [
                    jnp.stack([pick(stack, (x ^ k) * chips + block_of(chip, p, depth), 0) for p in range(chips)])
                    for k in range(mp)
                ]
            ).reshape(mp, model, 3, width)
            stack = [jnp.transpose(ordered[k], (1, 0, 2)) for k in range(mp)]
            stacked = False
        acts, matrices_in, grads = ffn_chunk(
            ffn_info, stack, width, stacked, normed2 + normed2_far, cots + cots_far, last
        )
        last = [acts[0]]
        chunk_acts.append(acts)
        chunk_weights.append(matrices_in)
        if stacked:
            sums.append(lax.psum_scatter(grads, ("mp", "chip"), scatter_dimension=0))
        else:
            chunk_grads.append(grads)
        if len(chunk_acts) < len(widths):
            prior = down(chunk_weights, chunk_acts, 0, 2, 0, 2 * groups, last)
            prior_ffn = down(chunk_weights, chunk_acts, 2, 1, 0, 2 * groups, [prior])
            last = [prior_ffn]
    back = functools.partial(down, chunk_weights[-1:], chunk_acts[-1:], 0, 2)
    back_far = back(groups, groups, last, prior)
    from_far = swap_dp(back_far, 1)
    back_own = back(0, groups, [back_far], prior)
    last = [back_own]

    z_count = len(far_masks)
    grad_attn, grad_q, grad_kv, bias_grads, gain2_grads = [], [], [], [], []
    for m in micros:
        low, grad_context, gain_grads = turn(
            m, layer_in[m], contexts[m], cots[m], (back_own, from_far), gain2, weights, last
        )
        last = [low]
        grad_attn.append(low)
        gain2_grads.append(gain_grads)
        dq, bias_grad, dkv = attend_grads(
            infos[m], qkvs[m], others[m], seg_q_rows[m], seg_k_columns[m], table,
            contexts[m], lses[m], grad_context, block, head_size, last,
        )
        last = [dq]
        if m == micros[0]:
            moving = [scatter_corner(grads, [], last) for grads in chunk_grads]
            last += [parts[1] for parts in moving]
        grad_q.append(dq)
        bias_grads.append(bias_grad)
        grad_kv.append((dkv[0], [swap_mp(dkv[k], k) for k in x_masks()]))
    moving = [scatter_xy(*parts, last) for parts in moving]
    grad_kv[0] = sum_rows([grad_kv[0][0], *hold(grad_kv[0][1], dq)], 1, after=[dq])
    weight_grads = outer_products(
        role_place,
        (0, 3),
        [
            [(normed1[m], grad_q[m]) for m in micros],
            [(grad_attn[m], contexts[m]) for m in micros],
        ],
        None,
        [dq, grad_kv[0]] + [first_of(parts) for parts in moving],
    )
    ffn = functools.partial(down, chunk_weights[-1:], chunk_acts[-1:], 2, 1)
    ffn_far = ffn(groups, groups, [weight_grads], prior_ffn)
    ffn_from = swap_dp(ffn_far, 1)
    grad_kv[1:] = [
        sum_rows([own, *hold(got, ffn_far)], 1, after=[ffn_far]) for own, got in grad_kv[1:]
    ]
    ffn_own = ffn(0, groups, [ffn_far, *grad_kv[1:]], prior_ffn)
    moving = [scatter_z(parts, 0, [ffn_own]) for parts in moving]
    weight_grads = outer_products(
        role_place,
        (1, 2),
        [[(normed1[m], (grad_kv[m], n)) for m in micros] for n in range(2)],
        weight_grads,
        [ffn_own] + [first_of(parts) for parts in moving],
    )

    half = model // 2
    split = [half, half // 2, half // 2]
    if part == inner:
        got = [swap_dp(weight_grads[2 * k + 1 : 2 * k + 2], 1) for k in range(mp)]
        quads = [
            sum_rows([weight_grads, got[k]], 2 if k == 0 else split, [2 * k, 0], 1)
            for k in range(mp)
        ]
    else:
        ordered = jnp.concatenate(
            [lax.dynamic_slice_in_dim(weight_grads, role_place[0] ^ r, 1, 0) for r in range(4)]
        )
        by_part = jnp.transpose(
            ordered.reshape(4, model, inner // part, part), (0, 2, 1, 3)
        ).reshape(mp, 2, model, part)
        near = add_low(pick(by_part, core, 1), swap_dp(pick(by_part, 1 - core, 1), 1))
        quads = []
        for k in range(mp):
            matrix = pick(near, x ^ k, 0)[None]
            sizes = [half, half] if k == 0 else split
            starts = [sum(sizes[:n]) for n in range(len(sizes))]
            quads.append(tuple(matrix[:, a : a + n] for a, n in zip(starts, sizes)))
    grad_inputs, gain1_grads = input_grads(
        place,
        [(layer_in[m], grad_attn[m], grad_q[m], grad_kv[m]) for m in micros],
        gain1,
        weights,
        chips,
        [weight_grads, quads[0][0]],
    )
    last = [gain1_grads]
    corner = scatter_corner(quads, [], last)
    sums += [scatter_z(parts, 1, last) for parts in moving]
    traded = [trade_rows(part, core, own_rows) for part in sums] if z_count == 2 else []

    bias_rows = sum(bias_grads)
    bias_tiles = sum(
        jnp.pad(bias_rows[:, :, :, t, : 2 * block - 7 + t], ((0, 0),) * 3 + ((7 - t, 0),))
        for t in range(8)
    )
    run = 2 * q_blocks - 1
    bias_flat = jnp.zeros((head_count, 2 * k_blocks - 1, 2 * block), F32)
    for k in range(mp):
        first = k_blocks - q_blocks - ((x ^ k) - x) * q_blocks
        held = lax.dynamic_slice_in_dim(bias_flat, first, run, 1)
        bias_flat = lax.dynamic_update_slice_in_dim(bias_flat, held + bias_tiles[:, k], first, 1)
    left = jnp.pad(bias_flat[:, :, :block], ((0, 0), (0, 1), (0, 0)))
    right = jnp.pad(bias_flat[:, :, block:], ((0, 0), (1, 0), (0, 0)))
    offsets_total = (left + right).reshape(head_count, 2 * k_blocks * block)
    bucket_part = jnp.dot(bucket_hot.T, offsets_total.T, precision=TOP_PRECISION)
    rel_part = jnp.dot(bucket_part, head_hot, precision=TOP_PRECISION)
    gain_parts = jnp.concatenate([gain1_grads, sum(gain2_grads)], axis=1)
    gain_parts = reorder(hold(gain_parts, corner[1])[None], 0, place, chips, True)
    small = jnp.concatenate([gain_parts[:, 0], gain_parts[:, 1], rel_part.reshape(-1)])

    small = small + swap_dp(small, 1)
    steps = [(swap_mp, mask) for mask in doubling(mp)]
    steps += [(swap_dp, mask) for mask in doubling(dp) if mask > 1]
    outputs = finish(
        place,
        [(layer_in[m], contexts[m]) for m in micros],
        (ffn_own, ffn_from),
        weights,
        chips,
        [corner[1], first_of(sums[-1])] + [got for _, got in traded[:-1]],
    )
    own, to_y, to_x = corner
    got = [swap_dp(to_y, 2)] + [swap_mp(other, k) for k, other in zip(x_masks(), to_x)]
    total = sum_rows([own, *hold(got, outputs)], 2, after=[outputs])
    for stage, mask in enumerate(reversed(far_masks)):
        got, small = beside(swap_dp(total[1], mask), small, steps)
        total = sum_rows([total[0], got], 1 if stage == z_count - 1 else 2)
    for stage in range(2, z_count):
        sums = [scatter_z(parts, stage) for parts in sums]
    piece = total[0]
    got, small = beside([swap_mp(piece, k) for k in x_masks()], small, steps)
    over_x = jnp.stack([piece] + got)
    kept = either(core, over_x[:, :own_rows], over_x[:, own_rows:])
    got = swap_dp(either(core, over_x[:, own_rows:], over_x[:, :own_rows]), 1)
    got, small = beside(got, small, steps)
    while steps:
        got, small = beside(got, small, steps)
    both = jnp.stack([kept, got], axis=1).reshape(2 * mp, own_rows, part)
    final = jnp.concatenate(
        [pick(both, (2 * x + core) ^ r, 0) for r in range(2 * mp)], axis=1
    ).astype(F32)

    traded = traded or [trade_rows(part, core, own_rows) for part in sums]
    kept, got = [part for part, _ in traded], [part for _, part in traded]
    ffn_grads = either(
        core, jnp.concatenate(kept + got, axis=2), jnp.concatenate(got + kept, axis=2)
    ).astype(F32)

    shape = inputs.shape

    def placed(array):
        return jnp.transpose(array, (0, 2, 1)).reshape(shape)

    return (
        placed(outputs),
        placed(grad_inputs),
        small[2 * model :].reshape(rel_table.shape),
        small[:model],
        small[model : 2 * model],
        final[:, :inner],
        final[:, inner : 2 * inner],
        final[:, 2 * inner : 3 * inner],
        jnp.transpose(final[:, 3 * inner :]),
        ffn_grads[0],
        ffn_grads[1],
        jnp.transpose(ffn_grads[2]),
    )


def solution(mesh):
    devices = mesh.devices.reshape(-1, 2, mesh.shape["mp"])
    return jax.shard_map(
        body,
        mesh=jax.sharding.Mesh(devices, DP + ("mp",)),
        in_specs=(
            P(None, DP, "mp", None),
            P(None, DP, "mp", None),
            P(None, DP, None),
            P(),
            P(),
            P(),
            P(),
            P(),
            P(DP, None),
            P(DP, None),
            P(DP, None),
            P(None, DP),
            P(DP, "mp"),
            P(DP, "mp"),
            P("mp", DP),
        ),
        out_specs=(
            P(None, DP, "mp", None),
            P(None, DP, "mp", None),
            P(),
            P(),
            P(),
            P(DP, None),
            P(DP, None),
            P(DP, None),
            P(None, DP),
            P(DP, "mp"),
            P(DP, "mp"),
            P("mp", DP),
        ),
        check_vma=False,
    )
```

```python
import functools

import jax
import jax.numpy as jnp
from jax import lax
from jax.experimental import pallas as pl
from jax.experimental.pallas import tpu as pltpu
from jax.sharding import PartitionSpec as P

EPSILON = 1e-06
TOP_PRECISION = lax.Precision.HIGHEST
GELU_SCALE = 0.7978845608028654
GELU_CUBE = 0.044715
BF16 = jnp.bfloat16
F32 = jnp.float32
NEGATIVE = -1e30
VMEM_BYTES = 60 * 1024 * 1024
LANES = 128
COST_SHARE = 1.0
FIRST_SEVENTHS = 4


DP = ("chip", "core")


def dp_size():
    return lax.axis_size("chip") * lax.axis_size("core")


def swap_dp(array, mask):
    return lax.ppermute(array, DP, [(i, i ^ mask) for i in range(dp_size())])


def swap_mp(array, mask):
    count = lax.axis_size("mp")
    return lax.ppermute(array, "mp", [(i, i ^ mask) for i in range(count)])


def pick(array, index, axis):
    return lax.dynamic_index_in_dim(array, index, axis, keepdims=False)


def add_low(*terms):
    total = terms[0].astype(F32)
    for term in terms[1:]:
        total = total + term.astype(F32)
    return total.astype(BF16)


def trade_rows(array, core, rows):
    low, high = array[:, :rows], array[:, rows:]
    return either(core, low, high), swap_dp(either(core, high, low), 1)


def first_of(parts):
    return parts[0] if isinstance(parts, tuple) else parts


def either(flag, first, second):
    return jnp.where(flag == 0, first, second)


def hold(value, *tokens):
    return lax.optimization_barrier((value, *tokens))[0] if tokens else value


def z_masks():
    masks, mask = [], dp_size() // 2
    while mask > 2:
        masks.append(mask)
        mask //= 2
    return masks


def x_masks():
    return range(1, lax.axis_size("mp"))


def merged(parts):
    kinds, rows, columns = parts[0].shape
    return jnp.stack(parts, axis=1).reshape(kinds, len(parts) * rows, columns)


def gather_xy(own, first=(), then=()):
    own = hold(own, *first)
    return hold((swap_dp(own, 2), [swap_mp(own, k) for k in x_masks()]), *then)


def gather_corner(over_y, over_x, first=(), then=()):
    half = over_y.shape[1] // 2
    low = hold(rows_of(over_y, 0, half), *first)
    result = []
    for k, other in zip(x_masks(), over_x):
        high = hold(rows_of(other, half, half), *first)
        result.append((swap_mp(low, k), swap_dp(high, 2)))
    return hold(result, *then)


def quads_of(own, over_y, over_x, corner):
    return [(own, over_y)] + [(other, *parts) for other, parts in zip(over_x, corner)]


def scatter_corner(quads, first=(), then=()):
    own, to_y = quads[0]
    got = []
    for k, (_, low, high) in zip(x_masks(), quads[1:]):
        got.append((swap_mp(hold(low, *first), k), swap_dp(hold(high, *first), 2)))
    got = hold(got, *then)
    if len(got) == 1:
        to_y, to_x = add_corner(to_y, got[0][0], quads[1][0], got[0][1], then)
        return own, to_y, [to_x]
    half = own.shape[1] // 2
    low = add_low(to_y[:, :half], *[part for part, _ in got])
    to_x = [
        jnp.concatenate([parts[0][:, :half], add_low(parts[0][:, half:], part)], axis=1)
        for parts, (_, part) in zip(quads[1:], got)
    ]
    return own, jnp.concatenate([low, to_y[:, half:]], axis=1), to_x


def scatter_xy(own, to_y, to_x, then=()):
    got = [swap_dp(to_y, 2)] + [swap_mp(other, k) for k, other in zip(x_masks(), to_x)]
    return sum_rows([own, *hold(got, *then)], 2, after=then)


def scatter_z(pair, stage, then=()):
    masks = z_masks()
    mask = masks[len(masks) - 1 - stage]
    got = hold(swap_dp(pair[1], mask), *then)
    return sum_rows([pair[0], got], 1 if stage == len(masks) - 1 else 2, after=then)


def doubling(count):
    masks, mask = [], 1
    while mask < count:
        masks.append(mask)
        mask *= 2
    return masks


def beside(got, values, steps):
    if not steps:
        return got, values
    swap, mask = steps.pop(0)
    got, other = lax.optimization_barrier((got, swap(values, mask)))
    return got, values + other


def call(
    kernel, name, grid, in_specs, out_specs, out_shape, operands, flops=0, scratch=(), scalars=0, after=(),
    aliases=None,
):
    moved = sum(a.size * a.dtype.itemsize for a in operands)
    moved += sum(s.size * s.dtype.itemsize for s in out_shape)
    count = len(operands)

    def run(*refs):
        kernel(*refs[:count], *refs[count + len(after) :])

    return pl.pallas_call(
        run,
        grid_spec=pltpu.PrefetchScalarGridSpec(
            num_scalar_prefetch=scalars,
            grid=grid,
            in_specs=list(in_specs) + [pl.BlockSpec(memory_space=pl.ANY)] * len(after),
            out_specs=out_specs,
            scratch_shapes=list(scratch),
        ),
        out_shape=out_shape,
        input_output_aliases=aliases or {},
        compiler_params=pltpu.CompilerParams(vmem_limit_bytes=VMEM_BYTES),
        cost_estimate=pl.CostEstimate(
            flops=int(flops * COST_SHARE),
            bytes_accessed=int(moved * COST_SHARE),
            transcendentals=0,
        ),
        name=name,
    )(*operands, *after)


def whole(shape):
    return pl.BlockSpec(shape, lambda *_: (0,) * len(shape), pipeline_mode=pl.Buffered(1))


def slab(*shape):
    return pl.BlockSpec((1,) + shape, lambda m, *_: (m,) + (0,) * len(shape))


def columns(wide, step):
    return pl.BlockSpec((wide, step), lambda j, *_: (0, j))


def lane_step(length):
    return 256 if length % 256 == 0 else length


def dot_nn(left, right):
    return lax.dot_general(left, right, (((1,), (0,)), ((), ())), preferred_element_type=F32)


def dot_tn(left, right):
    return lax.dot_general(left, right, (((0,), (0,)), ((), ())), preferred_element_type=F32)


def dot_nt(left, right):
    return lax.dot_general(left, right, (((1,), (1,)), ((), ())), preferred_element_type=F32)


def transposed(value):
    return jnp.transpose(value.astype(F32), (1, 0)).astype(BF16)


def block_of(place, position, depth):
    z, y = place // 2, place % 2
    masks, left, mask = 0, position % depth, depth
    while mask > 1:
        mask //= 2
        masks += mask * (left % 2)
        left //= 2
    return (z ^ masks) * 2 + (y ^ (position // depth))


def reorder_kernel(outward, info_ref, in_ref, out_ref):
    blocks = out_ref.shape[0]
    for p in range(blocks):
        chip = block_of(info_ref[0], p, blocks // 2)
        if outward:
            out_ref[chip] = in_ref[0, p]
        else:
            out_ref[p] = in_ref[0, chip]


def reorder(array, group, place, blocks, outward, after=()):
    groups, wide, length = array.shape
    split = array.reshape(groups, blocks, wide // blocks, length)
    return call(
        functools.partial(reorder_kernel, outward),
        "reorder",
        (1,),
        [pl.BlockSpec((1,) + split.shape[1:], lambda *_: (group, 0, 0, 0))],
        [pl.BlockSpec(split.shape[1:], lambda *_: (0, 0, 0))],
        [jax.ShapeDtypeStruct(split.shape[1:], array.dtype)],
        [place, split],
        scalars=1,
        after=after,
    )[0].reshape(wide, length)


def bias_kernel(window_ref, table_ref):
    count, block = table_ref.shape[1], table_ref.shape[-1]
    for entry in range(count):
        wide = jnp.broadcast_to(window_ref[0, entry], (block, 2 * block))
        rolled = pltpu.roll(wide, block + 1, 1, stride=1, stride_axis=0)
        table_ref[0, entry] = rolled[:, :block]


def bias_table(windows, block, after):
    heads, count = windows.shape[:2]
    return call(
        bias_kernel,
        "bias_table",
        (heads,),
        [slab(count, 1, 2 * block)],
        [slab(count, block, block)],
        [jax.ShapeDtypeStruct((heads, count, block, block), F32)],
        [windows],
        after=after,
    )[0]


def project_kernel(counts, limit, info_ref, x_ref, gain_ref, *refs):
    matrices, (normed_ref, out_ref, kv_ref) = split_refs(refs, counts)
    first = kv_ref.shape[0] // 2
    values = x_ref[...].astype(F32)
    factor = lax.rsqrt(jnp.mean(values * values, axis=0, keepdims=True) + EPSILON)
    normed = (values * factor * gain_ref[...]).astype(BF16)
    normed_ref[...] = normed
    for r, parts in enumerate(matrices):
        place = info_ref[0] ^ r

        @pl.when(place < limit)
        def _(parts=parts, place=place):
            weights = joined([ref[0] for ref in parts], 0)
            product = dot_tn(weights, normed).astype(BF16)
            out_ref[place] = product

            @pl.when(place >= first)
            def _():
                kv_ref[place - first] = product


def project(place, x, gain, matrices, after):
    wide, length = x.shape
    part = matrices[0][0].shape[2]
    limit = len(matrices) * 3 // 4
    step = lane_step(length)
    counts = [len(parts) for parts in matrices]
    flat = [ref for parts in matrices for ref in parts]
    return call(
        functools.partial(project_kernel, counts, limit),
        "project",
        (length // step,),
        [columns(wide, step), whole((wide, 1))] + [whole(ref.shape) for ref in flat],
        [
            columns(wide, step),
            pl.BlockSpec((len(matrices), part, step), lambda j, *_: (0, 0, j)),
            pl.BlockSpec((len(matrices) // 2, part, step), lambda j, *_: (0, 0, j)),
        ],
        [
            jax.ShapeDtypeStruct((wide, length), BF16),
            jax.ShapeDtypeStruct((len(matrices), part, length), BF16),
            jax.ShapeDtypeStruct((len(matrices) // 2, part, length), BF16),
        ],
        [place, x, gain, *flat],
        flops=2 * wide * length * limit * part,
        scalars=1,
        after=after,
    )


def assemble_kernel(counts, info_ref, *refs):
    matrices, (out_ref,) = split_refs(refs, counts)
    for r, parts in enumerate(matrices):
        place, row = info_ref[0] ^ r, 0
        for ref in parts:
            rows = ref.shape[1]
            out_ref[place, row : row + rows] = ref[0]
            row += rows


def assemble(place, matrices, inner, after):
    part = matrices[0][0].shape[2]
    counts = [len(parts) for parts in matrices]
    flat = [ref for parts in matrices for ref in parts]
    wide = sum(ref.shape[1] for ref in matrices[0])
    shape = (len(matrices), wide, part)
    ordered = call(
        functools.partial(assemble_kernel, counts),
        "assemble",
        (1,),
        [whole(ref.shape) for ref in flat],
        [pl.BlockSpec(shape, lambda *_: (0, 0, 0))],
        [jax.ShapeDtypeStruct(shape, BF16)],
        [place, *flat],
        scalars=1,
        after=after,
    )[0]
    return jnp.transpose(ordered.reshape(4, inner // part, wide, part), (0, 2, 1, 3)).reshape(
        4, wide, inner
    )


def middle_kernel(x_ref, context_ref, w_ref, gain_ref, normed_ref):
    values = x_ref[...].astype(F32) + dot_nn(w_ref[0], context_ref[...])
    factor = lax.rsqrt(jnp.mean(values * values, axis=0, keepdims=True) + EPSILON)
    normed_ref[...] = (values * factor * gain_ref[...]).astype(BF16)


def out_weights(weights):
    return pl.BlockSpec(
        (1,) + weights.shape[1:], lambda *_: (3, 0, 0), pipeline_mode=pl.Buffered(1)
    )


def middle_layer(x, context, weights, gain, after):
    wide, length = x.shape
    inner = weights.shape[2]
    step = lane_step(length)
    return call(
        middle_kernel,
        "middle",
        (length // step,),
        [columns(wide, step), columns(inner, step), out_weights(weights), whole((wide, 1))],
        [columns(wide, step)],
        [jax.ShapeDtypeStruct((wide, length), BF16)],
        [x, context, weights, gain],
        flops=2 * wide * length * inner,
        after=after,
    )[0]


def lifted_grads(values, gain, grad):
    factor = lax.rsqrt(jnp.mean(values * values, axis=0, keepdims=True) + EPSILON)
    scaled = values * factor
    lifted = grad * gain
    inner = jnp.mean(lifted * scaled, axis=0, keepdims=True)
    return factor * (lifted - scaled * inner), jnp.sum(grad * scaled, axis=1, keepdims=True)


def add_up(ref, value):
    first = pl.program_id(0) == 0

    @pl.when(first)
    def _():
        ref[...] = value

    @pl.when(jnp.logical_not(first))
    def _():
        ref[...] += value


def turn_kernel(
    x_ref, context_ref, cot_ref, back0_ref, back1_ref, gain_ref, w_ref, low_ref, grad_ref, gain_grad_ref
):
    middle = x_ref[...].astype(F32) + dot_nn(w_ref[0], context_ref[...])
    grad = back0_ref[0].astype(F32) + back1_ref[0].astype(F32)
    normed_grad, gain_grad = lifted_grads(middle, gain_ref[...], grad)
    add_up(gain_grad_ref, gain_grad)
    low = (cot_ref[...].astype(F32) + normed_grad).astype(BF16)
    low_ref[...] = low
    grad_ref[...] = dot_tn(w_ref[0], low).astype(BF16)


def turn(group, x, context, cot, back, gain, weights, after):
    wide, length = x.shape
    inner = weights.shape[2]
    step = lane_step(length)
    big = columns(wide, step)
    part = pl.BlockSpec((1, wide, step), lambda j, *_: (group, 0, j))
    return call(
        turn_kernel,
        "turn",
        (length // step,),
        [big, columns(inner, step), big, part, part, whole((wide, 1)), out_weights(weights)],
        [big, columns(inner, step), pl.BlockSpec((wide, 1), lambda *_: (0, 0))],
        [
            jax.ShapeDtypeStruct((wide, length), BF16),
            jax.ShapeDtypeStruct((inner, length), BF16),
            jax.ShapeDtypeStruct((wide, 1), F32),
        ],
        [x, context, cot, *back, gain, weights],
        flops=4 * wide * length * inner,
        after=after,
    )


def put_blocks(info_ref, out_ref, values):
    if len(out_ref.shape) == 3:
        out_ref[0] = values.astype(out_ref.dtype)
        return
    blocks, rows = out_ref.shape[1:3]
    for p in range(blocks):
        chip = block_of(info_ref[0], p, blocks // 2)
        out_ref[0, chip] = values[p * rows : (p + 1) * rows].astype(out_ref.dtype)


def outward_spec(groups, wide, length, blocks, step):
    rows, steps = wide // blocks, length // step
    if rows % 8:
        spec = pl.BlockSpec((1, wide, step), lambda j, *_: (j // steps, 0, j % steps))
        return spec, jax.ShapeDtypeStruct((groups, wide, length), BF16)
    return (
        pl.BlockSpec((1, blocks, rows, step), lambda j, *_: (j // steps, 0, 0, j % steps)),
        jax.ShapeDtypeStruct((groups, blocks, rows, length), BF16),
    )


def outward(array, place, blocks):
    if array.ndim == 4:
        return array.reshape(array.shape[0], -1, array.shape[3])
    return jnp.stack([reorder(array, m, place, blocks, True) for m in range(array.shape[0])])


def group_columns(group, steps, *shape):
    def index(j, *_):
        return (0,) * (len(shape) - 1) + (jnp.clip(j - group * steps, 0, steps - 1),)

    return pl.BlockSpec(shape, index)


def in_groups(kernel, counts, steps, *refs):
    lead, each, groups = counts
    group = pl.program_id(0) // steps
    shared, rest = refs[:lead], refs[lead:]
    parts, tail = rest[: each * groups], rest[each * groups :]
    for m in range(groups):

        @pl.when(group == m)
        def _(m=m):
            kernel(*shared, *parts[each * m : each * (m + 1)], *tail)


def finish_kernel(info_ref, x_ref, context_ref, ffn0_ref, ffn1_ref, w_ref, out_ref):
    middle = x_ref[...].astype(F32) + dot_nn(w_ref[0], context_ref[...])
    total = middle + (ffn0_ref[0].astype(F32) + ffn1_ref[0].astype(F32))
    put_blocks(info_ref, out_ref, total)


def finish(place, terms, ffn, weights, blocks, after):
    wide, length = terms[0][0].shape
    inner = weights.shape[2]
    step = lane_step(length)
    groups, steps = len(terms), length // step
    spec, shape = outward_spec(groups, wide, length, blocks, step)
    specs = []
    for m in range(groups):
        specs += [group_columns(m, steps, wide, step), group_columns(m, steps, inner, step)]
    part = pl.BlockSpec((1, wide, step), lambda j, *_: (j // steps, 0, j % steps))
    result = call(
        functools.partial(in_groups, finish_kernel, (1, 2, groups), steps),
        "finish",
        (groups * steps,),
        specs + [part, part, out_weights(weights)],
        [spec],
        [shape],
        [place, *[array for term in terms for array in term], *ffn, weights],
        flops=2 * groups * wide * length * inner,
        scalars=1,
        after=after,
    )[0]
    return outward(result, place, blocks)


def outer_kernel(count, info_ref, *refs):
    out_ref = refs[-1]
    step = pl.program_id(0)
    for r in range(len(refs) // (2 * count)):
        pairs = refs[2 * count * r : 2 * count * (r + 1)]

        @pl.when(step == r)
        def _(pairs=pairs):
            total = dot_nt(pairs[0][...], matrix_of(pairs[1]))
            for m in range(1, count):
                total = total + dot_nt(pairs[2 * m][...], matrix_of(pairs[2 * m + 1]))
            out_ref[0] = total.astype(BF16)


def matrix_of(ref):
    return ref[0] if len(ref.shape) == 3 else ref[...]


def outer_products(place, roles, matrices, into, after):
    count = len(matrices[0])
    wide, length = matrices[0][0][0].shape
    low, high = roles
    operands, specs = [], []
    for left, right in [pair for pairs in matrices for pair in pairs]:
        right, number = right if isinstance(right, tuple) else (right, None)
        inner = right.shape[-2]
        operands += [left, right]
        specs.append(whole(left.shape))
        if number is None:
            specs.append(whole(right.shape))
        else:
            specs.append(
                pl.BlockSpec(
                    (1, inner, length),
                    lambda *_, n=number: (n, 0, 0),
                    pipeline_mode=pl.Buffered(1),
                )
            )

    def index(step, info):
        return (jnp.where(step == 0, low, high) ^ info[0], 0, 0)

    if into is not None:
        operands.append(into)
        specs.append(pl.BlockSpec(memory_space=pl.ANY))

    def kernel(info_ref, *refs):
        if into is not None:
            refs = refs[:-2] + refs[-1:]
        outer_kernel(count, info_ref, *refs)

    return call(
        kernel,
        "outer_products",
        (len(matrices),),
        specs,
        [pl.BlockSpec((1, wide, inner), index)],
        [jax.ShapeDtypeStruct((4, wide, inner), BF16)],
        [place, *operands],
        flops=2 * wide * inner * length * count * len(matrices),
        scalars=1,
        after=after,
        aliases=None if into is None else {len(operands): 0},
    )[0]


def input_kernel(info_ref, x_ref, low_ref, dq_ref, dkv_ref, gain_ref, w_ref, out_ref, gain_grad_ref):
    grad = (
        dot_nn(w_ref[0], dq_ref[...]) + dot_nn(w_ref[1], dkv_ref[0]) + dot_nn(w_ref[2], dkv_ref[1])
    )
    normed_grad, gain_grad = lifted_grads(x_ref[...].astype(F32), gain_ref[...], grad)
    add_up(gain_grad_ref, gain_grad)
    put_blocks(info_ref, out_ref, low_ref[...].astype(F32) + normed_grad)


def input_grads(place, terms, gain, weights, blocks, after):
    wide, length = terms[0][0].shape
    inner = weights.shape[2]
    step = lane_step(length)
    groups, steps = len(terms), length // step
    spec, shape = outward_spec(groups, wide, length, blocks, step)
    specs = []
    for m in range(groups):
        big = group_columns(m, steps, wide, step)
        specs += [big, big, group_columns(m, steps, inner, step), group_columns(m, steps, 2, inner, step)]
    result, gain_grads = call(
        functools.partial(in_groups, input_kernel, (1, 4, groups), steps),
        "input_grads",
        (groups * steps,),
        specs
        + [
            whole((wide, 1)),
            pl.BlockSpec((3,) + weights.shape[1:], lambda *_: (0, 0, 0), pipeline_mode=pl.Buffered(1)),
        ],
        [spec, pl.BlockSpec((wide, 1), lambda *_: (0, 0))],
        [shape, jax.ShapeDtypeStruct((wide, 1), F32)],
        [place, *[array for term in terms for array in term], gain, weights],
        flops=6 * groups * wide * length * inner,
        scalars=1,
        after=after,
    )
    return outward(result, place, blocks), gain_grads


def rows_kernel(in_ref, out_ref):
    out_ref[...] = in_ref[...]


def rows_of(array, start, rows):
    kinds, _, width = array.shape
    if rows % 16:
        return array[:, start : start + rows]
    return call(
        rows_kernel,
        "rows",
        (kinds,),
        [pl.BlockSpec((1, rows, width), lambda k: (k, start // rows, 0))],
        [pl.BlockSpec((1, rows, width), lambda k: (k, 0, 0))],
        [jax.ShapeDtypeStruct((kinds, rows, width), array.dtype)],
        [array],
    )[0]


def merge_kernel(first_ref, second_ref, out_ref):
    parts = [first_ref[0].astype(F32), second_ref[0].astype(F32)]
    out_ref[0] = jnp.concatenate(parts, axis=0).astype(out_ref.dtype)


def merge(first, second):
    kinds, rows, width = first.shape
    if rows % 8:
        return jnp.concatenate([first, second], axis=1)
    return call(
        merge_kernel,
        "merge",
        (kinds,),
        [slab(rows, width), slab(rows, width)],
        [slab(2 * rows, width)],
        [jax.ShapeDtypeStruct((kinds, 2 * rows, width), first.dtype)],
        [first, second],
    )[0]


def sum_kernel(count, *refs):
    total = refs[0][0].astype(F32)
    for ref in refs[1:count]:
        total = total + ref[0].astype(F32)
    row = 0
    for ref in refs[count:]:
        rows = ref.shape[1]
        ref[0] = total[row : row + rows].astype(BF16)
        row += rows


def sum_rows(terms, parts, starts=None, kinds=None, after=()):
    starts = starts or [0] * len(terms)
    kinds = kinds or terms[0].shape[0]
    rows, width = terms[0].shape[1:]
    sizes = [rows // parts] * parts if isinstance(parts, int) else list(parts)
    if sizes[0] % 8:
        total = add_low(*[term[a : a + kinds] for term, a in zip(terms, starts)])
        results, row = [], 0
        for size in sizes:
            results.append(total[:, row : row + size])
            row += size
    else:
        results = call(
            functools.partial(sum_kernel, len(terms)),
            "sum_rows",
            (kinds,),
            [pl.BlockSpec((1, rows, width), lambda k, a=a: (a + k, 0, 0)) for a in starts],
            [slab(size, width) for size in sizes],
            [jax.ShapeDtypeStruct((kinds, size, width), BF16) for size in sizes],
            terms,
            after=after,
        )
    return results[0] if len(sizes) == 1 else tuple(results)


def corner_kernel(y_ref, first_ref, x_ref, second_ref, y_out, x_out):
    y_out[...] = (y_ref[...].astype(F32) + first_ref[...].astype(F32)).astype(BF16)
    x_out[...] = (x_ref[...].astype(F32) + second_ref[...].astype(F32)).astype(BF16)


def add_corner(to_y, first, to_x, second, after):
    kinds, half, width = first.shape
    upper = pl.BlockSpec((1, half, width), lambda k: (k, 0, 0))
    lower = pl.BlockSpec((1, half, width), lambda k: (k, 1, 0))
    return call(
        corner_kernel,
        "add_corner",
        (kinds,),
        [upper, upper, lower, upper],
        [upper, lower],
        [jax.ShapeDtypeStruct(to_y.shape, BF16), jax.ShapeDtypeStruct(to_x.shape, BF16)],
        [to_y, first, to_x, second],
        aliases={0: 0, 2: 1},
        after=after,
    )


def halves(value_t, half):
    zero = jnp.zeros((half, value_t.shape[1]), value_t.dtype)
    return (
        jnp.concatenate([value_t[:half], zero], axis=0),
        jnp.concatenate([zero, value_t[half:]], axis=0),
    )


def attend_kernel(sources, block, half, info_ref, q_ref, *refs):
    kv_refs = refs[: 2 * sources]
    segq_ref, segk_ref, table_ref, ctx_ref, lse_ref = refs[2 * sources : 2 * sources + 5]
    s_scr, m_scr, l_scr, acc_scr, k_scr = refs[2 * sources + 5 :]
    length = q_ref.shape[1]
    q_blocks = length // block
    k_blocks = q_blocks * sources
    place_x = info_ref[0]
    for s in range(sources):
        k_scr[s * length : (s + 1) * length, :] = transposed(kv_refs[2 * s][...])
    for qb in range(q_blocks):
        rows = pl.ds(qb * block, block)
        q_heads = halves(q_ref[:, rows], half)
        seg_q = segq_ref[:, rows]
        m_scr[...] = jnp.full(m_scr.shape, NEGATIVE, F32)
        l_scr[...] = jnp.zeros(l_scr.shape, F32)
        acc_scr[...] = jnp.zeros(acc_scr.shape, F32)
        for kb in range(k_blocks):
            s, lb = divmod(kb, q_blocks)
            live = info_ref[1 + qb * k_blocks + kb]

            @pl.when(live != 0)
            def _(s=s, lb=lb, kb=kb):
                entry = k_blocks - 1 - ((place_x ^ s) * q_blocks + lb - place_x * q_blocks - qb)
                keys = k_scr[pl.ds(kb * block, block), :]
                kept = segk_ref[pl.ds(kb * block, block), :] == seg_q
                for h in range(2):
                    score = dot_nn(keys, q_heads[h]) + table_ref[h, entry]
                    score = jnp.where(kept, score, NEGATIVE)
                    s_scr[h, kb] = score
                    m_scr[h] = jnp.maximum(m_scr[h], jnp.max(score, axis=0, keepdims=True))

        for kb in range(k_blocks):
            s, lb = divmod(kb, q_blocks)
            live = info_ref[1 + qb * k_blocks + kb]

            @pl.when(live != 0)
            def _(s=s, lb=lb, kb=kb):
                for h in range(2):
                    prob = jnp.exp(s_scr[h, kb] - m_scr[h])
                    l_scr[h] += jnp.sum(prob, axis=0, keepdims=True)
                    values_t = kv_refs[2 * s + 1][
                        h * half : (h + 1) * half, lb * block : (lb + 1) * block
                    ]
                    acc_scr[h * half : (h + 1) * half] += dot_nn(values_t, prob.astype(BF16))

        for h in range(2):
            lse_ref[0, h : h + 1, rows] = m_scr[h] + jnp.log(l_scr[h])
            ctx_ref[h * half : (h + 1) * half, rows] = (
                acc_scr[h * half : (h + 1) * half] / l_scr[h]
            ).astype(BF16)


def grad_kernel(sources, block, half, info_ref, q_ref, *refs):
    kv_refs = refs[: 2 * sources]
    refs = refs[2 * sources :]
    segq_ref, segk_ref, table_ref, ctx_ref, lse_ref, gctx_ref = refs[:6]
    dq_ref, gbias_ref = refs[6:8]
    dkv_refs = refs[8 : 8 + sources]
    dk_scr, dv_scr, dq_scr, k_scr, v_scr, db_scr = refs[8 + sources :]
    length = q_ref.shape[1]
    q_blocks = length // block
    k_blocks = q_blocks * sources
    place_x = info_ref[0]
    db_scr[...] = jnp.zeros(db_scr.shape, F32)
    for s in range(sources):
        k_scr[s * length : (s + 1) * length, :] = transposed(kv_refs[2 * s][...])
        v_scr[s * length : (s + 1) * length, :] = transposed(kv_refs[2 * s + 1][...])
    dk_scr[...] = jnp.zeros(dk_scr.shape, F32)
    dv_scr[...] = jnp.zeros(dv_scr.shape, F32)
    for qb in range(q_blocks):
        rows = pl.ds(qb * block, block)
        query_t = q_ref[:, rows]
        grad_out_t = gctx_ref[:, rows]
        product = grad_out_t.astype(F32) * ctx_ref[:, rows].astype(F32)
        deltas = (
            jnp.sum(product[:half], axis=0, keepdims=True),
            jnp.sum(product[half:], axis=0, keepdims=True),
        )
        q_heads = halves(query_t, half)
        g_heads = halves(grad_out_t, half)
        seg_q = segq_ref[:, rows]
        dq_scr[...] = jnp.zeros(dq_scr.shape, F32)
        for kb in range(k_blocks):
            s, lb = divmod(kb, q_blocks)
            live = info_ref[1 + qb * k_blocks + kb]

            @pl.when(live != 0)
            def _(s=s, lb=lb, kb=kb):
                entry = k_blocks - 1 - ((place_x ^ s) * q_blocks + lb - place_x * q_blocks - qb)
                key_rows = pl.ds(kb * block, block)
                keys = k_scr[key_rows, :]
                values = v_scr[key_rows, :]
                kept = segk_ref[key_rows, :] == seg_q
                for h in range(2):
                    score = dot_nn(keys, q_heads[h]) + table_ref[h, entry]
                    score = jnp.where(kept, score, NEGATIVE)
                    prob = jnp.exp(score - lse_ref[0, h : h + 1, rows])
                    grad_prob = dot_nn(values, g_heads[h])
                    grad_score = prob * (grad_prob - deltas[h])
                    db_scr[h, s, q_blocks - 1 - lb + qb] += grad_score
                    low = grad_score.astype(BF16)
                    head = slice(h * half, (h + 1) * half)
                    key_lanes = slice(kb * block, (kb + 1) * block)
                    dk_scr[head, key_lanes] += dot_nt(query_t[head], low)
                    dv_scr[head, key_lanes] += dot_nt(grad_out_t[head], prob.astype(BF16))
                    keys_t = kv_refs[2 * s][head, lb * block : (lb + 1) * block]
                    dq_scr[head] += dot_nn(keys_t, low)

        dq_ref[:, rows] = dq_scr[...].astype(BF16)
    for s in range(sources):
        lanes = slice(s * length, (s + 1) * length)
        dkv_refs[s][0] = dk_scr[:, lanes].astype(BF16)
        dkv_refs[s][1] = dv_scr[:, lanes].astype(BF16)

    for h in range(2):
        for s in range(sources):
            for n in range(2 * q_blocks - 1):
                gbias_ref[h, s, n] = diagonal_sums(db_scr[h, s, n])


def diagonal_sums(tile):
    block = tile.shape[0]
    count = block
    if block == 2 * LANES:
        zero = jnp.zeros((LANES, LANES), F32)
        tile = jnp.concatenate(
            [
                tile[LANES:, :LANES],
                tile[LANES:, LANES:] + tile[:LANES, :LANES],
                tile[:LANES, LANES:],
                zero,
            ],
            axis=1,
        )
        count = LANES
    else:
        tile = jnp.concatenate([tile, jnp.zeros_like(tile)], axis=1)
    while count > 8:
        count //= 2
        tile = pltpu.roll(tile[:count], count, 1) + tile[count:]
    return tile


def attention_specs(sources, length, block, pairs, width):
    k_blocks = length * sources // block
    entries = 2 * k_blocks - 1

    def rows(offset):
        return pl.BlockSpec((width, length), lambda p, info: (p + offset, 0))

    kv_specs = [rows(pairs), rows(2 * pairs)] + [rows(0), rows(pairs)] * (sources - 1)
    seg_specs = [whole((1, length)), whole((length * sources, 1))]
    table_spec = pl.BlockSpec((2, entries, block, block), lambda p, info: (p, 0, 0, 0))
    lse_spec = pl.BlockSpec((1, 8, length), lambda p, info: (p, 0, 0))
    return k_blocks, entries, rows, kv_specs, seg_specs, table_spec, lse_spec


def attend(info, qkv, others, seg_q, seg_k, table, block, head_size, inner, after):
    length = qkv.shape[1]
    sources = 1 + len(others)
    width = 2 * head_size
    pairs = inner // width
    k_blocks, entries, rows, kv_specs, seg_specs, table_spec, lse_spec = attention_specs(
        sources, length, block, pairs, width
    )
    kvs = [qkv, qkv] + [kv for kv in others for _ in range(2)]
    return call(
        functools.partial(attend_kernel, sources, block, head_size),
        "attend",
        (pairs,),
        [rows(0)] + kv_specs + seg_specs + [table_spec],
        [rows(0), lse_spec],
        [
            jax.ShapeDtypeStruct((inner, length), BF16),
            jax.ShapeDtypeStruct((pairs, 8, length), F32),
        ],
        [info, qkv, *kvs, seg_q, seg_k, table],
        flops=16 * inner * length * length * sources,
        scratch=[
            pltpu.VMEM((2, k_blocks, block, block), F32),
            pltpu.VMEM((2, 1, block), F32),
            pltpu.VMEM((2, 1, block), F32),
            pltpu.VMEM((width, block), F32),
            pltpu.VMEM((length * sources, width), BF16),
        ],
        scalars=1,
        after=after,
    )


def attend_grads(
    info, qkv, others, seg_q, seg_k, table, context, lse, grad_context, block, head_size, after
):
    inner, length = context.shape
    sources = 1 + len(others)
    width = 2 * head_size
    pairs = inner // width
    k_blocks, entries, rows, kv_specs, seg_specs, table_spec, lse_spec = attention_specs(
        sources, length, block, pairs, width
    )
    dkv_spec = pl.BlockSpec((2, width, length), lambda p, info: (0, p, 0))
    tiles = (sources, 2 * (length // block) - 1)
    kvs = [qkv, qkv] + [kv for kv in others for _ in range(2)]
    results = call(
        functools.partial(grad_kernel, sources, block, head_size),
        "attend_grads",
        (pairs,),
        [rows(0)] + kv_specs + seg_specs + [table_spec, rows(0), lse_spec, rows(0)],
        [rows(0), pl.BlockSpec((2,) + tiles + (8, 2 * block), lambda p, info: (p, 0, 0, 0, 0))]
        + [dkv_spec] * sources,
        [
            jax.ShapeDtypeStruct((inner, length), BF16),
            jax.ShapeDtypeStruct((2 * pairs,) + tiles + (8, 2 * block), F32),
        ]
        + [jax.ShapeDtypeStruct((2, inner, length), BF16)] * sources,
        [info, qkv, *kvs, seg_q, seg_k, table, context, lse, grad_context],
        flops=32 * inner * length * length * sources,
        scratch=[
            pltpu.VMEM((width, length * sources), F32),
            pltpu.VMEM((width, length * sources), F32),
            pltpu.VMEM((width, block), F32),
            pltpu.VMEM((length * sources, width), BF16),
            pltpu.VMEM((length * sources, width), BF16),
            pltpu.VMEM((2,) + tiles + (block, block), F32),
        ],
        scalars=1,
        after=after,
    )
    return results[0], results[1], results[2:]


def gelu_terms(gate, upward, grad_hidden):
    square = gate * gate
    tanh = jnp.tanh(GELU_SCALE * gate * (1.0 + GELU_CUBE * square))
    half = 0.5 + 0.5 * tanh
    gelu = gate * half
    slope = half + 0.5 * gate * (1.0 - tanh * tanh) * (
        GELU_SCALE + 3.0 * GELU_CUBE * GELU_SCALE * square
    )
    return (
        (gelu * upward).astype(BF16),
        (grad_hidden * upward * slope).astype(BF16),
        (grad_hidden * gelu).astype(BF16),
    )


def joined(parts, axis):
    return parts[0] if len(parts) == 1 else jnp.concatenate(parts, axis=axis)


def source_rows(refs, kind, columns):
    return joined([ref[kind][:, columns] for ref in refs], 0)


def batches_of(sources, tile):
    if tile % LANES:
        return [[s] for s in range(sources)]
    return [list(range(s, min(s + 2, sources))) for s in range(0, sources, 2)]


def split_refs(refs, counts):
    result, start = [], 0
    for count in counts:
        result.append(refs[start : start + count])
        start += count
    return result, refs[start:]


def ffn_kernel(counts, groups, gathered, stacked, info_ref, *refs):
    if gathered:
        stacks, refs = refs[:3], refs[3:]
        blocks = stacks[0].shape[0] // len(counts)
        tile = stacks[0].shape[2]
    else:
        sources, refs = refs[: len(counts)], refs[len(counts) :]
        tile = sources[0].shape[2]
    acts_hbm, refs = refs[: 2 * groups], refs[2 * groups :]
    (hid_ref, ggi_ref, gui_ref, w_ref), refs = refs[:4], refs[4:]
    if stacked:
        grads_ref, acts, sems = refs
    else:
        grads, (acts, sems) = split_refs(refs, counts)
    first = pl.program_id(0) == 0

    def fetch(n):
        return pltpu.make_async_copy(acts_hbm[n], acts.at[n], sems.at[n])

    def places(source):
        return [
            (info_ref[1] ^ source) * blocks + block_of(info_ref[0], p, blocks // 2)
            for p in range(blocks)
        ]

    def matrix(kind, source):
        if not gathered:
            return sources[source][kind]
        rows = [stacks[kind][place].astype(F32) for place in places(source)]
        return jnp.concatenate(rows, axis=0).astype(BF16)

    @pl.when(first)
    def _():
        for g in range(groups):
            fetch(g).start()
            fetch(groups + g).start()

    start = 0
    for number, batch in enumerate(batches_of(len(counts), tile)):
        units = tile * len(batch)
        rows = slice(start, start + units)
        start += units
        for kind in range(3):
            w_ref[kind, :, rows] = joined([matrix(kind, s) for s in batch], 1)
        for g in range(groups):
            if number == 0:

                @pl.when(first)
                def _(g=g):
                    fetch(g).wait()
                    fetch(groups + g).wait()

            gate = dot_tn(w_ref[0, :, rows], acts[g])
            upward = dot_tn(w_ref[1, :, rows], acts[g])
            grad_hidden = dot_tn(w_ref[2, :, rows], acts[groups + g])
            hidden, grad_gate, grad_up = gelu_terms(gate, upward, grad_hidden)
            hid_ref[g, rows] = hidden
            ggi_ref[g, rows] = grad_gate
            gui_ref[g, rows] = grad_up
        for kind, (left, right_ref) in enumerate(((0, ggi_ref), (0, gui_ref), (groups, hid_ref))):
            total = None
            for g in range(groups):
                product = dot_nt(acts[left + g], right_ref[g, rows])
                total = product if total is None else total + product
            if not stacked:
                total = total.astype(BF16)
            for n, s in enumerate(batch):
                row = 0
                if stacked:
                    depth = grads_ref.shape[2]
                    for place in places(s):
                        part = total[row : row + depth, n * tile : (n + 1) * tile]
                        grads_ref[place, kind] = part.astype(BF16)
                        row += depth
                    continue
                for ref in grads[s]:
                    depth = ref.shape[1]
                    ref[kind] = total[row : row + depth, n * tile : (n + 1) * tile]
                    row += depth


def tile_of(width):
    return LANES if width % LANES == 0 else width


def ffn_chunk(info, weights, width, stacked, normed, cot, after):
    groups = len(normed)
    wide, length = normed[0].shape
    gathered = not isinstance(weights, list)
    sources = lax.axis_size("mp")
    tile = tile_of(width)
    steps = width // tile
    half = wide // 2
    counts = [2] + [3] * (sources - 1)
    shapes = [(3, half, width)] * 2
    for _ in range(sources - 1):
        shapes += [(3, half, width)] + [(3, half // 2, width)] * 2
    grad_specs = [pl.BlockSpec(shape[:2] + (tile,), lambda j, *_: (0, 0, j)) for shape in shapes]
    if stacked:
        shapes = [(weights.shape[0], 3, weights.shape[1], width)]
        grad_specs = [pl.BlockSpec(shapes[0][:3] + (tile,), lambda j, *_: (0, 0, 0, j))]
    if gathered:
        weight_specs = [
            pl.BlockSpec(weights.shape[:2] + (tile,), lambda j, *_, n=n: (0, 0, n * steps + j))
            for n in range(3)
        ]
        operands = [weights] * 3
    else:
        weight_specs = [pl.BlockSpec((3, wide, tile), lambda j, *_: (0, 0, j))] * sources
        operands = list(weights)
    units = sources * tile
    act_spec = pl.BlockSpec((groups, units, length), lambda j, *_: (0, j, 0))
    act_shape = jax.ShapeDtypeStruct((groups, sources * width, length), BF16)
    results = call(
        functools.partial(ffn_kernel, counts, groups, gathered, stacked),
        "ffn_chunk",
        (steps,),
        weight_specs + [pl.BlockSpec(memory_space=pl.ANY)] * (2 * groups),
        [act_spec] * 3
        + [pl.BlockSpec((3, wide, units), lambda j, *_: (0, 0, j))]
        + grad_specs,
        [act_shape] * 3
        + [jax.ShapeDtypeStruct((3, wide, sources * width), BF16)]
        + [jax.ShapeDtypeStruct(shape, BF16) for shape in shapes],
        [info, *operands, *normed, *cot],
        flops=12 * groups * length * wide * sources * width,
        scratch=[
            pltpu.VMEM((2 * groups, wide, length), BF16),
            pltpu.SemaphoreType.DMA((2 * groups,)),
        ],
        scalars=1,
        after=after,
    )
    grads = results[4] if stacked else split_refs(results[4:], counts)[0]
    return results[:3], results[3], grads


def down_kernel(chunks, kinds, with_prior, *refs):
    total = None
    if with_prior:
        total, refs = refs[0][0].astype(F32), refs[1:]
    for _ in range(chunks):
        matrices, acts, refs = refs[:kinds], refs[kinds : 2 * kinds], refs[2 * kinds :]
        for matrix, act in zip(matrices, acts):
            product = dot_nn(matrix[0], act[0])
            total = product if total is None else total + product
    (out_ref,) = refs
    out_ref[0] = total.astype(BF16)


def down(chunk_weights, chunk_acts, first, kinds, start, count, after, prior=None):
    length = chunk_acts[0][0].shape[2]
    wide = chunk_weights[0].shape[1]
    operands, specs = [], []
    if prior is not None:
        operands.append(prior)
        specs.append(pl.BlockSpec((1, wide, length), lambda g: (start + g, 0, 0)))
    flops = 0
    for weights, acts in zip(chunk_weights, chunk_acts):
        acts = acts[1:] if kinds == 2 else acts[:1]
        operands += [weights] * kinds + list(acts)
        specs += [
            pl.BlockSpec(
                (1,) + weights.shape[1:], lambda g, n=n: (n, 0, 0), pipeline_mode=pl.Buffered(1)
            )
            for n in range(first, first + kinds)
        ]
        specs += [
            pl.BlockSpec((1, act.shape[1], length), lambda g: (start + g, 0, 0)) for act in acts
        ]
        flops += 2 * kinds * count * length * wide * acts[0].shape[1]
    return call(
        functools.partial(down_kernel, len(chunk_acts), kinds, prior is not None),
        "down",
        (count,),
        specs,
        [slab(wide, length)],
        [jax.ShapeDtypeStruct((count, wide, length), BF16)],
        operands,
        flops=flops,
        after=after,
    )[0]


def body(
    inputs,
    cotangent,
    segments,
    rel_bucket,
    head_order,
    rel_table,
    norm1_gain,
    norm2_gain,
    w_query,
    w_key,
    w_value,
    output_weight,
    w_gate,
    w_up,
    w_down,
):
    dp, mp = dp_size(), lax.axis_size("mp")
    x = lax.axis_index("mp")
    core, chip = lax.axis_index("core"), lax.axis_index("chip")
    chips, depth = dp // 2, dp // 4
    micro, rows, own_length, model = inputs.shape
    groups = micro * rows
    length = own_length * mp
    bucket_count, head_count = rel_table.shape
    inner = w_query.shape[1]
    head_size = inner // head_count
    block = min(256, own_length)
    q_blocks, k_blocks = own_length // block, length // block
    own_rows, own_units = w_gate.shape
    half_units = own_units // 2
    chip_rows = 2 * own_rows
    place = chip.reshape(1).astype(jnp.int32)

    micros = range(groups)
    own_place = (2 * x + core).reshape(1).astype(jnp.int32)
    role_place = own_place & 3

    def feature_major(array):
        return jnp.transpose(array.reshape(groups, own_length, model), (0, 2, 1))

    bucket_rev = jnp.concatenate([rel_bucket[::-1], jnp.full((1,), -1, jnp.int32)])
    bucket_hot = (bucket_rev[:, None] == jnp.arange(bucket_count, dtype=jnp.int32)[None, :]).astype(F32)
    head_hot = (head_order[:, None] == jnp.arange(head_count, dtype=jnp.int32)[None, :]).astype(F32)
    offset_table = jnp.dot(bucket_hot, rel_table, precision=TOP_PRECISION)
    offset_bias = jnp.dot(head_hot, offset_table.T, precision=TOP_PRECISION)
    bias_blocks = offset_bias.reshape(head_count, 2 * k_blocks, block)
    windows = jnp.concatenate([bias_blocks[:, :-1], bias_blocks[:, 1:]], axis=2)

    part = 4 * inner // (2 * mp)
    shard = jnp.concatenate([w_query, w_key, w_value, jnp.transpose(output_weight)], axis=1)
    kept = lax.dynamic_slice_in_dim(shard, (2 * x + core) * part, part, 1)
    sent = lax.dynamic_slice_in_dim(shard, (2 * x + 1 - core) * part, part, 1)
    got = swap_dp(sent, 1)
    attention_piece = either(
        core, jnp.concatenate([kept, got], axis=0), jnp.concatenate([got, kept], axis=0)
    )[None]
    ffn_shard = jnp.stack([w_gate, w_up, jnp.transpose(w_down)])
    low_half, high_half = ffn_shard[:, :, :half_units], ffn_shard[:, :, half_units:]
    kept = either(core, low_half, high_half)
    got = swap_dp(either(core, high_half, low_half), 1)
    ffn_piece = either(
        core, jnp.concatenate([kept, got], axis=1), jnp.concatenate([got, kept], axis=1)
    )
    if half_units % (7 * LANES) == 0:
        bounds = [0, half_units // 7 * FIRST_SEVENTHS, half_units]
    elif half_units > LANES:
        bounds = [0, LANES, half_units]
    else:
        bounds = [0, half_units]
    widths = [b - a for a, b in zip(bounds[:-1], bounds[1:])]
    chunk_stacks = []
    for a, width in zip(bounds, widths):
        flat = jnp.concatenate([ffn_piece[n, :, a : a + width] for n in range(3)], axis=1)
        chunk_stacks.append(lax.all_gather(flat, ("mp", "chip")))

    far_masks = z_masks()

    def gather_z(piece, masks, first=(), then=()):
        for mask in masks:
            piece = merge(piece, hold(swap_dp(hold(piece, *first), mask), *then))
        return piece

    own = gather_z(attention_piece, far_masks)
    arrays = feature_major(inputs)
    layer_in = [reorder(arrays, m, place, chips, False) for m in micros]
    arrays = feature_major(cotangent)
    cots = [reorder(arrays, m, place, chips, False, [*layer_in, own]) for m in micros]
    cots_far = [swap_dp(cot, 1) for cot in cots]
    table = bias_table(windows[:, :, None, :], block, cots)
    over_y, over_x = gather_xy(own, layer_in, [table])
    corner = gather_corner(over_y, over_x)
    quads = quads_of(own, over_y, over_x, corner)
    matrices = []
    for parts in quads:
        matrices += [parts, tuple(swap_dp(ref, 1) for ref in parts)]

    seg_flat = segments.reshape(groups, length)
    seg_q = lax.dynamic_slice_in_dim(seg_flat, x * own_length, own_length, 1)
    seg_parts = seg_flat.reshape(groups, mp, own_length)
    seg_k = jnp.concatenate([pick(seg_parts, x ^ k, 1) for k in range(mp)], axis=1)
    q_edges = seg_q.reshape(groups, q_blocks, block)
    k_edges = seg_k.reshape(groups, k_blocks, block)
    live = (q_edges[:, :, None, 0] <= k_edges[:, None, :, -1]) & (
        k_edges[:, None, :, 0] <= q_edges[:, :, None, -1]
    )
    infos = [
        jnp.concatenate([x.reshape(1).astype(jnp.int32), live[m].reshape(-1).astype(jnp.int32)])
        for m in micros
    ]
    seg_q_rows = [seg_q[m][None, :] for m in micros]
    seg_k_columns = [seg_k[m][:, None] for m in micros]

    gains = reorder(jnp.stack([norm1_gain, norm2_gain], axis=1)[None], 0, place, chips, False)
    gain1, gain2 = gains[:, :1], gains[:, 1:]
    normed1, qkvs, others = [], [], []
    last = cots_far
    for m in micros:
        normed, qkv, kv = project(own_place, layer_in[m], gain1, matrices, last)
        last = [normed]
        normed1.append(normed)
        qkvs.append(qkv.reshape(4 * inner, own_length))
        others.append([swap_mp(kv, k).reshape(2 * inner, own_length) for k in x_masks()])
    weights = assemble(own_place, matrices, inner, [normed1[-1]])
    last = [weights]
    contexts, lses, normed2, normed2_far = [], [], [], []
    for m in micros:
        context, lse = attend(
            infos[m], qkvs[m], others[m], seg_q_rows[m], seg_k_columns[m], table,
            block, head_size, inner, last,
        )
        contexts.append(context)
        lses.append(lse)
        last = [context]
        normed = middle_layer(layer_in[m], context, weights, gain2, last)
        last = [normed]
        normed2.append(normed)
        normed2_far.append(swap_dp(normed, 1))

    ffn_info = jnp.concatenate([place, x.reshape(1).astype(jnp.int32)])
    chunk_acts, chunk_weights, chunk_grads = [], [], []
    prior = prior_ffn = None
    sums = []
    for stack, width in zip(chunk_stacks, widths):
        stacked = len(chunk_acts) + 1 < len(widths)
        if own_rows % 4 or width % LANES:
            ordered = jnp.stack(
                [
                    jnp.stack([pick(stack, (x ^ k) * chips + block_of(chip, p, depth), 0) for p in range(chips)])
                    for k in range(mp)
                ]
            ).reshape(mp, model, 3, width)
            stack = [jnp.transpose(ordered[k], (1, 0, 2)) for k in range(mp)]
            stacked = False
        acts, matrices_in, grads = ffn_chunk(
            ffn_info, stack, width, stacked, normed2 + normed2_far, cots + cots_far, last
        )
        last = [acts[0]]
        chunk_acts.append(acts)
        chunk_weights.append(matrices_in)
        if stacked:
            sums.append(lax.psum_scatter(grads, ("mp", "chip"), scatter_dimension=0))
        else:
            chunk_grads.append(grads)
        if len(chunk_acts) < len(widths):
            prior = down(chunk_weights, chunk_acts, 0, 2, 0, 2 * groups, last)
            prior_ffn = down(chunk_weights, chunk_acts, 2, 1, 0, 2 * groups, [prior])
            last = [prior_ffn]
    back = functools.partial(down, chunk_weights[-1:], chunk_acts[-1:], 0, 2)
    back_far = back(groups, groups, last, prior)
    from_far = swap_dp(back_far, 1)
    back_own = back(0, groups, [back_far], prior)
    last = [back_own]

    z_count = len(far_masks)
    grad_attn, grad_q, grad_kv, bias_grads, gain2_grads = [], [], [], [], []
    for m in micros:
        low, grad_context, gain_grads = turn(
            m, layer_in[m], contexts[m], cots[m], (back_own, from_far), gain2, weights, last
        )
        last = [low]
        grad_attn.append(low)
        gain2_grads.append(gain_grads)
        dq, bias_grad, dkv = attend_grads(
            infos[m], qkvs[m], others[m], seg_q_rows[m], seg_k_columns[m], table,
            contexts[m], lses[m], grad_context, block, head_size, last,
        )
        last = [dq]
        if m == micros[0]:
            moving = [scatter_corner(grads, [], last) for grads in chunk_grads]
            last += [parts[1] for parts in moving]
        grad_q.append(dq)
        bias_grads.append(bias_grad)
        grad_kv.append((dkv[0], [swap_mp(dkv[k], k) for k in x_masks()]))
    grad_kv[0] = sum_rows([grad_kv[0][0], *hold(grad_kv[0][1], dq)], 1, after=[dq])
    weight_grads = outer_products(
        role_place,
        (0, 3),
        [
            [(normed1[m], grad_q[m]) for m in micros],
            [(grad_attn[m], contexts[m]) for m in micros],
        ],
        None,
        [dq, grad_kv[0]],
    )
    ffn = functools.partial(down, chunk_weights[-1:], chunk_acts[-1:], 2, 1)
    ffn_far = ffn(groups, groups, [weight_grads], prior_ffn)
    ffn_from = swap_dp(ffn_far, 1)
    grad_kv[1:] = [
        sum_rows([own, *hold(got, ffn_far)], 1, after=[ffn_far]) for own, got in grad_kv[1:]
    ]
    ffn_own = ffn(0, groups, [ffn_far, *grad_kv[1:]], prior_ffn)
    from_y = [swap_dp(to_y, 2) for _, to_y, _ in moving]
    weight_grads = outer_products(
        role_place,
        (1, 2),
        [[(normed1[m], (grad_kv[m], n)) for m in micros] for n in range(2)],
        weight_grads,
        [ffn_own],
    )

    half = model // 2
    split = [half, half // 2, half // 2]
    if part == inner:
        got = [swap_dp(weight_grads[2 * k + 1 : 2 * k + 2], 1) for k in range(mp)]
        quads = [
            sum_rows([weight_grads, got[k]], 2 if k == 0 else split, [2 * k, 0], 1)
            for k in range(mp)
        ]
    else:
        ordered = jnp.concatenate(
            [lax.dynamic_slice_in_dim(weight_grads, role_place[0] ^ r, 1, 0) for r in range(4)]
        )
        by_part = jnp.transpose(
            ordered.reshape(4, model, inner // part, part), (0, 2, 1, 3)
        ).reshape(mp, 2, model, part)
        near = add_low(pick(by_part, core, 1), swap_dp(pick(by_part, 1 - core, 1), 1))
        quads = []
        for k in range(mp):
            matrix = pick(near, x ^ k, 0)[None]
            sizes = [half, half] if k == 0 else split
            starts = [sum(sizes[:n]) for n in range(len(sizes))]
            quads.append(tuple(matrix[:, a : a + n] for a, n in zip(starts, sizes)))
    xy_sums = []
    for (own, _, to_x), got in zip(moving, from_y):
        to_x = hold(to_x, *grad_kv[1:])
        got = [got] + [swap_mp(other, k) for k, other in zip(x_masks(), to_x)]
        xy_sums.append(sum_rows([own, *hold(got, quads[0][0])], 2, after=[quads[0][0]]))
    grad_inputs, gain1_grads = input_grads(
        place,
        [(layer_in[m], grad_attn[m], grad_q[m], grad_kv[m]) for m in micros],
        gain1,
        weights,
        chips,
        [weight_grads, quads[0][0]] + [parts[0] for parts in xy_sums],
    )
    last = [gain1_grads]
    corner = scatter_corner(quads, [], last)
    traded = [trade_rows(part, core, own_rows) for part in sums] if z_count == 2 else []
    moving = [scatter_z(parts, 0, last) for parts in xy_sums]

    bias_rows = sum(bias_grads)
    bias_tiles = sum(
        jnp.pad(bias_rows[:, :, :, t, : 2 * block - 7 + t], ((0, 0),) * 3 + ((7 - t, 0),))
        for t in range(8)
    )
    run = 2 * q_blocks - 1
    bias_flat = jnp.zeros((head_count, 2 * k_blocks - 1, 2 * block), F32)
    for k in range(mp):
        first = k_blocks - q_blocks - ((x ^ k) - x) * q_blocks
        held = lax.dynamic_slice_in_dim(bias_flat, first, run, 1)
        bias_flat = lax.dynamic_update_slice_in_dim(bias_flat, held + bias_tiles[:, k], first, 1)
    left = jnp.pad(bias_flat[:, :, :block], ((0, 0), (0, 1), (0, 0)))
    right = jnp.pad(bias_flat[:, :, block:], ((0, 0), (1, 0), (0, 0)))
    offsets_total = (left + right).reshape(head_count, 2 * k_blocks * block)
    bucket_part = jnp.dot(bucket_hot.T, offsets_total.T, precision=TOP_PRECISION)
    rel_part = jnp.dot(bucket_part, head_hot, precision=TOP_PRECISION)
    gain_parts = jnp.concatenate([gain1_grads, sum(gain2_grads)], axis=1)
    gain_parts = reorder(hold(gain_parts, corner[1])[None], 0, place, chips, True)
    small = jnp.concatenate([gain_parts[:, 0], gain_parts[:, 1], rel_part.reshape(-1)])

    small = small + swap_dp(small, 1)
    steps = [(swap_mp, mask) for mask in doubling(mp)]
    steps += [(swap_dp, mask) for mask in doubling(dp) if mask > 1]
    outputs = finish(
        place,
        [(layer_in[m], contexts[m]) for m in micros],
        (ffn_own, ffn_from),
        weights,
        chips,
        [corner[1]] + [first_of(parts) for parts in moving] + [got for _, got in traded],
    )
    own, to_y, to_x = corner
    got = [swap_dp(to_y, 2)] + [swap_mp(other, k) for k, other in zip(x_masks(), to_x)]
    total = sum_rows([own, *hold(got, outputs)], 2, after=[outputs])
    moving = [scatter_z(parts, 1, [outputs]) for parts in moving]
    for stage, mask in enumerate(reversed(far_masks)):
        got, small = beside(swap_dp(total[1], mask), small, steps)
        waited = moving if stage == z_count - 1 and z_count == 2 else []
        total = sum_rows([total[0], got], 1 if stage == z_count - 1 else 2, after=waited)
    for stage in range(2, z_count):
        moving = [scatter_z(parts, stage) for parts in moving]
    piece = total[0]
    got, small = beside([swap_mp(piece, k) for k in x_masks()], small, steps)
    over_x = jnp.stack([piece] + got)
    kept = either(core, over_x[:, :own_rows], over_x[:, own_rows:])
    got = swap_dp(either(core, over_x[:, own_rows:], over_x[:, :own_rows]), 1)
    got, small = beside(got, small, steps)
    while steps:
        got, small = beside(got, small, steps)
    both = jnp.stack([kept, got], axis=1).reshape(2 * mp, own_rows, part)
    final = jnp.concatenate(
        [pick(both, (2 * x + core) ^ r, 0) for r in range(2 * mp)], axis=1
    ).astype(F32)

    late = moving if traded else sums + moving
    traded = traded + [trade_rows(part, core, own_rows) for part in late]
    kept, got = [part for part, _ in traded], [part for _, part in traded]
    ffn_grads = either(
        core, jnp.concatenate(kept + got, axis=2), jnp.concatenate(got + kept, axis=2)
    ).astype(F32)

    shape = inputs.shape

    def placed(array):
        return jnp.transpose(array, (0, 2, 1)).reshape(shape)

    return (
        placed(outputs),
        placed(grad_inputs),
        small[2 * model :].reshape(rel_table.shape),
        small[:model],
        small[model : 2 * model],
        final[:, :inner],
        final[:, inner : 2 * inner],
        final[:, 2 * inner : 3 * inner],
        jnp.transpose(final[:, 3 * inner :]),
        ffn_grads[0],
        ffn_grads[1],
        jnp.transpose(ffn_grads[2]),
    )


def solution(mesh):
    devices = mesh.devices.reshape(-1, 2, mesh.shape["mp"])
    return jax.shard_map(
        body,
        mesh=jax.sharding.Mesh(devices, DP + ("mp",)),
        in_specs=(
            P(None, DP, "mp", None),
            P(None, DP, "mp", None),
            P(None, DP, None),
            P(),
            P(),
            P(),
            P(),
            P(),
            P(DP, None),
            P(DP, None),
            P(DP, None),
            P(None, DP),
            P(DP, "mp"),
            P(DP, "mp"),
            P("mp", DP),
        ),
        out_specs=(
            P(None, DP, "mp", None),
            P(None, DP, "mp", None),
            P(),
            P(),
            P(),
            P(DP, None),
            P(DP, None),
            P(DP, None),
            P(None, DP),
            P(DP, "mp"),
            P(DP, "mp"),
            P("mp", DP),
        ),
        check_vma=False,
    )
```
